256 devices in a mesh: gx: 8 (over x_hi, y), gy: 32 (over x_lo, z, core).
Axes of the slice: x: 4 (x_hi: 2, x_lo: 2; x = x_hi * 2 + x_lo), y: 4, z: 8, core: 2. Of those that a mesh axis runs over, the one named last changes fastest.
Arguments:
- images: bfloat16 [256, 14, 14, 512], P(('gx', 'gy')), may hold values from -6 to 6
- conv_weight: bfloat16 [4608, 512], replicated, may hold values from -0.09375 to 0.09375
- fc6_weight: bfloat16 [25088, 4096], P('gx', 'gy'), may hold values from -0.0390625 to 0.0390625
- fc7_weight: bfloat16 [4096, 4096], P(None, ('gx', 'gy')), may hold values from -0.09375 to 0.09375
- cotangent: bfloat16 [256, 4096], P(None, ('gx', 'gy')), may hold values from -12 to 12
Outputs:
- grad_conv: float32 [4608, 512], P('gy', 'gx')
- grad_fc6: float32 [25088, 4096], P('gx', 'gy')
- grad_fc7: float32 [4096, 4096], P(None, ('gx', 'gy'))
- grad_images: float32 [256, 14, 14, 512], P(('gx', 'gy'))
The draws below stay inside these ranges and needn't reach their ends.
All inputs are finite; a program needn't handle non-finite values.
Results may differ from the reference program's by a relative error of at most 0.012.
Values may be sent and summed in bfloat16 or wider, within the bound.
No kernel may reach another device: no remote copies, remote signals or barrier semaphores. Data moves between devices by JAX's collectives and lax.ppermute only.
A program may use at most 128 MiB of HBM per device.

```python
import jax
import jax.numpy as jnp

C = 512
SIDE = 14
HIDDEN6 = 4096
HIDDEN7 = 4096
IMAGES = 256
FEAT = 25088


def levels(stream_key, shape, shards, least, high):
    def one(dim, parts):
        heights = jax.random.uniform(jax.random.fold_in(jax.random.fold_in(stream_key, 6), dim), (parts,), jnp.float32, least / len(shards), high / len(shards))
        return jnp.repeat(jnp.exp(heights), shape[dim] // parts).reshape((-1,) + (1,) * (len(shape) - dim - 1))

    loudness = one(*shards[0])
    for cut in shards[1:]:
        loudness = loudness * one(*cut)
    return loudness


def scatter_about(rng, dims, scale, limit, shards=(), kind=jnp.bfloat16):
    gain = levels(rng, dims, shards, -0.22, 0.18) if shards else 1.0
    entries = jax.random.normal(rng, dims, jnp.float32) * scale * gain
    return jnp.minimum(jnp.maximum(entries, -limit), limit).astype(kind)


def setup_inputs(seed: int = 0) -> dict:
    seeds = jax.random.split(jax.random.key(seed), 6)
    images = scatter_about(seeds[0], (IMAGES, SIDE, SIDE, C), 1.0, 6.0, ((0, 256),))
    conv_weight = scatter_about(seeds[1], (9 * C, C), (9 * C) ** -0.5, 0.09375)
    fc6_weight = scatter_about(seeds[2], (FEAT, HIDDEN6), FEAT ** -0.5, 0.0390625, ((0, 8), (1, 32)))
    fc7_weight = scatter_about(seeds[3], (HIDDEN6, HIDDEN7), HIDDEN6 ** -0.5, 0.09375, ((1, 256),))
    cotangent = scatter_about(seeds[4], (IMAGES, HIDDEN7), 2.0, 12.0, ((1, 256),))
    return {"images": images, "conv_weight": conv_weight, "fc6_weight": fc6_weight, "fc7_weight": fc7_weight, "cotangent": cotangent}


def shifted(arr, row, col, side):
    return arr[:, row:row + side, col:col + side, :].reshape(-1, arr.shape[3])


def activate(value):
    return value * jax.nn.sigmoid(value)


def slope(value):
    sig = jax.nn.sigmoid(value)
    return sig * (1.0 + value * (1.0 - sig))


def reference(images, conv_weight, fc6_weight, fc7_weight, cotangent):
    count = images.shape[0]
    side = images.shape[1]
    chans = images.shape[3]
    half = side // 2
    padded = jnp.pad(images, ((0, 0), (1, 1), (1, 1), (0, 0)))
    conv_pre = jnp.zeros((count * side * side, chans), jnp.float32)
    for row in range(3):
        for col in range(3):
            kernel = conv_weight[(3 * row + col) * chans:(3 * row + col + 1) * chans]
            conv_pre = conv_pre + jnp.dot(shifted(padded, row, col, side), kernel, preferred_element_type=jnp.float32)
    active = activate(conv_pre).reshape(count, half, 2, half, 2, chans)
    feat = (0.25 * active.sum(axis=(2, 4))).reshape(count, -1).astype(jnp.bfloat16)
    h6_pre = jnp.dot(feat, fc6_weight, preferred_element_type=jnp.float32)
    hidden = activate(h6_pre).astype(jnp.bfloat16)
    y7_pre = jnp.dot(hidden, fc7_weight, preferred_element_type=jnp.float32)
    g_seven = (cotangent.astype(jnp.float32) * slope(y7_pre)).astype(jnp.bfloat16)
    grad_fc7 = jnp.dot(hidden.T, g_seven, preferred_element_type=jnp.float32)
    grad_hidden = jnp.dot(g_seven, fc7_weight.T, preferred_element_type=jnp.float32)
    g_six = (grad_hidden * slope(h6_pre)).astype(jnp.bfloat16)
    grad_fc6 = jnp.dot(feat.T, g_six, preferred_element_type=jnp.float32)
    dfeat = jnp.dot(g_six, fc6_weight.T, preferred_element_type=jnp.float32).astype(jnp.bfloat16)
    spread = dfeat.astype(jnp.float32).reshape(count, half, 1, half, 1, chans)
    spread = jnp.broadcast_to(spread, (count, half, 2, half, 2, chans)).reshape(count * side * side, chans)
    g_conv = (0.25 * spread * slope(conv_pre)).astype(jnp.bfloat16)
    g_padded = jnp.pad(g_conv.reshape(count, side, side, chans), ((0, 0), (1, 1), (1, 1), (0, 0)))
    blocks = []
    grad_in = jnp.zeros((count * side * side, chans), jnp.float32)
    for row in range(3):
        for col in range(3):
            kernel = conv_weight[(3 * row + col) * chans:(3 * row + col + 1) * chans]
            blocks.append(jnp.dot(shifted(padded, row, col, side).T, g_conv, preferred_element_type=jnp.float32))
            grad_in = grad_in + jnp.dot(shifted(g_padded, 2 - row, 2 - col, side), kernel.T, preferred_element_type=jnp.float32)
    grad_conv = jnp.concatenate(blocks, axis=0)
    grad_images = grad_in.reshape(count, side, side, chans)
    return grad_conv, grad_fc6, grad_fc7, grad_images
```

```python
import jax
import jax.numpy as jnp
from jax import lax
from jax.sharding import Mesh, PartitionSpec as P

BF = jnp.bfloat16
F32 = jnp.float32


def activate(value):
    return value * jax.nn.sigmoid(value)


def slope(value):
    sig = jax.nn.sigmoid(value)
    return sig * (1.0 + value * (1.0 - sig))


def dot(a, b, dims):
    return lax.dot_general(a, b, (dims, ((), ())), preferred_element_type=F32)


def swap(value, axis):
    return lax.all_to_all(value, axis, 0, 0, tiled=True)


def share(value, axis, count):
    return swap(jnp.broadcast_to(value, (count,) + value.shape), axis)


def patches(arr, flip):
    side = arr.shape[1]
    padded = jnp.pad(arr, ((0, 0), (1, 1), (1, 1), (0, 0)))
    out = []
    for row in range(3):
        for col in range(3):
            r, q = (2 - row, 2 - col) if flip else (row, col)
            out.append(padded[:, r : r + side, q : q + side, :].reshape(-1, arr.shape[3]))
    return out


def make(nx, nz, nc):
    ny = nz * nc

    def on_device(images, conv_weight, fc6_weight, fc7_weight, cotangent):
        side, chans = images.shape[1], images.shape[3]
        half = side // 2
        pix = side * side
        feats, units = fc6_weight.shape
        rows7, cols7 = fc7_weight.shape
        group = cotangent.shape[0] // nc
        wide = units * nc

        weight6 = lax.all_gather(fc6_weight, "core", axis=0, tiled=False)
        gathered = lax.all_gather(images[0], "gx", axis=0, tiled=False)
        send7 = fc7_weight.T.reshape(cols7, nz, wide).transpose(1, 0, 2)
        send7 = jnp.broadcast_to(send7[:, None], (nz, nc, cols7, wide)).reshape(ny, cols7, wide)
        weight7 = swap(send7, ("gz", "core")).reshape(ny * cols7, wide)
        cot = cotangent.T.reshape(cols7, nx, nz, nc).transpose(0, 3, 2, 1)
        cot = cot.reshape(cols7, nc * group).astype(F32)

        taps = jnp.concatenate(patches(images, False), axis=1)
        conv_pre = jnp.dot(taps, conv_weight, preferred_element_type=F32)
        pooled = activate(conv_pre).reshape(half, 2, half, 2, chans).sum(axis=(1, 3))
        feat = (0.25 * pooled).astype(BF).reshape(nx, feats)
        inputs = share(swap(feat, "gx"), "gz", nz).reshape(group, feats)

        h6_terms = jnp.concatenate([dot(inputs, weight6[k], ((1,), (0,))) for k in range(nc)], 1)
        h6_pre = share(h6_terms.astype(BF), "gx", nx).astype(F32).sum(axis=0)
        hidden = activate(h6_pre).astype(BF)
        all_hidden = lax.all_gather(hidden, ("gz", "core"), axis=0, tiled=False)

        y7_terms = dot(weight7, hidden, ((1,), (1,))).astype(BF)
        y7_pre = swap(y7_terms.reshape(ny, cols7, group), ("gz", "core"))
        y7_pre = y7_pre.reshape(nz, nc, cols7, group).astype(F32).sum(axis=0)
        y7_pre = y7_pre.transpose(1, 0, 2).reshape(cols7, nc * group)
        g_seven = (cot * slope(y7_pre)).astype(BF)
        send = g_seven.reshape(cols7, nc, group).transpose(1, 0, 2)
        send = jnp.broadcast_to(send[None], (nz, nc, cols7, group)).reshape(ny, cols7, group)
        g7_cols = swap(send, ("gz", "core")).reshape(ny * cols7, group)

        dh6_terms = dot(g7_cols, weight7, ((0,), (0,))).astype(BF)
        grad_hidden = share(dh6_terms, "gx", nx).astype(F32).sum(axis=0)
        g_six = (grad_hidden * slope(h6_pre)).astype(BF)

        feat_terms = sum(
            dot(g_six[:, k * units : (k + 1) * units], weight6[k], ((1,), (1,)))
            for k in range(nc)
        )
        feat_terms = swap(feat_terms.astype(BF).reshape(nz, nx, feats), "gz")
        dfeat = swap(feat_terms.astype(F32).sum(axis=0).astype(BF), "gx")

        spread = jnp.broadcast_to(
            dfeat.reshape(half, 1, half, 1, chans).astype(F32), (half, 2, half, 2, chans)
        ).reshape(pix, chans)
        g_conv = (0.25 * spread * slope(conv_pre)).astype(BF)

        part = chans // nx
        g_cols = swap(g_conv.reshape(pix, nx, part).transpose(1, 0, 2), "gx")
        g_cols = g_cols.reshape(nx * pix, part)
        kernel_terms = jnp.concatenate(
            [dot(p, g_cols, ((0,), (0,))) for p in patches(gathered, False)], axis=0
        )
        block = kernel_terms.shape[0] // ny
        packed = kernel_terms.astype(BF).reshape(ny, 2, block // 2, part)
        packed = jnp.concatenate([packed[:, 0], packed[:, 1]], axis=2)
        summed = swap(packed, ("gz", "core")).astype(F32).sum(axis=0)
        grad_conv = jnp.concatenate([summed[:, :part], summed[:, part:]], axis=0)

        grad6_terms = jnp.stack(
            [dot(inputs, g_six[:, k * units : (k + 1) * units], ((0,), (0,))) for k in range(nc)]
        )
        grad_fc6 = lax.psum_scatter(grad6_terms, "core", scatter_dimension=0, tiled=False)
        all_hidden = all_hidden.reshape(nz, nc, group, wide)
        grad7 = sum(
            dot(g_seven[:, k * group : (k + 1) * group], all_hidden[:, k], ((1,), (1,)))
            for k in range(nc)
        )
        grad_fc7 = grad7.reshape(cols7, rows7).T
        taps = jnp.concatenate(patches(g_conv.reshape(1, side, side, chans), True), axis=1)
        flipped = conv_weight.reshape(9, chans, chans)
        grad_in = sum(
            dot(taps[:, k * chans : (k + 1) * chans], flipped[k], ((1,), (1,))) for k in range(9)
        )
        grad_images = grad_in.reshape(1, side, side, chans)
        return (grad_conv, grad_fc6, grad_fc7, grad_images)

    return on_device


def solution(mesh):
    nx, ny = mesh.shape["gx"], mesh.shape["gy"]
    nc = 2
    nz = ny // nc
    fine = Mesh(mesh.devices.reshape(nx, nz, nc), ("gx", "gz", "core"))
    gy = ("gz", "core")
    both = ("gx", "gz", "core")
    placed = (
        P(both, None, None, None),
        P(),
        P("gx", gy),
        P(None, both),
        P(None, both),
    )
    return jax.shard_map(
        make(nx, nz, nc),
        mesh=fine,
        in_specs=placed,
        out_specs=(
            P(gy, "gx"),
            P("gx", gy),
            P(None, both),
            P(both, None, None, None),
        ),
        check_vma=False,
    )
```

```python
import jax
import jax.numpy as jnp
from jax import lax
from jax.experimental import pallas as pl
from jax.experimental.pallas import tpu as pltpu
from jax.sharding import Mesh, PartitionSpec as P

BF = jnp.bfloat16
F32 = jnp.float32
LANES = 128
LINE = 16


def slope(value):
    sig = jax.nn.sigmoid(value)
    return sig * (1.0 + value * (1.0 - sig))


def activate(value):
    return value * jax.nn.sigmoid(value)


def forward_kernel(image_ref, weight_ref, pre_ref, feat_ref, sums_ref, pool_ref):
    step = pl.program_id(0)
    col = lax.rem(step, 3)
    rows = sums_ref.shape[1]
    start = pl.multiple_of((step // 3) * LINE, LINE)
    part = jnp.dot(
        image_ref[pl.ds(start, rows), :], weight_ref[...], preferred_element_type=F32
    )

    @pl.when(step < 3)
    def _():
        sums_ref[col] = part

    @pl.when(step >= 3)
    def _():
        sums_ref[col] += part

    @pl.when(step == 8)
    def _():
        pix, chans = pre_ref.shape
        pre = sums_ref[0, 0:pix, :] + sums_ref[1, 1 : pix + 1, :] + sums_ref[2, 2 : pix + 2, :]
        pre_ref[...] = pre
        act = activate(pre).reshape(pix // (2 * LINE), 2, LINE, chans)
        lines = (act[:, 0] + act[:, 1]).reshape(pix // 2, chans)
        half = pix // 4
        for k in range(chans // LANES):
            pool_ref[k] = lines[:, k * LANES : (k + 1) * LANES]
            total = pool_ref[k, pl.ds(0, half, 2), :] + pool_ref[k, pl.ds(1, half, 2), :]
            feat_ref[:, k * LANES : (k + 1) * LANES] = 0.25 * total


def conv_forward(lines, weight, side):
    chans = weight.shape[1]
    depth = lines.shape[1]
    pix = side * LINE
    return pl.pallas_call(
        forward_kernel,
        grid=(9,),
        in_specs=[
            pl.BlockSpec(lines.shape, lambda t: (0, 0)),
            pl.BlockSpec((depth, chans), lambda t: (t, 0)),
        ],
        out_specs=[
            pl.BlockSpec((pix, chans), lambda t: (0, 0)),
            pl.BlockSpec((pix // 4, chans), lambda t: (0, 0)),
        ],
        out_shape=[
            jax.ShapeDtypeStruct((pix, chans), F32),
            jax.ShapeDtypeStruct((pix // 4, chans), F32),
        ],
        scratch_shapes=[pltpu.VMEM((3, pix + LINE, chans), F32), pltpu.VMEM((chans // LANES, pix // 2, LANES), F32)],
        compiler_params=pltpu.CompilerParams(vmem_limit_bytes=32 * 2**20),
        cost_estimate=pl.CostEstimate(
            flops=18 * pix * depth * chans, bytes_accessed=weight.size * 2, transcendentals=pix * chans
        ),
    )(lines, weight)


def slope_kernel(pre_ref, dfeat_ref, lines_ref, turned_ref, wide_ref):
    pix, chans = pre_ref.shape
    half = pix // 4
    for k in range(chans // LANES):
        dfeat = dfeat_ref[:, k * LANES : (k + 1) * LANES]
        wide_ref[k, pl.ds(0, half, 2), :] = dfeat
        wide_ref[k, pl.ds(1, half, 2), :] = dfeat
    spread = jnp.concatenate([wide_ref[k] for k in range(chans // LANES)], axis=1)
    spread = spread.reshape(pix // (2 * LINE), 1, LINE, chans)
    spread = jnp.broadcast_to(spread, (pix // (2 * LINE), 2, LINE, chans)).reshape(pix, chans)
    grad = 0.25 * spread * slope(pre_ref[...])
    extra = turned_ref.shape[1] - pix
    grad = jnp.concatenate([grad, jnp.zeros((extra, chans), F32)], axis=0)
    turned_ref[...] = grad.T.astype(BF)
    lines_ref[...] = grad.astype(BF)


def conv_slope(pre, dfeat, rows):
    pix, chans = pre.shape
    return pl.pallas_call(
        slope_kernel,
        out_shape=[
            jax.ShapeDtypeStruct((rows, chans), BF),
            jax.ShapeDtypeStruct((chans, rows), BF),
        ],
        scratch_shapes=[pltpu.VMEM((chans // LANES, pix // 2, LANES), F32)],
        compiler_params=pltpu.CompilerParams(vmem_limit_bytes=32 * 2**20),
        cost_estimate=pl.CostEstimate(
            flops=8 * pix * chans, bytes_accessed=pix * chans * 8, transcendentals=pix * chans
        ),
    )(pre, dfeat)


def kernel_kernel(lines_ref, turned_ref, out_ref, sums_ref, flat_ref):
    step = pl.program_id(0)
    part, rows = turned_ref.shape
    chans = lines_ref.shape[1]
    turned = turned_ref[...].astype(F32)
    moved = [turned] + [pltpu.roll(turned, k, 1) for k in (1, 2)]
    moved = jnp.concatenate(moved, axis=0).astype(BF)

    for row in range(3):
        term = jnp.dot(
            moved, lines_ref[row * LINE : row * LINE + rows, :], preferred_element_type=F32
        )

        @pl.when(step == 0)
        def _():
            sums_ref[row] = term

        @pl.when(step > 0)
        def _():
            sums_ref[row] += term

    @pl.when(step == pl.num_programs(0) - 1)
    def _():
        for row in range(3):
            for col in range(3):
                tap = 3 * row + col
                flat_ref[tap * chans : (tap + 1) * chans, :] = sums_ref[
                    row, col * part : (col + 1) * part, :
                ].T
        count, size, _ = out_ref.shape
        for dest in range(count):
            at = dest * 2 * size
            both = [flat_ref[at : at + size, :], flat_ref[at + size : at + 2 * size, :]]
            out_ref[dest] = jnp.concatenate(both, axis=1).astype(BF)


def conv_kernel_grad(lines, turned, count):
    images, rows, chans = lines.shape
    _, part, cols = turned.shape
    size = 9 * chans // (2 * count)
    return pl.pallas_call(
        kernel_kernel,
        grid=(images,),
        in_specs=[
            pl.BlockSpec((None, rows, chans), lambda n: (n, 0, 0)),
            pl.BlockSpec((None, part, cols), lambda n: (n, 0, 0)),
        ],
        out_specs=pl.BlockSpec((count, size, 2 * part), lambda n: (0, 0, 0)),
        out_shape=jax.ShapeDtypeStruct((count, size, 2 * part), BF),
        scratch_shapes=[
            pltpu.VMEM((3, 3 * part, chans), F32),
            pltpu.VMEM((9 * chans, part), F32),
        ],
        compiler_params=pltpu.CompilerParams(vmem_limit_bytes=32 * 2**20),
        cost_estimate=pl.CostEstimate(
            flops=18 * images * cols * chans * part, bytes_accessed=lines.size * 2, transcendentals=0
        ),
    )(lines, turned)


def backward_kernel(lines_ref, weight_ref, out_ref, sums_ref):
    step = pl.program_id(0)
    col = lax.rem(step, 3)
    rows = sums_ref.shape[1]
    start = pl.multiple_of((2 - step // 3) * LINE, LINE)
    part = lax.dot_general(
        lines_ref[pl.ds(start, rows), :],
        weight_ref[...],
        (((1,), (1,)), ((), ())),
        preferred_element_type=F32,
    )

    @pl.when(step < 3)
    def _():
        sums_ref[col] = part

    @pl.when(step >= 3)
    def _():
        sums_ref[col] += part

    @pl.when(step == 8)
    def _():
        _, side, _, chans = out_ref.shape
        pix = side * LINE
        grad = sums_ref[0, 2 : pix + 2, :] + sums_ref[1, 1 : pix + 1, :] + sums_ref[2, 0:pix, :]
        out_ref[0] = grad.reshape(side, LINE, chans)[:, :side, :]


def conv_backward(lines, weight, side):
    chans = lines.shape[1]
    depth = weight.shape[0] // 9
    pix = side * LINE
    return pl.pallas_call(
        backward_kernel,
        grid=(9,),
        in_specs=[
            pl.BlockSpec(lines.shape, lambda t: (0, 0)),
            pl.BlockSpec((depth, chans), lambda t: (t, 0)),
        ],
        out_specs=pl.BlockSpec((1, side, side, depth), lambda t: (0, 0, 0, 0)),
        out_shape=jax.ShapeDtypeStruct((1, side, side, depth), F32),
        scratch_shapes=[pltpu.VMEM((3, pix + LINE, depth), F32)],
        compiler_params=pltpu.CompilerParams(vmem_limit_bytes=32 * 2**20),
        cost_estimate=pl.CostEstimate(
            flops=18 * pix * depth * chans, bytes_accessed=weight.size * 2, transcendentals=0
        ),
    )(lines, weight)


def dot(a, b, dims):
    return lax.dot_general(a, b, (dims, ((), ())), preferred_element_type=F32)


def swap(value, axis):
    return lax.all_to_all(value, axis, 0, 0, tiled=True)


def share(value, axis, count):
    return swap(jnp.broadcast_to(value, (count,) + value.shape), axis)


def bordered(maps):
    side, _, chans = maps.shape
    padded = jnp.pad(maps, ((1, 3), (1, LINE - side - 1), (0, 0)))
    return padded.reshape((side + 4) * LINE, chans)


def make(nx, nz, nc):
    ny = nz * nc

    def on_device(images, conv_weight, fc6_weight, fc7_weight, cotangent):
        side, chans = images.shape[1], images.shape[3]
        half = side // 2
        feats, units = fc6_weight.shape
        rows7, cols7 = fc7_weight.shape
        group = cotangent.shape[0] // nc
        wide = units * nc

        weight6 = lax.all_gather(fc6_weight, "core", axis=0, tiled=False)
        lines = bordered(images[0])
        gathered = lax.all_gather(lines, "gx", axis=0, tiled=False)
        send7 = fc7_weight.T.reshape(cols7, nz, wide).transpose(1, 0, 2)
        send7 = jnp.broadcast_to(send7[:, None], (nz, nc, cols7, wide)).reshape(ny, cols7, wide)
        weight7 = swap(send7, ("gz", "core")).reshape(ny * cols7, wide)
        cot = cotangent.T.reshape(cols7, nx, nz, nc).transpose(0, 3, 2, 1)
        cot = cot.reshape(cols7, nc * group).astype(F32)

        conv_pre, pooled = conv_forward(lines, conv_weight, side)
        pooled = pooled.reshape(half, half + 1, chans)[:, :half]
        feat = pooled.astype(BF).reshape(nx, feats)
        feat, weight7 = lax.optimization_barrier((feat, weight7))
        inputs = share(swap(feat, "gx"), "gz", nz).reshape(group, feats)

        weight6 = jnp.concatenate([weight6[k] for k in range(nc)], axis=1)
        inputs, weight6 = lax.optimization_barrier((inputs, weight6))
        h6_terms = dot(inputs, weight6, ((1,), (0,)))
        h6_pre = share(h6_terms.astype(BF), "gx", nx).astype(F32).sum(axis=0)
        hidden = activate(h6_pre).astype(BF)
        all_hidden = lax.all_gather(hidden, ("gz", "core"), axis=0, tiled=False)

        y7_terms = dot(weight7, hidden, ((1,), (1,))).astype(BF)
        y7_pre = swap(y7_terms.reshape(ny, cols7, group), ("gz", "core"))
        y7_pre = y7_pre.reshape(nz, nc, cols7, group).astype(F32).sum(axis=0)
        y7_pre = y7_pre.transpose(1, 0, 2).reshape(cols7, nc * group)
        g_seven = (cot * slope(y7_pre)).astype(BF)
        send = g_seven.reshape(cols7, nc, group).transpose(1, 0, 2)
        send = jnp.broadcast_to(send[None], (nz, nc, cols7, group)).reshape(ny, cols7, group)
        g7_cols = swap(send, ("gz", "core")).reshape(ny * cols7, group)

        dh6_terms = dot(g7_cols, weight7, ((0,), (0,))).astype(BF)
        grad_hidden = share(dh6_terms, "gx", nx).astype(F32).sum(axis=0)
        g_six = (grad_hidden * slope(h6_pre)).astype(BF)

        feat_terms = dot(g_six, weight6, ((1,), (1,))).astype(BF)
        feat_terms, g_late = lax.optimization_barrier((feat_terms, g_six))
        feat_terms = swap(feat_terms.reshape(nz, nx, feats), "gz")
        dfeat = swap(feat_terms.astype(F32).sum(axis=0).astype(BF), "gx")
        dfeat = dfeat.reshape(half, half, chans).astype(F32)
        dfeat = jnp.pad(dfeat, ((0, 0), (0, 1), (0, 0))).reshape(half * (half + 1), chans)

        g_lines, g_turned = conv_slope(conv_pre, dfeat, 2 * LANES)
        g_cols = swap(g_turned.reshape(nx, chans // nx, 2 * LANES), "gx")
        packed = swap(conv_kernel_grad(gathered, g_cols, ny), ("gz", "core"))
        packed = packed.astype(F32).sum(axis=0)
        part = chans // nx
        grad_conv = jnp.concatenate([packed[:, :part], packed[:, part:]], axis=0)

        grad6_terms = jnp.stack(
            [dot(inputs, g_late[:, k * units : (k + 1) * units], ((0,), (0,))) for k in range(nc)]
        )
        grad_fc6 = lax.psum_scatter(grad6_terms, "core", scatter_dimension=0, tiled=False)
        all_hidden = all_hidden.reshape(nz, nc, group, wide)
        grad7 = sum(
            dot(g_seven[:, k * group : (k + 1) * group], all_hidden[:, k], ((1,), (1,)))
            for k in range(nc)
        )
        grad_fc7 = grad7.reshape(cols7, rows7).T
        g_maps = g_lines[: side * LINE].reshape(side, LINE, chans)[:, :side]
        grad_images = conv_backward(bordered(g_maps), conv_weight, side)
        return (grad_conv, grad_fc6, grad_fc7, grad_images)

    return on_device


def solution(mesh):
    nx, ny = mesh.shape["gx"], mesh.shape["gy"]
    nc = 2
    nz = ny // nc
    fine = Mesh(mesh.devices.reshape(nx, nz, nc), ("gx", "gz", "core"))
    gy = ("gz", "core")
    both = ("gx", "gz", "core")
    return jax.shard_map(
        make(nx, nz, nc),
        mesh=fine,
        in_specs=(P(both, None, None, None), P(), P("gx", gy), P(None, both), P(None, both)),
        out_specs=(P(gy, "gx"), P("gx", gy), P(None, both), P(both, None, None, None)),
        check_vma=False,
    )
```

```python
import jax
import jax.numpy as jnp
from jax import lax
from jax.experimental import pallas as pl
from jax.experimental.pallas import tpu as pltpu
from jax.sharding import Mesh, PartitionSpec as P

BF = jnp.bfloat16
F32 = jnp.float32
LANES = 128
LINE = 16


def slope(value):
    sig = jax.nn.sigmoid(value)
    return sig * (1.0 + value * (1.0 - sig))


def activate(value):
    return value * jax.nn.sigmoid(value)


def forward_kernel(image_ref, weight_ref, pre_ref, feat_ref, sums_ref, pool_ref):
    step = pl.program_id(0)
    col = lax.rem(step, 3)
    rows = sums_ref.shape[1]
    start = pl.multiple_of((step // 3) * LINE, LINE)
    part = jnp.dot(
        image_ref[pl.ds(start, rows), :], weight_ref[...], preferred_element_type=F32
    )

    @pl.when(step < 3)
    def _():
        sums_ref[col] = part

    @pl.when(step >= 3)
    def _():
        sums_ref[col] += part

    @pl.when(step == 8)
    def _():
        pix, chans = pre_ref.shape
        pre = sums_ref[0, 0:pix, :] + sums_ref[1, 1 : pix + 1, :] + sums_ref[2, 2 : pix + 2, :]
        pre_ref[...] = pre
        act = activate(pre).reshape(pix // (2 * LINE), 2, LINE, chans)
        lines = (act[:, 0] + act[:, 1]).reshape(pix // 2, chans)
        half = pix // 4
        for k in range(chans // LANES):
            pool_ref[k] = lines[:, k * LANES : (k + 1) * LANES]
            total = pool_ref[k, pl.ds(0, half, 2), :] + pool_ref[k, pl.ds(1, half, 2), :]
            feat_ref[:, k * LANES : (k + 1) * LANES] = 0.25 * total


def conv_forward(lines, weight, side):
    chans = weight.shape[1]
    depth = lines.shape[1]
    pix = side * LINE
    return pl.pallas_call(
        forward_kernel,
        grid=(9,),
        in_specs=[
            pl.BlockSpec(lines.shape, lambda t: (0, 0)),
            pl.BlockSpec((depth, chans), lambda t: (t, 0)),
        ],
        out_specs=[
            pl.BlockSpec((pix, chans), lambda t: (0, 0)),
            pl.BlockSpec((pix // 4, chans), lambda t: (0, 0)),
        ],
        out_shape=[
            jax.ShapeDtypeStruct((pix, chans), F32),
            jax.ShapeDtypeStruct((pix // 4, chans), F32),
        ],
        scratch_shapes=[pltpu.VMEM((3, pix + LINE, chans), F32), pltpu.VMEM((chans // LANES, pix // 2, LANES), F32)],
        compiler_params=pltpu.CompilerParams(vmem_limit_bytes=32 * 2**20),
        cost_estimate=pl.CostEstimate(
            flops=18 * pix * depth * chans, bytes_accessed=weight.size * 2, transcendentals=pix * chans
        ),
    )(lines, weight)


def slope_kernel(pre_ref, dfeat_ref, lines_ref, turned_ref, wide_ref):
    pix, chans = pre_ref.shape
    half = pix // 4
    for k in range(chans // LANES):
        dfeat = dfeat_ref[:, k * LANES : (k + 1) * LANES]
        wide_ref[k, pl.ds(0, half, 2), :] = dfeat
        wide_ref[k, pl.ds(1, half, 2), :] = dfeat
    spread = jnp.concatenate([wide_ref[k] for k in range(chans // LANES)], axis=1)
    spread = spread.reshape(pix // (2 * LINE), 1, LINE, chans)
    spread = jnp.broadcast_to(spread, (pix // (2 * LINE), 2, LINE, chans)).reshape(pix, chans)
    grad = 0.25 * spread * slope(pre_ref[...])
    extra = turned_ref.shape[1] - pix
    grad = jnp.concatenate([grad, jnp.zeros((extra, chans), F32)], axis=0)
    turned_ref[...] = grad.T.astype(BF)
    lines_ref[...] = grad.astype(BF)


def conv_slope(pre, dfeat, rows):
    pix, chans = pre.shape
    return pl.pallas_call(
        slope_kernel,
        out_shape=[
            jax.ShapeDtypeStruct((rows, chans), BF),
            jax.ShapeDtypeStruct((chans, rows), BF),
        ],
        scratch_shapes=[pltpu.VMEM((chans // LANES, pix // 2, LANES), F32)],
        compiler_params=pltpu.CompilerParams(vmem_limit_bytes=32 * 2**20),
        cost_estimate=pl.CostEstimate(
            flops=8 * pix * chans, bytes_accessed=pix * chans * 8, transcendentals=pix * chans
        ),
    )(pre, dfeat)


def kernel_kernel(lines_ref, turned_ref, out_ref, sums_ref, flat_ref):
    step = pl.program_id(0)
    part, rows = turned_ref.shape
    chans = lines_ref.shape[1]
    turned = turned_ref[...].astype(F32)
    moved = [turned] + [pltpu.roll(turned, k, 1) for k in (1, 2)]
    moved = jnp.concatenate(moved, axis=0).astype(BF)

    for row in range(3):
        term = jnp.dot(
            moved, lines_ref[row * LINE : row * LINE + rows, :], preferred_element_type=F32
        )

        @pl.when(step == 0)
        def _():
            sums_ref[row] = term

        @pl.when(step > 0)
        def _():
            sums_ref[row] += term

    @pl.when(step == pl.num_programs(0) - 1)
    def _():
        for row in range(3):
            for col in range(3):
                tap = 3 * row + col
                flat_ref[tap * chans : (tap + 1) * chans, :] = sums_ref[
                    row, col * part : (col + 1) * part, :
                ].T
        count, size, _ = out_ref.shape
        for dest in range(count):
            at = dest * 2 * size
            both = [flat_ref[at : at + size, :], flat_ref[at + size : at + 2 * size, :]]
            out_ref[dest] = jnp.concatenate(both, axis=1).astype(BF)


def conv_kernel_grad(lines, turned, count):
    images, rows, chans = lines.shape
    _, part, cols = turned.shape
    size = 9 * chans // (2 * count)
    return pl.pallas_call(
        kernel_kernel,
        grid=(images,),
        in_specs=[
            pl.BlockSpec((None, rows, chans), lambda n: (n, 0, 0)),
            pl.BlockSpec((None, part, cols), lambda n: (n, 0, 0)),
        ],
        out_specs=pl.BlockSpec((count, size, 2 * part), lambda n: (0, 0, 0)),
        out_shape=jax.ShapeDtypeStruct((count, size, 2 * part), BF),
        scratch_shapes=[
            pltpu.VMEM((3, 3 * part, chans), F32),
            pltpu.VMEM((9 * chans, part), F32),
        ],
        compiler_params=pltpu.CompilerParams(vmem_limit_bytes=32 * 2**20),
        cost_estimate=pl.CostEstimate(
            flops=18 * images * cols * chans * part, bytes_accessed=lines.size * 2, transcendentals=0
        ),
    )(lines, turned)


def backward_kernel(lines_ref, weight_ref, out_ref, sums_ref):
    step = pl.program_id(0)
    col = lax.rem(step, 3)
    rows = sums_ref.shape[1]
    start = pl.multiple_of((2 - step // 3) * LINE, LINE)
    part = lax.dot_general(
        lines_ref[pl.ds(start, rows), :],
        weight_ref[...],
        (((1,), (1,)), ((), ())),
        preferred_element_type=F32,
    )

    @pl.when(step < 3)
    def _():
        sums_ref[col] = part

    @pl.when(step >= 3)
    def _():
        sums_ref[col] += part

    @pl.when(step == 8)
    def _():
        _, side, _, chans = out_ref.shape
        pix = side * LINE
        grad = sums_ref[0, 2 : pix + 2, :] + sums_ref[1, 1 : pix + 1, :] + sums_ref[2, 0:pix, :]
        out_ref[0] = grad.reshape(side, LINE, chans)[:, :side, :]


def conv_backward(lines, weight, side):
    chans = lines.shape[1]
    depth = weight.shape[0] // 9
    pix = side * LINE
    return pl.pallas_call(
        backward_kernel,
        grid=(9,),
        in_specs=[
            pl.BlockSpec(lines.shape, lambda t: (0, 0)),
            pl.BlockSpec((depth, chans), lambda t: (t, 0)),
        ],
        out_specs=pl.BlockSpec((1, side, side, depth), lambda t: (0, 0, 0, 0)),
        out_shape=jax.ShapeDtypeStruct((1, side, side, depth), F32),
        scratch_shapes=[pltpu.VMEM((3, pix + LINE, depth), F32)],
        compiler_params=pltpu.CompilerParams(vmem_limit_bytes=32 * 2**20),
        cost_estimate=pl.CostEstimate(
            flops=18 * pix * depth * chans, bytes_accessed=weight.size * 2, transcendentals=0
        ),
    )(lines, weight)


def dot(a, b, dims):
    return lax.dot_general(a, b, (dims, ((), ())), preferred_element_type=F32)


def swap(value, axis):
    return lax.all_to_all(value, axis, 0, 0, tiled=True)


def share(value, axis, count):
    return swap(jnp.broadcast_to(value, (count,) + value.shape), axis)


def bordered(maps):
    side, _, chans = maps.shape
    padded = jnp.pad(maps, ((1, 3), (1, LINE - side - 1), (0, 0)))
    return padded.reshape((side + 4) * LINE, chans)


def back_kernel(g_ref, weight_ref, out_ref):
    out_ref[...] = dot(g_ref[...], weight_ref[...], ((1,), (1,))).astype(BF)


def features_back(g_six, weight):
    count, feats = g_six.shape[0], weight.shape[0]
    return pl.pallas_call(
        back_kernel,
        out_shape=jax.ShapeDtypeStruct((count, feats), BF),
        compiler_params=pltpu.CompilerParams(vmem_limit_bytes=32 * 2**20),
        cost_estimate=pl.CostEstimate(
            flops=2 * count * weight.size, bytes_accessed=weight.size * 2, transcendentals=0
        ),
    )(g_six, weight)


def outer_kernel(inputs_ref, g_ref, out_ref):
    out_ref[0] = dot(inputs_ref[...], g_ref[...], ((0,), (0,))).astype(BF)


def weight_terms(inputs, g_six, parts):
    count, feats = inputs.shape
    units = g_six.shape[1] // parts
    return pl.pallas_call(
        outer_kernel,
        grid=(parts,),
        in_specs=[
            pl.BlockSpec((count, feats), lambda k: (0, 0)),
            pl.BlockSpec((count, units), lambda k: (0, k)),
        ],
        out_specs=pl.BlockSpec((1, feats, units), lambda k: (k, 0, 0)),
        out_shape=jax.ShapeDtypeStruct((parts, feats, units), BF),
        compiler_params=pltpu.CompilerParams(vmem_limit_bytes=32 * 2**20),
        cost_estimate=pl.CostEstimate(
            flops=2 * inputs.size * g_six.shape[1], bytes_accessed=4 * feats * units, transcendentals=0
        ),
    )(inputs, g_six)


def make(nx, nz, nc):
    ny = nz * nc
    near = nz // nx
    gy = ("gz", "core")

    def on_device(images, conv_weight, fc6_weight, fc7_weight, cotangent):
        side, chans = images.shape[1], images.shape[3]
        half = side // 2
        feats, units = fc6_weight.shape
        rows7, cols7 = fc7_weight.shape
        total = cotangent.shape[0]
        group = total // nc
        mine = group // nx
        wide = units * nc

        known = lax.all_gather(
            jnp.concatenate([fc7_weight.T, cotangent.T], axis=1), "gx", axis=0, tiled=False
        )
        gathered = lax.all_gather(images[0], "gx", axis=0, tiled=False)
        lines = bordered(images[0])
        weight6 = share(fc6_weight, "core", nc)
        conv_pre, pooled = conv_forward(lines, conv_weight, side)
        pooled = pooled.reshape(half, half + 1, chans)[:, :half]
        feat = pooled.astype(BF).reshape(nx, feats)
        feat, weight6 = lax.optimization_barrier((feat, weight6))
        inputs = share(swap(feat, "gx"), "gz", nz).reshape(group, feats)
        weight6 = jnp.concatenate([weight6[k] for k in range(nc)], axis=1)
        inputs, weight6 = lax.optimization_barrier((inputs, weight6))

        h6_terms = dot(inputs, weight6, ((1,), (0,))).astype(BF).reshape(nx, mine, wide)
        h6_pre = swap(h6_terms, "gx").astype(F32).sum(axis=0)
        own_hidden = activate(h6_pre).astype(BF)
        hidden = share(own_hidden, gy, ny).reshape(nz, nc, mine, wide)
        hidden = hidden.transpose(1, 2, 0, 3).reshape(nc * mine, rows7)

        known = known.reshape(nx * cols7, rows7 + total)
        weight7 = known[:, :rows7]
        place = lax.broadcasted_iota(jnp.int32, (total, nc * mine), 1)
        core, rest = place // mine, place % mine
        source = (rest % nx) * ny + (lax.axis_index("gx") * near + rest // nx) * nc + core
        pick = (lax.broadcasted_iota(jnp.int32, (total, nc * mine), 0) == source).astype(BF)
        cot = dot(known[:, rows7:], pick, ((1,), (0,)))
        y7_pre = dot(weight7, hidden, ((1,), (1,)))
        g_seven = (cot * slope(y7_pre)).astype(BF)
        dh6_terms = dot(g_seven, weight7, ((0,), (0,))).astype(BF)
        dh6_terms = dh6_terms.reshape(nc, mine, nz, wide).transpose(2, 0, 1, 3)
        grad_hidden = swap(dh6_terms.reshape(ny, mine, wide), gy).astype(F32).sum(axis=0)
        own_six = (grad_hidden * slope(h6_pre)).astype(BF)

        columns = g_seven.reshape(nx, cols7, nc * mine)
        columns = jnp.pad(columns, ((0, 0), (0, mine - cols7), (0, LANES - nc * mine)))
        both = jnp.concatenate([jnp.broadcast_to(own_six, (nx, mine, wide)), columns], axis=2)
        both = swap(both, "gx")
        g_six = both[:, :, :wide].reshape(group, wide)
        columns = both[:, :cols7, wide : wide + nc * mine]

        feat_terms = features_back(g_six, weight6).reshape(nz, nx, feats)
        dfeat = swap(swap(feat_terms, "gz").astype(F32).sum(axis=0).astype(BF), "gx")
        dfeat = dfeat.reshape(half, half, chans).astype(F32)
        dfeat = jnp.pad(dfeat, ((0, 0), (0, 1), (0, 0))).reshape(half * (half + 1), chans)

        g_lines, g_turned = conv_slope(conv_pre, dfeat, 2 * LANES)
        part = chans // nx
        g_cols = swap(g_turned.reshape(nx, part, 2 * LANES), "gx")
        all_lines = jax.vmap(bordered)(gathered)
        terms6 = weight_terms(inputs, g_six, nc)
        g_cols, terms6 = lax.optimization_barrier((g_cols, terms6))
        terms6 = swap(terms6, "core")
        packed = conv_kernel_grad(all_lines, g_cols, ny)
        packed, terms6 = lax.optimization_barrier((packed, terms6))
        packed = swap(packed, gy).astype(F32).sum(axis=0)
        grad_conv = jnp.concatenate([packed[:, :part], packed[:, part:]], axis=0)
        grad_fc6 = terms6.astype(F32).sum(axis=0)

        all_hidden = lax.all_gather(hidden, "gx", axis=0, tiled=False).reshape(total, rows7)
        columns = columns.transpose(1, 0, 2).reshape(cols7, total)
        grad_fc7 = dot(columns, all_hidden, ((1,), (0,))).T
        g_maps = g_lines[: side * LINE].reshape(side, LINE, chans)[:, :side]
        grad_images = conv_backward(bordered(g_maps), conv_weight, side)
        return (grad_conv, grad_fc6, grad_fc7, grad_images)

    return on_device


def solution(mesh):
    nx, ny = mesh.shape["gx"], mesh.shape["gy"]
    nc = 2
    nz = ny // nc
    fine = Mesh(mesh.devices.reshape(nx, nz, nc), ("gx", "gz", "core"))
    gy = ("gz", "core")
    both = ("gx", "gz", "core")
    return jax.shard_map(
        make(nx, nz, nc),
        mesh=fine,
        in_specs=(P(both, None, None, None), P(), P("gx", gy), P(None, both), P(None, both)),
        out_specs=(P(gy, "gx"), P("gx", gy), P(None, both), P(both, None, None, None)),
        check_vma=False,
    )
```

```python
import jax
import jax.numpy as jnp
from jax import lax
from jax.experimental import pallas as pl
from jax.experimental.pallas import tpu as pltpu
from jax.sharding import Mesh, PartitionSpec as P

BF = jnp.bfloat16
F32 = jnp.float32
LANES = 128
LINE = 16
VMEM = pltpu.CompilerParams(vmem_limit_bytes=20 * 2**20)


def activate(value):
    return value * jax.nn.sigmoid(value)


def slope(value):
    sig = jax.nn.sigmoid(value)
    return sig * (1.0 + value * (1.0 - sig))


def dot(a, b, dims):
    return lax.dot_general(a, b, (dims, ((), ())), preferred_element_type=F32)


def cost(flops, moved, special=0):
    return pl.CostEstimate(flops=flops, bytes_accessed=moved, transcendentals=special)


def forward_kernel(image_ref, weight_ref, pre_ref, feat_ref, held_ref, sums_ref, pool_ref, sems):
    pix, chans = pre_ref.shape
    depth = image_ref.shape[1]
    rows = sums_ref.shape[1]

    def load(tap):
        return pltpu.make_async_copy(
            weight_ref.at[pl.ds(tap * depth, depth), :],
            held_ref.at[tap % 3, pl.ds(tap // 3 * depth, depth), :],
            sems.at[tap],
        )

    order = [3 * row + col for col in range(3) for row in range(3)]
    for tap in order:
        load(tap).start()
    image = jnp.concatenate([image_ref[k * LINE : k * LINE + rows, :] for k in range(3)], axis=1)
    for col in range(3):
        for row in range(3):
            load(3 * row + col).wait()
        sums_ref[col] = dot(image, held_ref[col], ((1,), (0,)))
    pre = sums_ref[0, 0:pix, :] + sums_ref[1, 1 : pix + 1, :] + sums_ref[2, 2 : pix + 2, :]
    pre_ref[...] = pre
    act = activate(pre).reshape(pix // (2 * LINE), 2, LINE, chans)
    lines = (act[:, 0] + act[:, 1]).reshape(pix // 2, chans)
    half = pix // 4
    for k in range(chans // LANES):
        pool_ref[k] = lines[:, k * LANES : (k + 1) * LANES]
        total = pool_ref[k, pl.ds(0, half, 2), :] + pool_ref[k, pl.ds(1, half, 2), :]
        feat_ref[:, k * LANES : (k + 1) * LANES] = (0.25 * total).astype(BF)


def conv_forward(lines, weight, side):
    depth, chans = lines.shape[1], weight.shape[1]
    pix = side * LINE
    return pl.pallas_call(
        forward_kernel,
        in_specs=[
            pl.BlockSpec(memory_space=pltpu.VMEM),
            pl.BlockSpec(memory_space=pl.ANY),
        ],
        out_shape=[
            jax.ShapeDtypeStruct((pix, chans), F32),
            jax.ShapeDtypeStruct((pix // 4, chans), BF),
        ],
        scratch_shapes=[
            pltpu.VMEM((3, 3 * depth, chans), BF),
            pltpu.VMEM((3, pix + LINE, chans), F32),
            pltpu.VMEM((chans // LANES, pix // 2, LANES), F32),
            pltpu.SemaphoreType.DMA((9,)),
        ],
        compiler_params=VMEM,
        cost_estimate=cost(18 * pix * depth * chans, weight.size * 2, pix * chans),
    )(lines, weight)


def turn_kernel(pre_ref, out_ref):
    pix, chans = pre_ref.shape
    grad = 0.25 * slope(pre_ref[...])
    grad = jnp.concatenate([grad, jnp.zeros((out_ref.shape[1] - pix, chans), F32)], axis=0)
    out_ref[...] = grad.T.astype(BF)


def turned_slope(pre, cols):
    pix, chans = pre.shape
    return pl.pallas_call(
        turn_kernel,
        out_shape=jax.ShapeDtypeStruct((chans, cols), BF),
        compiler_params=VMEM,
        cost_estimate=cost(8 * pix * chans, pix * chans * 6, pix * chans),
    )(pre)


def lines_kernel(pre_ref, dfeat_ref, out_ref, wide_ref):
    pix, chans = pre_ref.shape
    half = pix // 4
    for k in range(chans // LANES):
        dfeat = dfeat_ref[:, k * LANES : (k + 1) * LANES]
        wide_ref[k, pl.ds(0, half, 2), :] = dfeat
        wide_ref[k, pl.ds(1, half, 2), :] = dfeat
    spread = jnp.concatenate([wide_ref[k] for k in range(chans // LANES)], axis=1)
    spread = spread.reshape(pix // (2 * LINE), 1, LINE, chans)
    spread = jnp.broadcast_to(spread, (pix // (2 * LINE), 2, LINE, chans)).reshape(pix, chans)
    out_ref[...] = (0.25 * spread * slope(pre_ref[...])).astype(BF)


def conv_slope(pre, dfeat):
    pix, chans = pre.shape
    return pl.pallas_call(
        lines_kernel,
        out_shape=jax.ShapeDtypeStruct((pix, chans), BF),
        scratch_shapes=[pltpu.VMEM((chans // LANES, pix // 2, LANES), F32)],
        compiler_params=VMEM,
        cost_estimate=cost(8 * pix * chans, pix * chans * 6, pix * chans),
    )(pre, dfeat)


def fc7_kernel(known_ref, hidden_ref, pick_ref, seven_ref, terms_ref):
    count, mine, wide = hidden_ref.shape
    rows7 = count // 2 * wide
    y7_pre = jnp.zeros(seven_ref.shape, F32)
    for g in range(count // 2):
        block = hidden_ref[2 * g : 2 * g + 2].reshape(2 * mine, wide)
        y7_pre += dot(known_ref[:, g * wide : (g + 1) * wide], block, ((1,), (1,)))
    cot = dot(known_ref[:, rows7:], pick_ref[...], ((1,), (0,)))
    seven = (cot * slope(y7_pre)).astype(BF)
    seven_ref[...] = seven
    for g in range(count // 2):
        part = dot(seven, known_ref[:, g * wide : (g + 1) * wide], ((0,), (0,)))
        terms_ref[2 * g : 2 * g + 2] = part.astype(BF).reshape(2, mine, wide)


def fc7_step(known, hidden, pick):
    cols = known.shape[0]
    return pl.pallas_call(
        fc7_kernel,
        out_shape=[
            jax.ShapeDtypeStruct((cols, pick.shape[1]), BF),
            jax.ShapeDtypeStruct(hidden.shape, BF),
        ],
        compiler_params=VMEM,
        cost_estimate=cost(4 * known.size * pick.shape[1], known.size * 2),
    )(known, hidden, pick)


def back_kernel(g_ref, weight_ref, out_ref):
    out_ref[...] = dot(g_ref[...], weight_ref[...], ((1,), (1,))).astype(BF)


def features_back(g_six, weight):
    count, feats = g_six.shape[0], weight.shape[0]
    return pl.pallas_call(
        back_kernel,
        out_shape=jax.ShapeDtypeStruct((count, feats), BF),
        compiler_params=VMEM,
        cost_estimate=cost(2 * count * weight.size, weight.size * 2),
    )(g_six, weight)


def outer_kernel(which_ref, inputs_ref, g_ref, out_ref):
    units = out_ref.shape[1]
    g_six = g_ref[:, pl.ds(pl.multiple_of(which_ref[0] * units, units), units)]
    out_ref[...] = dot(inputs_ref[...], g_six, ((0,), (0,))).astype(out_ref.dtype)


def outer_add_kernel(which_ref, inputs_ref, g_ref, more_ref, out_ref):
    units = out_ref.shape[1]
    g_six = g_ref[:, pl.ds(pl.multiple_of(which_ref[0] * units, units), units)]
    out_ref[...] = dot(inputs_ref[...], g_six, ((0,), (0,))) + more_ref[...].astype(F32)


def weight_terms(which, inputs, g_six, units, more=None):
    feats = inputs.shape[1]
    operands = (inputs, g_six) if more is None else (inputs, g_six, more)
    in_vmem = [pl.BlockSpec(memory_space=pltpu.VMEM)] * len(operands)
    return pl.pallas_call(
        outer_kernel if more is None else outer_add_kernel,
        in_specs=[pl.BlockSpec(memory_space=pltpu.SMEM)] + in_vmem,
        out_shape=jax.ShapeDtypeStruct((feats, units), BF if more is None else F32),
        compiler_params=VMEM,
        cost_estimate=cost(2 * inputs.size * units, 4 * feats * units),
    )(which.reshape(1).astype(jnp.int32), *operands)


def pack_kernel(me_ref, terms_ref, out_ref, parts_ref, own_ref):
    nx, rows, _ = out_ref.shape
    feats = terms_ref.shape[2]
    run = LANES // 2
    runs = feats // run
    total = terms_ref[...].astype(F32).sum(axis=0).astype(BF).astype(F32)
    total = jnp.concatenate([total, jnp.zeros((nx, -feats % LANES), F32)], axis=1)
    parts_ref[...] = jnp.zeros(parts_ref.shape, F32)
    own_ref[...] = jnp.zeros(own_ref.shape, F32)
    for t in range(runs):
        tile = total[:, t // 2 * LANES : (t // 2 + 1) * LANES]
        other = pltpu.roll(tile, run, 1)
        low, high = (tile, other) if t % 2 == 0 else (other, tile)
        parts_ref[t % nx, t // nx * nx : (t // nx + 1) * nx, :] = low
        own_ref[pl.ds(t, nx, rows), :] = high
    lane = lax.broadcasted_iota(jnp.int32, (rows, LANES), 1)
    for e in range(nx):
        dest = lax.rem(me_ref[0] + e, nx)
        own = own_ref[pl.ds(pl.multiple_of(dest * rows, rows), rows), :]
        out_ref[dest] = jnp.where(lane < run, parts_ref[e], own).astype(BF)


def pack_dfeat(me, terms):
    _, nx, feats = terms.shape
    rows = nx * nx
    return pl.pallas_call(
        pack_kernel,
        in_specs=[
            pl.BlockSpec(memory_space=pltpu.SMEM),
            pl.BlockSpec(memory_space=pltpu.VMEM),
        ],
        out_shape=jax.ShapeDtypeStruct((nx, rows, LANES), BF),
        scratch_shapes=[
            pltpu.VMEM((nx, rows, LANES), F32),
            pltpu.VMEM((nx * rows, LANES), F32),
        ],
        compiler_params=VMEM,
        cost_estimate=cost(4 * terms.size, terms.size * 2),
    )(me, terms)


def kernel_kernel(lines_ref, slope_ref, dfeat_ref, spread_ref, out_ref, grad_ref, flat_ref, wide_ref):
    images, part, cols = slope_ref.shape
    chans = lines_ref.shape[2]
    wide_ref[...] = dfeat_ref[...].astype(F32).reshape(wide_ref.shape)
    for n in range(images):
        cells = wide_ref[pl.ds(n, wide_ref.shape[0] // images, images), :].astype(BF)
        spread = dot(cells, spread_ref[...], ((0,), (0,)))[:part]
        turned = (spread * slope_ref[n].astype(F32)).astype(BF).astype(F32)
        moved = [turned] + [pltpu.roll(turned, k, 1) for k in (1, 2)]
        grad_ref[:, n * cols : (n + 1) * cols] = jnp.concatenate(moved, axis=0).astype(BF)
    for row in range(3):
        block = lines_ref[:, row * LINE : row * LINE + cols, :].reshape(images * cols, chans)
        term = dot(grad_ref[...], block, ((1,), (0,)))
        for col in range(3):
            tap = 3 * row + col
            flat_ref[tap * chans : (tap + 1) * chans, :] = term[col * part : (col + 1) * part].T
    count, size, _ = out_ref.shape
    for dest in range(count):
        at = dest * 2 * size
        both = [flat_ref[at : at + size, :], flat_ref[at + size : at + 2 * size, :]]
        out_ref[dest] = jnp.concatenate(both, axis=1).astype(BF)


def conv_kernel_grad(lines, slopes, dfeat, spread, count):
    images, rows, chans = lines.shape
    _, part, cols = slopes.shape
    size = 9 * chans // (2 * count)
    return pl.pallas_call(
        kernel_kernel,
        out_shape=jax.ShapeDtypeStruct((count, size, 2 * part), BF),
        scratch_shapes=[
            pltpu.VMEM((3 * part, images * cols), BF),
            pltpu.VMEM((9 * chans, part), F32),
            pltpu.VMEM((dfeat.shape[0] * dfeat.shape[1], LANES), F32),
        ],
        compiler_params=VMEM,
        cost_estimate=cost(18 * images * cols * chans * part, lines.size * 2),
    )(lines, slopes, dfeat, spread)


def backward_kernel(lines_ref, weight_ref, out_ref, sums_ref):
    step = pl.program_id(0)
    col = lax.rem(step, 3)
    rows = sums_ref.shape[1]
    start = pl.multiple_of((2 - step // 3) * LINE, LINE)
    part = dot(lines_ref[pl.ds(start, rows), :], weight_ref[...], ((1,), (1,)))

    @pl.when(step < 3)
    def _():
        sums_ref[col] = part

    @pl.when(step >= 3)
    def _():
        sums_ref[col] += part

    @pl.when(step == 8)
    def _():
        _, side, _, chans = out_ref.shape
        pix = side * LINE
        grad = sums_ref[0, 2 : pix + 2, :] + sums_ref[1, 1 : pix + 1, :] + sums_ref[2, 0:pix, :]
        out_ref[0] = grad.reshape(side, LINE, chans)[:, :side, :]


def conv_backward(lines, weight, side):
    chans = lines.shape[1]
    depth = weight.shape[0] // 9
    pix = side * LINE
    return pl.pallas_call(
        backward_kernel,
        grid=(9,),
        in_specs=[
            pl.BlockSpec(lines.shape, lambda t: (0, 0)),
            pl.BlockSpec((depth, chans), lambda t: (t, 0)),
        ],
        out_specs=pl.BlockSpec((1, side, side, depth), lambda t: (0, 0, 0, 0)),
        out_shape=jax.ShapeDtypeStruct((1, side, side, depth), F32),
        scratch_shapes=[pltpu.VMEM((3, pix + LINE, depth), F32)],
        compiler_params=VMEM,
        cost_estimate=cost(18 * pix * depth * chans, weight.size * 2),
    )(lines, weight)


def spread_matrix(me, nx, half, cols):
    at = lax.broadcasted_iota(jnp.int32, (nx * nx, cols), 0)
    pixel = lax.broadcasted_iota(jnp.int32, (nx * nx, cols), 1)
    source, run = at // nx, at % nx
    line, place = pixel // LINE, pixel % LINE
    per = half * half // nx
    cell = jnp.where((line < 2 * half) & (place < 2 * half), line // 2 * half + place // 2, -1)
    mine = per * source + run + (me < source).astype(jnp.int32)
    return ((cell == mine) & (run <= per)).astype(BF)


def swap(value, axis):
    return lax.all_to_all(value, axis, 0, 0, tiled=True)


def share(value, axis, count):
    return swap(jnp.broadcast_to(value, (count,) + value.shape), axis)


def bordered(maps):
    side, _, chans = maps.shape
    padded = jnp.pad(maps, ((1, 3), (1, LINE - side - 1), (0, 0)))
    return padded.reshape((side + 4) * LINE, chans)


def make(nx, nz, nc):
    ny = nz * nc
    near = nz // nx
    gy = ("gz", "core")
    pair = [(k, nc - 1 - k) for k in range(nc)]

    def on_device(images, conv_weight, fc6_weight, fc7_weight, cotangent):
        side, chans = images.shape[1], images.shape[3]
        half = side // 2
        feats, units = fc6_weight.shape
        rows7, cols7 = fc7_weight.shape
        total = cotangent.shape[0]
        group = total // nc
        mine = group // nx
        wide = units * nc
        part = chans // nx
        cols = 2 * LANES
        me, core = lax.axis_index("gx"), lax.axis_index("core")

        known = lax.all_gather(
            jnp.concatenate([fc7_weight.T, cotangent.T], axis=1), "gx", axis=0, tiled=False
        )
        gathered = lax.all_gather(images[0], "gx", axis=0, tiled=False)
        other6 = lax.ppermute(fc6_weight, "core", pair)
        lines = bordered(images[0])
        conv_pre, pooled = conv_forward(lines, conv_weight, side)
        slopes = turned_slope(conv_pre, cols).reshape(nx, part, cols)
        feat = pooled.reshape(half, half + 1, chans)[:, :half].reshape(nx, feats)
        inputs = share(swap(feat, "gx"), "gz", nz).reshape(group, feats)
        first = jnp.where(core == 0, fc6_weight, other6)
        second = jnp.where(core == 0, other6, fc6_weight)
        weight6 = jnp.concatenate([first, second], axis=1)
        inputs, weight6 = lax.optimization_barrier((inputs, weight6))

        h6_terms = dot(inputs, weight6, ((1,), (0,))).astype(BF).reshape(nx, mine, wide)
        both = swap(jnp.concatenate([h6_terms, slopes], axis=1), "gx")
        h6_pre = both[:, :mine].astype(F32).sum(axis=0)
        slopes = both[:, mine:]
        own_hidden = activate(h6_pre).astype(BF)
        hidden = share(own_hidden, gy, ny)

        place = lax.broadcasted_iota(jnp.int32, (total, nc * mine), 1)
        half_of, rest = place // mine, place % mine
        source = (rest % nx) * ny + (me * near + rest // nx) * nc + half_of
        pick = (lax.broadcasted_iota(jnp.int32, (total, nc * mine), 0) == source).astype(BF)
        g_seven, dh6_terms = fc7_step(known.reshape(nx * cols7, rows7 + total), hidden, pick)
        grad_hidden = swap(dh6_terms, gy).astype(F32).sum(axis=0)
        own_six = (grad_hidden * slope(h6_pre)).astype(BF)

        columns = g_seven.reshape(nx, cols7, nc * mine)
        columns = jnp.pad(columns, ((0, 0), (0, mine - cols7), (0, LANES - nc * mine)))
        both = jnp.concatenate([jnp.broadcast_to(own_six, (nx, mine, wide)), columns], axis=2)
        both = swap(both, "gx")
        g_six = both[:, :, :wide].reshape(group, wide)
        columns = both[:, :cols7, wide : wide + nc * mine]

        feat_terms = features_back(g_six, weight6).reshape(nz, nx, feats)
        feat_terms, g_six = lax.optimization_barrier((feat_terms, g_six))
        feat_terms = swap(feat_terms, "gz")
        sent6 = weight_terms(nc - 1 - core, inputs, g_six, units)
        packs = pack_dfeat(me.reshape(1).astype(jnp.int32), feat_terms)
        packs = swap(packs, "gx")
        gathered, sent6 = lax.optimization_barrier((gathered, sent6))
        all_lines = jax.vmap(bordered)(gathered)
        grad_fc6 = weight_terms(core, inputs, g_six, units, lax.ppermute(sent6, "core", pair))
        spread = spread_matrix(me, nx, half, cols)
        packed = conv_kernel_grad(all_lines, slopes, packs, spread, ny)
        packed = swap(packed, gy)

        runs = feats // part
        dfeat = packs[:, :runs, part : 2 * part].reshape(half, half, chans).astype(F32)
        dfeat = jnp.pad(dfeat, ((0, 0), (0, 1), (0, 0))).reshape(half * (half + 1), chans)
        g_lines = conv_slope(conv_pre, dfeat).reshape(side, LINE, chans)[:, :side]
        grad_images = conv_backward(bordered(g_lines), conv_weight, side)

        hidden = hidden.reshape(nz, nc * mine, wide).transpose(1, 0, 2).reshape(nc * mine, rows7)
        all_hidden = lax.all_gather(hidden, "gx", axis=0, tiled=False).reshape(total, rows7)
        columns = columns.transpose(1, 0, 2).reshape(cols7, total)
        grad_fc7 = dot(columns, all_hidden, ((1,), (0,))).T
        packed, grad_fc7 = lax.optimization_barrier((packed, grad_fc7))
        packed = packed.astype(F32).sum(axis=0)
        grad_conv = jnp.concatenate([packed[:, :part], packed[:, part:]], axis=0)
        return (grad_conv, grad_fc6, grad_fc7, grad_images)

    return on_device


def solution(mesh):
    nx, ny = mesh.shape["gx"], mesh.shape["gy"]
    nc = 2
    nz = ny // nc
    fine = Mesh(mesh.devices.reshape(nx, nz, nc), ("gx", "gz", "core"))
    gy = ("gz", "core")
    both = ("gx", "gz", "core")
    return jax.shard_map(
        make(nx, nz, nc),
        mesh=fine,
        in_specs=(P(both, None, None, None), P(), P("gx", gy), P(None, both), P(None, both)),
        out_specs=(P(gy, "gx"), P("gx", gy), P(None, both), P(both, None, None, None)),
        check_vma=False,
    )
```

```python
import jax
import jax.numpy as jnp
from jax import lax
from jax.experimental import pallas as pl
from jax.experimental.pallas import tpu as pltpu
from jax.sharding import Mesh, PartitionSpec as P

BF = jnp.bfloat16
F32 = jnp.float32
LANES = 128
LINE = 16
VMEM = pltpu.CompilerParams(vmem_limit_bytes=20 * 2**20)


def activate(value):
    return value * jax.nn.sigmoid(value)


def slope(value):
    sig = jax.nn.sigmoid(value)
    return sig * (1.0 + value * (1.0 - sig))


def dot(a, b, dims):
    return lax.dot_general(a, b, (dims, ((), ())), preferred_element_type=F32)


def cost(flops, moved, special=0):
    return pl.CostEstimate(flops=flops, bytes_accessed=moved, transcendentals=special)


def forward_kernel(image_ref, weight_ref, pre_ref, feat_ref, held_ref, sums_ref, pool_ref, sems):
    pix, chans = pre_ref.shape
    depth = image_ref.shape[1]
    rows = sums_ref.shape[1]

    def load(tap):
        return pltpu.make_async_copy(
            weight_ref.at[pl.ds(tap * depth, depth), :],
            held_ref.at[tap % 3, pl.ds(tap // 3 * depth, depth), :],
            sems.at[tap],
        )

    order = [3 * row + col for col in range(3) for row in range(3)]
    for tap in order:
        load(tap).start()
    image = jnp.concatenate([image_ref[k * LINE : k * LINE + rows, :] for k in range(3)], axis=1)
    for col in range(3):
        for row in range(3):
            load(3 * row + col).wait()
        sums_ref[col] = dot(image, held_ref[col], ((1,), (0,)))
    pre = sums_ref[0, 0:pix, :] + sums_ref[1, 1 : pix + 1, :] + sums_ref[2, 2 : pix + 2, :]
    pre_ref[...] = pre
    act = activate(pre).reshape(pix // (2 * LINE), 2, LINE, chans)
    lines = (act[:, 0] + act[:, 1]).reshape(pix // 2, chans)
    half = pix // 4
    for k in range(chans // LANES):
        pool_ref[k] = lines[:, k * LANES : (k + 1) * LANES]
        total = pool_ref[k, pl.ds(0, half, 2), :] + pool_ref[k, pl.ds(1, half, 2), :]
        feat_ref[:, k * LANES : (k + 1) * LANES] = (0.25 * total).astype(BF)


def conv_forward(lines, weight, side):
    depth, chans = lines.shape[1], weight.shape[1]
    pix = side * LINE
    return pl.pallas_call(
        forward_kernel,
        in_specs=[
            pl.BlockSpec(memory_space=pltpu.VMEM),
            pl.BlockSpec(memory_space=pl.ANY),
        ],
        out_shape=[
            jax.ShapeDtypeStruct((pix, chans), F32),
            jax.ShapeDtypeStruct((pix // 4, chans), BF),
        ],
        scratch_shapes=[
            pltpu.VMEM((3, 3 * depth, chans), BF),
            pltpu.VMEM((3, pix + LINE, chans), F32),
            pltpu.VMEM((chans // LANES, pix // 2, LANES), F32),
            pltpu.SemaphoreType.DMA((9,)),
        ],
        compiler_params=VMEM,
        cost_estimate=cost(18 * pix * depth * chans, weight.size * 2, pix * chans),
    )(lines, weight)


def turn_kernel(pre_ref, out_ref):
    pix, chans = pre_ref.shape
    grad = 0.25 * slope(pre_ref[...])
    grad = jnp.concatenate([grad, jnp.zeros((out_ref.shape[1] - pix, chans), F32)], axis=0)
    out_ref[...] = grad.T.astype(BF)


def turned_slope(pre, cols):
    pix, chans = pre.shape
    return pl.pallas_call(
        turn_kernel,
        out_shape=jax.ShapeDtypeStruct((chans, cols), BF),
        compiler_params=VMEM,
        cost_estimate=cost(8 * pix * chans, pix * chans * 6, pix * chans),
    )(pre)


def lines_kernel(pre_ref, dfeat_ref, out_ref, wide_ref):
    pix, chans = pre_ref.shape
    half = pix // 4
    for k in range(chans // LANES):
        dfeat = dfeat_ref[:, k * LANES : (k + 1) * LANES]
        wide_ref[k, pl.ds(0, half, 2), :] = dfeat
        wide_ref[k, pl.ds(1, half, 2), :] = dfeat
    spread = jnp.concatenate([wide_ref[k] for k in range(chans // LANES)], axis=1)
    spread = spread.reshape(pix // (2 * LINE), 1, LINE, chans)
    spread = jnp.broadcast_to(spread, (pix // (2 * LINE), 2, LINE, chans)).reshape(pix, chans)
    out_ref[...] = (0.25 * spread * slope(pre_ref[...])).astype(BF)


def conv_slope(pre, dfeat):
    pix, chans = pre.shape
    return pl.pallas_call(
        lines_kernel,
        out_shape=jax.ShapeDtypeStruct((pix, chans), BF),
        scratch_shapes=[pltpu.VMEM((chans // LANES, pix // 2, LANES), F32)],
        compiler_params=VMEM,
        cost_estimate=cost(8 * pix * chans, pix * chans * 6, pix * chans),
    )(pre, dfeat)


def fc7_kernel(own_ref, other_ref, hidden_ref, pick_ref, seven_ref, terms_ref):
    count, mine, wide = hidden_ref.shape
    rows7 = count * wide
    weights = (own_ref, other_ref)
    sevens = []
    for k, ref in enumerate(weights):
        y7_pre = jnp.zeros((ref.shape[0], mine), F32)
        for g in range(count):
            y7_pre += dot(ref[:, g * wide : (g + 1) * wide], hidden_ref[g], ((1,), (1,)))
        cot = dot(ref[:, rows7:], pick_ref[...], ((1,), (0,)))
        sevens.append((cot * slope(y7_pre)).astype(BF))
        seven_ref[:, k * mine : (k + 1) * mine] = sevens[k]
    for g in range(count):
        parts = [dot(v, ref[:, g * wide : (g + 1) * wide], ((0,), (0,))) for v, ref in zip(sevens, weights)]
        terms_ref[g] = (parts[0] + parts[1]).astype(BF)


def fc7_step(own, other, hidden, pick):
    cols = own.shape[0]
    return pl.pallas_call(
        fc7_kernel,
        out_shape=[
            jax.ShapeDtypeStruct((cols, 2 * pick.shape[1]), BF),
            jax.ShapeDtypeStruct(hidden.shape, BF),
        ],
        compiler_params=VMEM,
        cost_estimate=cost(8 * own.size * pick.shape[1], own.size * 4),
    )(own, other, hidden, pick)


def back_kernel(g_ref, weight_ref, out_ref):
    out_ref[...] = dot(g_ref[...], weight_ref[...], ((1,), (1,))).astype(BF)


def features_back(g_six, weight):
    count, feats = g_six.shape[0], weight.shape[0]
    return pl.pallas_call(
        back_kernel,
        out_shape=jax.ShapeDtypeStruct((count, feats), BF),
        compiler_params=VMEM,
        cost_estimate=cost(2 * count * weight.size, weight.size * 2),
    )(g_six, weight)


def outer_kernel(which_ref, inputs_ref, g_ref, out_ref):
    units = out_ref.shape[1]
    g_six = g_ref[:, pl.ds(pl.multiple_of(which_ref[0] * units, units), units)]
    out_ref[...] = dot(inputs_ref[...], g_six, ((0,), (0,))).astype(out_ref.dtype)


def outer_add_kernel(which_ref, inputs_ref, g_ref, more_ref, out_ref):
    units = out_ref.shape[1]
    g_six = g_ref[:, pl.ds(pl.multiple_of(which_ref[0] * units, units), units)]
    out_ref[...] = dot(inputs_ref[...], g_six, ((0,), (0,))) + more_ref[...].astype(F32)


def weight_terms(which, inputs, g_six, units, more=None):
    feats = inputs.shape[1]
    operands = (inputs, g_six) if more is None else (inputs, g_six, more)
    in_vmem = [pl.BlockSpec(memory_space=pltpu.VMEM)] * len(operands)
    return pl.pallas_call(
        outer_kernel if more is None else outer_add_kernel,
        in_specs=[pl.BlockSpec(memory_space=pltpu.SMEM)] + in_vmem,
        out_shape=jax.ShapeDtypeStruct((feats, units), BF if more is None else F32),
        compiler_params=VMEM,
        cost_estimate=cost(2 * inputs.size * units, 4 * feats * units),
    )(which.reshape(1).astype(jnp.int32), *operands)


def pack_kernel(me_ref, terms_ref, out_ref, parts_ref, own_ref):
    nx, rows, _ = out_ref.shape
    feats = terms_ref.shape[2]
    run = LANES // 2
    runs = feats // run
    total = terms_ref[...].astype(F32).sum(axis=0).astype(BF).astype(F32)
    total = jnp.concatenate([total, jnp.zeros((nx, -feats % LANES), F32)], axis=1)
    parts_ref[...] = jnp.zeros(parts_ref.shape, F32)
    own_ref[...] = jnp.zeros(own_ref.shape, F32)
    for t in range(runs):
        tile = total[:, t // 2 * LANES : (t // 2 + 1) * LANES]
        other = pltpu.roll(tile, run, 1)
        low, high = (tile, other) if t % 2 == 0 else (other, tile)
        parts_ref[t % nx, t // nx * nx : (t // nx + 1) * nx, :] = low
        own_ref[pl.ds(t, nx, rows), :] = high
    lane = lax.broadcasted_iota(jnp.int32, (rows, LANES), 1)
    for e in range(nx):
        dest = lax.rem(me_ref[0] + e, nx)
        own = own_ref[pl.ds(pl.multiple_of(dest * rows, rows), rows), :]
        out_ref[dest] = jnp.where(lane < run, parts_ref[e], own).astype(BF)


def pack_dfeat(me, terms):
    _, nx, feats = terms.shape
    rows = nx * nx
    return pl.pallas_call(
        pack_kernel,
        in_specs=[
            pl.BlockSpec(memory_space=pltpu.SMEM),
            pl.BlockSpec(memory_space=pltpu.VMEM),
        ],
        out_shape=jax.ShapeDtypeStruct((nx, rows, LANES), BF),
        scratch_shapes=[
            pltpu.VMEM((nx, rows, LANES), F32),
            pltpu.VMEM((nx * rows, LANES), F32),
        ],
        compiler_params=VMEM,
        cost_estimate=cost(4 * terms.size, terms.size * 2),
    )(me, terms)


def kernel_kernel(me_ref, slope_ref, dfeat_ref, spread_ref, *refs):
    images, part, cols = slope_ref.shape
    lines_refs = refs[:images]
    out_ref, grad_ref, flat_ref, wide_ref = refs[images:]
    chans = lines_refs[0].shape[1]
    wide_ref[...] = dfeat_ref[...].astype(F32).reshape(wide_ref.shape)
    for k in range(images):
        n = lax.rem(me_ref[0] + images - k, images)
        cells = wide_ref[pl.ds(n, wide_ref.shape[0] // images, images), :].astype(BF)
        spread = dot(cells, spread_ref[...], ((0,), (0,)))[:part]
        turned = (spread * slope_ref[n].astype(F32)).astype(BF).astype(F32)
        moved = [turned] + [pltpu.roll(turned, j, 1) for j in (1, 2)]
        grad_ref[:, k * cols : (k + 1) * cols] = jnp.concatenate(moved, axis=0).astype(BF)
    for row in range(3):
        block = [ref[row * LINE : row * LINE + cols, :] for ref in lines_refs]
        term = dot(grad_ref[...], jnp.concatenate(block, axis=0), ((1,), (0,)))
        for col in range(3):
            tap = 3 * row + col
            flat_ref[tap * chans : (tap + 1) * chans, :] = term[col * part : (col + 1) * part].T
    count, size, _ = out_ref.shape
    for dest in range(count):
        at = dest * 2 * size
        both = [flat_ref[at : at + size, :], flat_ref[at + size : at + 2 * size, :]]
        out_ref[dest] = jnp.concatenate(both, axis=1).astype(BF)


def conv_kernel_grad(me, lines, slopes, dfeat, spread, count):
    chans = lines[0].shape[1]
    images, part, cols = slopes.shape
    size = 9 * chans // (2 * count)
    in_vmem = [pl.BlockSpec(memory_space=pltpu.VMEM)] * (3 + images)
    return pl.pallas_call(
        kernel_kernel,
        in_specs=[pl.BlockSpec(memory_space=pltpu.SMEM)] + in_vmem,
        out_shape=jax.ShapeDtypeStruct((count, size, 2 * part), BF),
        scratch_shapes=[
            pltpu.VMEM((3 * part, images * cols), BF),
            pltpu.VMEM((9 * chans, part), F32),
            pltpu.VMEM((dfeat.shape[0] * dfeat.shape[1], LANES), F32),
        ],
        compiler_params=VMEM,
        cost_estimate=cost(18 * images * cols * chans * part, images * lines[0].size * 2),
    )(me, slopes, dfeat, spread, *lines)


def backward_kernel(lines_ref, weight_ref, out_ref, sums_ref):
    step = pl.program_id(0)
    col = lax.rem(step, 3)
    rows = sums_ref.shape[1]
    start = pl.multiple_of((2 - step // 3) * LINE, LINE)
    part = dot(lines_ref[pl.ds(start, rows), :], weight_ref[...], ((1,), (1,)))

    @pl.when(step < 3)
    def _():
        sums_ref[col] = part

    @pl.when(step >= 3)
    def _():
        sums_ref[col] += part

    @pl.when(step == 8)
    def _():
        _, side, _, chans = out_ref.shape
        pix = side * LINE
        grad = sums_ref[0, 2 : pix + 2, :] + sums_ref[1, 1 : pix + 1, :] + sums_ref[2, 0:pix, :]
        out_ref[0] = grad.reshape(side, LINE, chans)[:, :side, :]


def conv_backward(lines, weight, side):
    chans = lines.shape[1]
    depth = weight.shape[0] // 9
    pix = side * LINE
    return pl.pallas_call(
        backward_kernel,
        grid=(9,),
        in_specs=[
            pl.BlockSpec(lines.shape, lambda t: (0, 0)),
            pl.BlockSpec((depth, chans), lambda t: (t, 0)),
        ],
        out_specs=pl.BlockSpec((1, side, side, depth), lambda t: (0, 0, 0, 0)),
        out_shape=jax.ShapeDtypeStruct((1, side, side, depth), F32),
        scratch_shapes=[pltpu.VMEM((3, pix + LINE, depth), F32)],
        compiler_params=VMEM,
        cost_estimate=cost(18 * pix * depth * chans, weight.size * 2),
    )(lines, weight)


def spread_matrix(me, nx, half, cols):
    at = lax.broadcasted_iota(jnp.int32, (nx * nx, cols), 0)
    pixel = lax.broadcasted_iota(jnp.int32, (nx * nx, cols), 1)
    source, run = at // nx, at % nx
    line, place = pixel // LINE, pixel % LINE
    per = half * half // nx
    cell = jnp.where((line < 2 * half) & (place < 2 * half), line // 2 * half + place // 2, -1)
    mine = per * source + run + (me < source).astype(jnp.int32)
    return ((cell == mine) & (run <= per)).astype(BF)


def swap(value, axis):
    return lax.all_to_all(value, axis, 0, 0, tiled=True)


def share(value, axis, count):
    return swap(jnp.broadcast_to(value, (count,) + value.shape), axis)


def bordered(maps):
    side, _, chans = maps.shape
    padded = jnp.pad(maps, ((1, 3), (1, LINE - side - 1), (0, 0)))
    return padded.reshape((side + 4) * LINE, chans)


def make(nx, nz, nc):
    ny = nz * nc
    near = nz // nx
    gy = ("gz", "core")
    pair = [(k, nc - 1 - k) for k in range(nc)]

    def on_device(images, conv_weight, fc6_weight, fc7_weight, cotangent):
        side, chans = images.shape[1], images.shape[3]
        half = side // 2
        feats, units = fc6_weight.shape
        rows7, cols7 = fc7_weight.shape
        total = cotangent.shape[0]
        group = total // nc
        mine = group // nx
        wide = units * nc
        part = chans // nx
        cols = 2 * LANES
        me, core = lax.axis_index("gx"), lax.axis_index("core")
        me_word = me.reshape(1).astype(jnp.int32)

        known = lax.all_gather(
            jnp.concatenate([fc7_weight.T, cotangent.T], axis=1), "gx", axis=0, tiled=False
        )
        other6 = lax.ppermute(fc6_weight, "core", pair)
        lines = bordered(images[0])
        all_lines = [lines]
        for _ in range(1, nx):
            all_lines.append(lax.ppermute(all_lines[-1], "gx", [(k, (k + 1) % nx) for k in range(nx)]))
        conv_pre, pooled = conv_forward(lines, conv_weight, side)
        slopes = turned_slope(conv_pre, cols).reshape(nx, part, cols)
        feat = pooled.reshape(half, half + 1, chans)[:, :half].reshape(nx, feats)
        inputs = share(swap(feat, "gx"), "gz", nz).reshape(group, feats)
        first = jnp.where(core == 0, fc6_weight, other6)
        second = jnp.where(core == 0, other6, fc6_weight)
        weight6 = jnp.concatenate([first, second], axis=1)
        inputs, weight6 = lax.optimization_barrier((inputs, weight6))

        h6_terms = dot(inputs, weight6, ((1,), (0,))).astype(BF).reshape(nx, mine, wide)
        both = swap(jnp.concatenate([h6_terms, slopes], axis=1), "gx")
        both, known = lax.optimization_barrier((both, known.reshape(nx * cols7, rows7 + total)))
        known_other = lax.ppermute(known, "core", pair)
        h6_pre = both[:, :mine].astype(F32).sum(axis=0)
        slopes = both[:, mine:]
        own_hidden = activate(h6_pre).astype(BF)
        hidden = share(own_hidden, "gz", nz)

        place = lax.broadcasted_iota(jnp.int32, (total, mine), 1)
        source = (place % nx) * ny + (me * near + place // nx) * nc + core
        pick = (lax.broadcasted_iota(jnp.int32, (total, mine), 0) == source).astype(BF)
        g_seven, dh6_terms = fc7_step(known, known_other, hidden, pick)
        hidden = hidden.transpose(1, 0, 2).reshape(mine, rows7)
        all_hidden = lax.all_gather(hidden, "gx", axis=0, tiled=False).reshape(group, rows7)
        grad_hidden = swap(dh6_terms, "gz").astype(F32).sum(axis=0)
        own_six = (grad_hidden * slope(h6_pre)).astype(BF)

        columns = g_seven.reshape(nx, cols7, nc * mine)
        columns = jnp.pad(columns, ((0, 0), (0, mine - cols7), (0, LANES - nc * mine)))
        both = jnp.concatenate([jnp.broadcast_to(own_six, (nx, mine, wide)), columns], axis=2)
        both = swap(both, "gx")
        g_six = both[:, :, :wide].reshape(group, wide)
        columns = both[:, :cols7, wide : wide + nc * mine]

        feat_terms = features_back(g_six, weight6).reshape(nz, nx, feats)
        feat_terms, g_six = lax.optimization_barrier((feat_terms, g_six))
        feat_terms = swap(feat_terms, "gz")
        feat_terms, all_hidden = lax.optimization_barrier((feat_terms, all_hidden))
        sent6 = weight_terms(nc - 1 - core, inputs, g_six, units)
        packs = pack_dfeat(me_word, feat_terms)
        packs = swap(packs, "gx")
        grad_fc6 = weight_terms(core, inputs, g_six, units, lax.ppermute(sent6, "core", pair))
        spread = spread_matrix(me, nx, half, cols)
        packed = conv_kernel_grad(me_word, all_lines, slopes, packs, spread, ny)
        packed = swap(packed, gy)

        runs = feats // part
        dfeat = packs[:, :runs, part : 2 * part].reshape(half, half, chans).astype(F32)
        dfeat = jnp.pad(dfeat, ((0, 0), (0, 1), (0, 0))).reshape(half * (half + 1), chans)
        g_lines = conv_slope(conv_pre, dfeat).reshape(side, LINE, chans)[:, :side]
        grad_images = conv_backward(bordered(g_lines), conv_weight, side)

        columns = columns.reshape(nx, cols7, nc, mine).transpose(2, 1, 0, 3).reshape(nc * cols7, group)
        terms7 = dot(columns, all_hidden, ((1,), (0,)))
        grad_fc7 = (terms7[:cols7] + lax.ppermute(terms7[cols7:], "core", pair)).T
        packed, grad_fc7 = lax.optimization_barrier((packed, grad_fc7))
        packed = packed.astype(F32).sum(axis=0)
        grad_conv = jnp.concatenate([packed[:, :part], packed[:, part:]], axis=0)
        return (grad_conv, grad_fc6, grad_fc7, grad_images)

    return on_device


def solution(mesh):
    nx, ny = mesh.shape["gx"], mesh.shape["gy"]
    nc = 2
    nz = ny // nc
    fine = Mesh(mesh.devices.reshape(nx, nz, nc), ("gx", "gz", "core"))
    gy = ("gz", "core")
    both = ("gx", "gz", "core")
    return jax.shard_map(
        make(nx, nz, nc),
        mesh=fine,
        in_specs=(P(both, None, None, None), P(), P("gx", gy), P(None, both), P(None, both)),
        out_specs=(P(gy, "gx"), P("gx", gy), P(None, both), P(both, None, None, None)),
        check_vma=False,
    )
```

```python
import jax
import jax.numpy as jnp
from jax import lax
from jax.experimental import pallas as pl
from jax.experimental.pallas import tpu as pltpu
from jax.sharding import Mesh, PartitionSpec as P

BF = jnp.bfloat16
F32 = jnp.float32
LANES = 128
LINE = 16
VMEM = pltpu.CompilerParams(vmem_limit_bytes=20 * 2**20)


def activate(value):
    return value * jax.nn.sigmoid(value)


def slope(value):
    sig = jax.nn.sigmoid(value)
    return sig * (1.0 + value * (1.0 - sig))


def dot(a, b, dims):
    return lax.dot_general(a, b, (dims, ((), ())), preferred_element_type=F32)


def cost(flops, moved, special=0):
    return pl.CostEstimate(flops=flops, bytes_accessed=moved, transcendentals=special)


def forward_kernel(image_ref, weight_ref, pre_ref, feat_ref, held_ref, sums_ref, pool_ref, sems):
    pix, chans = pre_ref.shape
    depth = image_ref.shape[1]
    rows = sums_ref.shape[1]

    def load(tap):
        return pltpu.make_async_copy(
            weight_ref.at[pl.ds(tap * depth, depth), :],
            held_ref.at[tap % 3, pl.ds(tap // 3 * depth, depth), :],
            sems.at[tap],
        )

    order = [3 * row + col for col in range(3) for row in range(3)]
    for tap in order:
        load(tap).start()
    image = jnp.concatenate([image_ref[k * LINE : k * LINE + rows, :] for k in range(3)], axis=1)
    for col in range(3):
        for row in range(3):
            load(3 * row + col).wait()
        sums_ref[col] = dot(image, held_ref[col], ((1,), (0,)))
    pre = sums_ref[0, 0:pix, :] + sums_ref[1, 1 : pix + 1, :] + sums_ref[2, 2 : pix + 2, :]
    pre_ref[...] = pre
    act = activate(pre).reshape(pix // (2 * LINE), 2, LINE, chans)
    lines = (act[:, 0] + act[:, 1]).reshape(pix // 2, chans)
    half = pix // 4
    for k in range(chans // LANES):
        pool_ref[k] = lines[:, k * LANES : (k + 1) * LANES]
        total = pool_ref[k, pl.ds(0, half, 2), :] + pool_ref[k, pl.ds(1, half, 2), :]
        feat_ref[:, k * LANES : (k + 1) * LANES] = (0.25 * total).astype(BF)


def conv_forward(lines, weight, side):
    depth, chans = lines.shape[1], weight.shape[1]
    pix = side * LINE
    return pl.pallas_call(
        forward_kernel,
        in_specs=[
            pl.BlockSpec(memory_space=pltpu.VMEM),
            pl.BlockSpec(memory_space=pl.ANY),
        ],
        out_shape=[
            jax.ShapeDtypeStruct((pix, chans), F32),
            jax.ShapeDtypeStruct((pix // 4, chans), BF),
        ],
        scratch_shapes=[
            pltpu.VMEM((3, 3 * depth, chans), BF),
            pltpu.VMEM((3, pix + LINE, chans), F32),
            pltpu.VMEM((chans // LANES, pix // 2, LANES), F32),
            pltpu.SemaphoreType.DMA((9,)),
        ],
        compiler_params=VMEM,
        cost_estimate=cost(18 * pix * depth * chans, weight.size * 2, pix * chans),
    )(lines, weight)


def turn_kernel(pre_ref, out_ref):
    pix, chans = pre_ref.shape
    grad = 0.25 * slope(pre_ref[...])
    grad = jnp.concatenate([grad, jnp.zeros((out_ref.shape[1] - pix, chans), F32)], axis=0)
    out_ref[...] = grad.T.astype(BF)


def turned_slope(pre, cols):
    pix, chans = pre.shape
    return pl.pallas_call(
        turn_kernel,
        out_shape=jax.ShapeDtypeStruct((chans, cols), BF),
        compiler_params=VMEM,
        cost_estimate=cost(8 * pix * chans, pix * chans * 6, pix * chans),
    )(pre)


def lines_kernel(pre_ref, dfeat_ref, out_ref, wide_ref):
    pix, chans = pre_ref.shape
    half = pix // 4
    for k in range(chans // LANES):
        dfeat = dfeat_ref[:, k * LANES : (k + 1) * LANES]
        wide_ref[k, pl.ds(0, half, 2), :] = dfeat
        wide_ref[k, pl.ds(1, half, 2), :] = dfeat
    spread = jnp.concatenate([wide_ref[k] for k in range(chans // LANES)], axis=1)
    spread = spread.reshape(pix // (2 * LINE), 1, LINE, chans)
    spread = jnp.broadcast_to(spread, (pix // (2 * LINE), 2, LINE, chans)).reshape(pix, chans)
    out_ref[...] = (0.25 * spread * slope(pre_ref[...])).astype(BF)


def conv_slope(pre, dfeat):
    pix, chans = pre.shape
    return pl.pallas_call(
        lines_kernel,
        out_shape=jax.ShapeDtypeStruct((pix, chans), BF),
        scratch_shapes=[pltpu.VMEM((chans // LANES, pix // 2, LANES), F32)],
        compiler_params=VMEM,
        cost_estimate=cost(8 * pix * chans, pix * chans * 6, pix * chans),
    )(pre, dfeat)


def fc7_kernel(known_ref, hidden_ref, pick_ref, seven_ref, terms_ref):
    count, mine, wide = hidden_ref.shape
    lines, both, _ = known_ref.shape
    rows7, cols7 = count * wide, both // 2

    def weight(k, start, size):
        block = known_ref[:, k * cols7 : (k + 1) * cols7, start : start + size]
        return block.reshape(lines * cols7, size)

    sevens = []
    for k in range(2):
        y7_pre = jnp.zeros((lines * cols7, mine), F32)
        for g in range(count):
            y7_pre += dot(weight(k, g * wide, wide), hidden_ref[g], ((1,), (1,)))
        cot = dot(weight(k, rows7, pick_ref.shape[0]), pick_ref[...], ((1,), (0,)))
        sevens.append((cot * slope(y7_pre)).astype(BF))
        seven_ref[:, k * mine : (k + 1) * mine] = sevens[k]
    for g in range(count):
        parts = [dot(sevens[k], weight(k, g * wide, wide), ((0,), (0,))) for k in range(2)]
        terms_ref[g] = (parts[0] + parts[1]).astype(BF)


def fc7_step(known, hidden, pick):
    lines, both, _ = known.shape
    return pl.pallas_call(
        fc7_kernel,
        out_shape=[
            jax.ShapeDtypeStruct((lines * both // 2, 2 * pick.shape[1]), BF),
            jax.ShapeDtypeStruct(hidden.shape, BF),
        ],
        compiler_params=VMEM,
        cost_estimate=cost(4 * known.size * pick.shape[1], known.size * 2),
    )(known, hidden, pick)


def back_kernel(g_ref, weight_ref, out_ref):
    out_ref[...] = dot(g_ref[...], weight_ref[...], ((1,), (1,))).astype(BF)


def features_back(g_six, weight):
    count, feats = g_six.shape[0], weight.shape[0]
    return pl.pallas_call(
        back_kernel,
        out_shape=jax.ShapeDtypeStruct((count, feats), BF),
        compiler_params=VMEM,
        cost_estimate=cost(2 * count * weight.size, weight.size * 2),
    )(g_six, weight)


def outer_kernel(which_ref, inputs_ref, g_ref, out_ref):
    units = out_ref.shape[1]
    g_six = g_ref[:, pl.ds(pl.multiple_of(which_ref[0] * units, units), units)]
    out_ref[...] = dot(inputs_ref[...], g_six, ((0,), (0,))).astype(out_ref.dtype)


def outer_add_kernel(which_ref, inputs_ref, g_ref, more_ref, out_ref):
    units = out_ref.shape[1]
    g_six = g_ref[:, pl.ds(pl.multiple_of(which_ref[0] * units, units), units)]
    out_ref[...] = dot(inputs_ref[...], g_six, ((0,), (0,))) + more_ref[...].astype(F32)


def weight_terms(which, inputs, g_six, units, more=None):
    feats = inputs.shape[1]
    operands = (inputs, g_six) if more is None else (inputs, g_six, more)
    in_vmem = [pl.BlockSpec(memory_space=pltpu.VMEM)] * len(operands)
    return pl.pallas_call(
        outer_kernel if more is None else outer_add_kernel,
        in_specs=[pl.BlockSpec(memory_space=pltpu.SMEM)] + in_vmem,
        out_shape=jax.ShapeDtypeStruct((feats, units), BF if more is None else F32),
        compiler_params=VMEM,
        cost_estimate=cost(2 * inputs.size * units, 4 * feats * units),
    )(which.reshape(1).astype(jnp.int32), *operands)


def pack_kernel(me_ref, terms_ref, out_ref, parts_ref, own_ref):
    nx, rows, _ = out_ref.shape
    feats = terms_ref.shape[2]
    run = LANES // 2
    runs = feats // run
    total = terms_ref[...].astype(F32).sum(axis=0).astype(BF).astype(F32)
    total = jnp.concatenate([total, jnp.zeros((nx, -feats % LANES), F32)], axis=1)
    parts_ref[...] = jnp.zeros(parts_ref.shape, F32)
    own_ref[...] = jnp.zeros(own_ref.shape, F32)
    for t in range(runs):
        tile = total[:, t // 2 * LANES : (t // 2 + 1) * LANES]
        other = pltpu.roll(tile, run, 1)
        low, high = (tile, other) if t % 2 == 0 else (other, tile)
        parts_ref[t % nx, t // nx * nx : (t // nx + 1) * nx, :] = low
        own_ref[pl.ds(t, nx, rows), :] = high
    lane = lax.broadcasted_iota(jnp.int32, (rows, LANES), 1)
    for e in range(nx):
        dest = lax.rem(me_ref[0] + e, nx)
        own = own_ref[pl.ds(pl.multiple_of(dest * rows, rows), rows), :]
        out_ref[dest] = jnp.where(lane < run, parts_ref[e], own).astype(BF)


def pack_dfeat(me, terms):
    _, nx, feats = terms.shape
    rows = nx * nx
    return pl.pallas_call(
        pack_kernel,
        in_specs=[
            pl.BlockSpec(memory_space=pltpu.SMEM),
            pl.BlockSpec(memory_space=pltpu.VMEM),
        ],
        out_shape=jax.ShapeDtypeStruct((nx, rows, LANES), BF),
        scratch_shapes=[
            pltpu.VMEM((nx, rows, LANES), F32),
            pltpu.VMEM((nx * rows, LANES), F32),
        ],
        compiler_params=VMEM,
        cost_estimate=cost(4 * terms.size, terms.size * 2),
    )(me, terms)


def kernel_kernel(lines_ref, slope_ref, dfeat_ref, spread_ref, out_ref, grad_ref, flat_ref, wide_ref):
    images, part, cols = slope_ref.shape
    chans = lines_ref.shape[2]
    wide_ref[...] = dfeat_ref[...].astype(F32).reshape(wide_ref.shape)
    for n in range(images):
        cells = wide_ref[pl.ds(n, wide_ref.shape[0] // images, images), :].astype(BF)
        spread = dot(cells, spread_ref[...], ((0,), (0,)))[:part]
        turned = (spread * slope_ref[n].astype(F32)).astype(BF).astype(F32)
        moved = [turned] + [pltpu.roll(turned, k, 1) for k in (1, 2)]
        grad_ref[:, n * cols : (n + 1) * cols] = jnp.concatenate(moved, axis=0).astype(BF)
    for row in range(3):
        block = lines_ref[:, row * LINE : row * LINE + cols, :].reshape(images * cols, chans)
        term = dot(grad_ref[...], block, ((1,), (0,)))
        for col in range(3):
            tap = 3 * row + col
            flat_ref[tap * chans : (tap + 1) * chans, :] = term[col * part : (col + 1) * part].T
    count, size, _ = out_ref.shape
    for dest in range(count):
        at = dest * 2 * size
        both = [flat_ref[at : at + size, :], flat_ref[at + size : at + 2 * size, :]]
        out_ref[dest] = jnp.concatenate(both, axis=1).astype(BF)


def conv_kernel_grad(lines, slopes, dfeat, spread, count):
    images, rows, chans = lines.shape
    _, part, cols = slopes.shape
    size = 9 * chans // (2 * count)
    return pl.pallas_call(
        kernel_kernel,
        out_shape=jax.ShapeDtypeStruct((count, size, 2 * part), BF),
        scratch_shapes=[
            pltpu.VMEM((3 * part, images * cols), BF),
            pltpu.VMEM((9 * chans, part), F32),
            pltpu.VMEM((dfeat.shape[0] * dfeat.shape[1], LANES), F32),
        ],
        compiler_params=VMEM,
        cost_estimate=cost(18 * images * cols * chans * part, lines.size * 2),
    )(lines, slopes, dfeat, spread)


def backward_kernel(lines_ref, weight_ref, out_ref, sums_ref):
    step = pl.program_id(0)
    col = lax.rem(step, 3)
    rows = sums_ref.shape[1]
    start = pl.multiple_of((2 - step // 3) * LINE, LINE)
    part = dot(lines_ref[pl.ds(start, rows), :], weight_ref[...], ((1,), (1,)))

    @pl.when(step < 3)
    def _():
        sums_ref[col] = part

    @pl.when(step >= 3)
    def _():
        sums_ref[col] += part

    @pl.when(step == 8)
    def _():
        _, side, _, chans = out_ref.shape
        pix = side * LINE
        grad = sums_ref[0, 2 : pix + 2, :] + sums_ref[1, 1 : pix + 1, :] + sums_ref[2, 0:pix, :]
        out_ref[0] = grad.reshape(side, LINE, chans)[:, :side, :]


def conv_backward(lines, weight, side):
    chans = lines.shape[1]
    depth = weight.shape[0] // 9
    pix = side * LINE
    return pl.pallas_call(
        backward_kernel,
        grid=(9,),
        in_specs=[
            pl.BlockSpec(lines.shape, lambda t: (0, 0)),
            pl.BlockSpec((depth, chans), lambda t: (t, 0)),
        ],
        out_specs=pl.BlockSpec((1, side, side, depth), lambda t: (0, 0, 0, 0)),
        out_shape=jax.ShapeDtypeStruct((1, side, side, depth), F32),
        scratch_shapes=[pltpu.VMEM((3, pix + LINE, depth), F32)],
        compiler_params=VMEM,
        cost_estimate=cost(18 * pix * depth * chans, weight.size * 2),
    )(lines, weight)


def spread_matrix(me, nx, half, cols):
    at = lax.broadcasted_iota(jnp.int32, (nx * nx, cols), 0)
    pixel = lax.broadcasted_iota(jnp.int32, (nx * nx, cols), 1)
    source, run = at // nx, at % nx
    line, place = pixel // LINE, pixel % LINE
    per = half * half // nx
    cell = jnp.where((line < 2 * half) & (place < 2 * half), line // 2 * half + place // 2, -1)
    mine = per * source + run + (me < source).astype(jnp.int32)
    return ((cell == mine) & (run <= per)).astype(BF)


def swap(value, axis):
    return lax.all_to_all(value, axis, 0, 0, tiled=True)


def share(value, axis, count):
    return swap(jnp.broadcast_to(value, (count,) + value.shape), axis)


def bordered(maps):
    side, _, chans = maps.shape
    padded = jnp.pad(maps, ((1, 3), (1, LINE - side - 1), (0, 0)))
    return padded.reshape((side + 4) * LINE, chans)


def make(nx, nz, nc):
    ny = nz * nc
    near = nz // nx
    gy = ("gz", "core")
    rise = [(k, (k + 1) % nx) for k in range(nx)]
    fall = [(k, (k - 1) % nx) for k in range(nx)]
    pair = [(k, nc - 1 - k) for k in range(nc)]

    def on_device(images, conv_weight, fc6_weight, fc7_weight, cotangent):
        side, chans = images.shape[1], images.shape[3]
        half = side // 2
        feats, units = fc6_weight.shape
        rows7, cols7 = fc7_weight.shape
        total = cotangent.shape[0]
        group = total // nc
        mine = group // nx
        wide = units * nc
        part = chans // nx
        cols = 2 * LANES
        me, core = lax.axis_index("gx"), lax.axis_index("core")
        me_word = me.reshape(1).astype(jnp.int32)

        known = jnp.concatenate([fc7_weight.T, cotangent.T], axis=1)
        known = jnp.concatenate([known, lax.ppermute(known, "core", pair)], axis=0)
        known = lax.all_gather(known, "gx", axis=0, tiled=False)
        gathered = lax.all_gather(images[0], "gx", axis=0, tiled=False)
        other6 = lax.ppermute(fc6_weight, "core", pair)
        lines = bordered(images[0])
        conv_pre, pooled = conv_forward(lines, conv_weight, side)
        slopes = turned_slope(conv_pre, cols).reshape(nx, part, cols)
        feat = pooled.reshape(half, half + 1, chans)[:, :half].reshape(nx, feats)
        inputs = share(swap(feat, "gx"), "gz", nz).reshape(group, feats)
        first = jnp.where(core == 0, fc6_weight, other6)
        second = jnp.where(core == 0, other6, fc6_weight)
        weight6 = jnp.concatenate([first, second], axis=1)
        inputs, weight6 = lax.optimization_barrier((inputs, weight6))

        h6_terms = dot(inputs, weight6, ((1,), (0,))).astype(BF).reshape(nx, mine, wide)
        both = swap(jnp.concatenate([h6_terms, slopes], axis=1), "gx")
        h6_pre = both[:, :mine].astype(F32).sum(axis=0)
        slopes = both[:, mine:]
        own_hidden = activate(h6_pre).astype(BF)
        hidden = share(own_hidden, "gz", nz)

        place = lax.broadcasted_iota(jnp.int32, (total, mine), 1)
        source = (place % nx) * ny + (me * near + place // nx) * nc + core
        pick = (lax.broadcasted_iota(jnp.int32, (total, mine), 0) == source).astype(BF)
        g_seven, dh6_terms = fc7_step(known, hidden, pick)
        hidden = hidden.transpose(1, 0, 2).reshape(mine, rows7)
        up = [hidden, lax.ppermute(hidden, "gx", rise)]
        down = [hidden, lax.ppermute(hidden, "gx", fall)]
        dh6_terms = swap(dh6_terms, "gz")
        dh6_terms, up[1], down[1] = lax.optimization_barrier((dh6_terms, up[1], down[1]))
        grad_hidden = dh6_terms.astype(F32).sum(axis=0)
        own_six = (grad_hidden * slope(h6_pre)).astype(BF)

        columns = g_seven.reshape(nx, cols7, nc * mine)
        columns = jnp.pad(columns, ((0, 0), (0, mine - cols7), (0, LANES - nc * mine)))
        both = jnp.concatenate([jnp.broadcast_to(own_six, (nx, mine, wide)), columns], axis=2)
        both = swap(both, "gx")
        up.append(lax.ppermute(up[1], "gx", rise))
        down.append(lax.ppermute(down[1], "gx", fall))
        both, up[2], down[2] = lax.optimization_barrier((both, up[2], down[2]))
        g_six = both[:, :, :wide].reshape(group, wide)
        columns = both[:, :cols7, wide : wide + nc * mine]

        feat_terms = features_back(g_six, weight6).reshape(nz, nx, feats)
        feat_terms, g_six = lax.optimization_barrier((feat_terms, g_six))
        feat_terms = swap(feat_terms, "gz")
        up.append(lax.ppermute(up[2], "gx", rise))
        down.append(lax.ppermute(down[2], "gx", fall))
        up.append(lax.ppermute(up[3], "gx", rise))
        feat_terms, up[3], down[3] = lax.optimization_barrier((feat_terms, up[3], down[3]))
        sent6 = weight_terms(nc - 1 - core, inputs, g_six, units)
        packs = pack_dfeat(me_word, feat_terms)
        packs = swap(packs, "gx")
        gathered, sent6 = lax.optimization_barrier((gathered, sent6))
        all_lines = jax.vmap(bordered)(gathered)
        grad_fc6 = weight_terms(core, inputs, g_six, units, lax.ppermute(sent6, "core", pair))
        spread = spread_matrix(me, nx, half, cols)
        packed = conv_kernel_grad(all_lines, slopes, packs, spread, ny)
        packed = swap(packed, gy)

        runs = feats // part
        dfeat = packs[:, :runs, part : 2 * part].reshape(half, half, chans).astype(F32)
        dfeat = jnp.pad(dfeat, ((0, 0), (0, 1), (0, 0))).reshape(half * (half + 1), chans)
        g_lines = conv_slope(conv_pre, dfeat).reshape(side, LINE, chans)[:, :side]
        grad_images = conv_backward(bordered(g_lines), conv_weight, side)

        all_hidden = jnp.concatenate([down[k] for k in range(nx // 2)] + up[nx // 2 : 0 : -1], axis=0)
        columns = lax.dynamic_slice_in_dim(jnp.concatenate([columns, columns]), me, nx)
        columns = columns.reshape(nx, cols7, nc, mine).transpose(2, 1, 0, 3).reshape(nc * cols7, group)
        terms7 = dot(columns, all_hidden, ((1,), (0,)))
        grad_fc7 = (terms7[:cols7] + lax.ppermute(terms7[cols7:], "core", pair)).T
        packed, grad_fc7 = lax.optimization_barrier((packed, grad_fc7))
        packed = packed.astype(F32).sum(axis=0)
        grad_conv = jnp.concatenate([packed[:, :part], packed[:, part:]], axis=0)
        return (grad_conv, grad_fc6, grad_fc7, grad_images)

    return on_device


def solution(mesh):
    nx, ny = mesh.shape["gx"], mesh.shape["gy"]
    nc = 2
    nz = ny // nc
    fine = Mesh(mesh.devices.reshape(nx, nz, nc), ("gx", "gz", "core"))
    gy = ("gz", "core")
    both = ("gx", "gz", "core")
    return jax.shard_map(
        make(nx, nz, nc),
        mesh=fine,
        in_specs=(P(both, None, None, None), P(), P("gx", gy), P(None, both), P(None, both)),
        out_specs=(P(gy, "gx"), P("gx", gy), P(None, both), P(both, None, None, None)),
        check_vma=False,
    )
```

```python
import jax
import jax.numpy as jnp
from jax import lax
from jax.experimental import pallas as pl
from jax.experimental.pallas import tpu as pltpu
from jax.sharding import Mesh, PartitionSpec as P

BF = jnp.bfloat16
F32 = jnp.float32
LANES = 128
LINE = 16
VMEM = pltpu.CompilerParams(vmem_limit_bytes=20 * 2**20)


def activate(value):
    return value * jax.nn.sigmoid(value)


def slope(value):
    sig = jax.nn.sigmoid(value)
    return sig * (1.0 + value * (1.0 - sig))


def dot(a, b, dims):
    return lax.dot_general(a, b, (dims, ((), ())), preferred_element_type=F32)


def cost(flops, moved, special=0):
    return pl.CostEstimate(flops=flops, bytes_accessed=moved, transcendentals=special)


def forward_kernel(image_ref, weight_ref, pre_ref, feat_ref, held_ref, sums_ref, pool_ref, sems):
    pix, chans = pre_ref.shape
    depth = image_ref.shape[1]
    rows = sums_ref.shape[1]

    def load(tap):
        return pltpu.make_async_copy(
            weight_ref.at[pl.ds(tap * depth, depth), :],
            held_ref.at[tap % 3, pl.ds(tap // 3 * depth, depth), :],
            sems.at[tap],
        )

    order = [3 * row + col for col in range(3) for row in range(3)]
    for tap in order:
        load(tap).start()
    image = jnp.concatenate([image_ref[k * LINE : k * LINE + rows, :] for k in range(3)], axis=1)
    for col in range(3):
        for row in range(3):
            load(3 * row + col).wait()
        sums_ref[col] = dot(image, held_ref[col], ((1,), (0,)))
    pre = sums_ref[0, 0:pix, :] + sums_ref[1, 1 : pix + 1, :] + sums_ref[2, 2 : pix + 2, :]
    pre_ref[...] = pre
    act = activate(pre).reshape(pix // (2 * LINE), 2, LINE, chans)
    lines = (act[:, 0] + act[:, 1]).reshape(pix // 2, chans)
    half = pix // 4
    for k in range(chans // LANES):
        pool_ref[k] = lines[:, k * LANES : (k + 1) * LANES]
        total = pool_ref[k, pl.ds(0, half, 2), :] + pool_ref[k, pl.ds(1, half, 2), :]
        feat_ref[:, k * LANES : (k + 1) * LANES] = (0.25 * total).astype(BF)


def conv_forward(lines, weight, side):
    depth, chans = lines.shape[1], weight.shape[1]
    pix = side * LINE
    return pl.pallas_call(
        forward_kernel,
        in_specs=[
            pl.BlockSpec(memory_space=pltpu.VMEM),
            pl.BlockSpec(memory_space=pl.ANY),
        ],
        out_shape=[
            jax.ShapeDtypeStruct((pix, chans), F32),
            jax.ShapeDtypeStruct((pix // 4, chans), BF),
        ],
        scratch_shapes=[
            pltpu.VMEM((3, 3 * depth, chans), BF),
            pltpu.VMEM((3, pix + LINE, chans), F32),
            pltpu.VMEM((chans // LANES, pix // 2, LANES), F32),
            pltpu.SemaphoreType.DMA((9,)),
        ],
        compiler_params=VMEM,
        cost_estimate=cost(18 * pix * depth * chans, weight.size * 2, pix * chans),
    )(lines, weight)


def turn_kernel(pre_ref, out_ref):
    pix, chans = pre_ref.shape
    grad = 0.25 * slope(pre_ref[...])
    grad = jnp.concatenate([grad, jnp.zeros((out_ref.shape[1] - pix, chans), F32)], axis=0)
    out_ref[...] = grad.T.astype(BF)


def turned_slope(pre, cols):
    pix, chans = pre.shape
    return pl.pallas_call(
        turn_kernel,
        out_shape=jax.ShapeDtypeStruct((chans, cols), BF),
        compiler_params=VMEM,
        cost_estimate=cost(8 * pix * chans, pix * chans * 6, pix * chans),
    )(pre)


def lines_kernel(pre_ref, dfeat_ref, out_ref, wide_ref):
    pix, chans = pre_ref.shape
    half = pix // 4
    for k in range(chans // LANES):
        dfeat = dfeat_ref[:, k * LANES : (k + 1) * LANES]
        wide_ref[k, pl.ds(0, half, 2), :] = dfeat
        wide_ref[k, pl.ds(1, half, 2), :] = dfeat
    spread = jnp.concatenate([wide_ref[k] for k in range(chans // LANES)], axis=1)
    spread = spread.reshape(pix // (2 * LINE), 1, LINE, chans)
    spread = jnp.broadcast_to(spread, (pix // (2 * LINE), 2, LINE, chans)).reshape(pix, chans)
    out_ref[...] = (0.25 * spread * slope(pre_ref[...])).astype(BF)


def conv_slope(pre, dfeat):
    pix, chans = pre.shape
    return pl.pallas_call(
        lines_kernel,
        out_shape=jax.ShapeDtypeStruct((pix, chans), BF),
        scratch_shapes=[pltpu.VMEM((chans // LANES, pix // 2, LANES), F32)],
        compiler_params=VMEM,
        cost_estimate=cost(8 * pix * chans, pix * chans * 6, pix * chans),
    )(pre, dfeat)


def fc7_kernel(known_ref, hidden_ref, pick_ref, seven_ref, terms_ref):
    count, mine, wide = hidden_ref.shape
    lines, both, _ = known_ref.shape
    rows7, cols7 = count * wide, both // 2

    def weight(k, start, size):
        block = known_ref[:, k * cols7 : (k + 1) * cols7, start : start + size]
        return block.reshape(lines * cols7, size)

    sevens = []
    for k in range(2):
        y7_pre = jnp.zeros((lines * cols7, mine), F32)
        for g in range(count):
            y7_pre += dot(weight(k, g * wide, wide), hidden_ref[g], ((1,), (1,)))
        cot = dot(weight(k, rows7, pick_ref.shape[0]), pick_ref[...], ((1,), (0,)))
        sevens.append((cot * slope(y7_pre)).astype(BF))
        seven_ref[:, k * mine : (k + 1) * mine] = sevens[k]
    for g in range(count):
        parts = [dot(sevens[k], weight(k, g * wide, wide), ((0,), (0,))) for k in range(2)]
        terms_ref[g] = (parts[0] + parts[1]).astype(BF)


def fc7_step(known, hidden, pick):
    lines, both, _ = known.shape
    return pl.pallas_call(
        fc7_kernel,
        out_shape=[
            jax.ShapeDtypeStruct((lines * both // 2, 2 * pick.shape[1]), BF),
            jax.ShapeDtypeStruct(hidden.shape, BF),
        ],
        compiler_params=VMEM,
        cost_estimate=cost(4 * known.size * pick.shape[1], known.size * 2),
    )(known, hidden, pick)


def back_kernel(g_ref, weight_ref, out_ref):
    out_ref[...] = dot(g_ref[...], weight_ref[...], ((1,), (1,))).astype(BF)


def features_back(g_six, weight):
    count, feats = g_six.shape[0], weight.shape[0]
    return pl.pallas_call(
        back_kernel,
        out_shape=jax.ShapeDtypeStruct((count, feats), BF),
        compiler_params=VMEM,
        cost_estimate=cost(2 * count * weight.size, weight.size * 2),
    )(g_six, weight)


def outer_kernel(which_ref, inputs_ref, g_ref, out_ref):
    units = out_ref.shape[1]
    g_six = g_ref[:, pl.ds(pl.multiple_of(which_ref[0] * units, units), units)]
    out_ref[...] = dot(inputs_ref[...], g_six, ((0,), (0,))).astype(out_ref.dtype)


def outer_add_kernel(which_ref, inputs_ref, g_ref, more_ref, out_ref):
    units = out_ref.shape[1]
    g_six = g_ref[:, pl.ds(pl.multiple_of(which_ref[0] * units, units), units)]
    out_ref[...] = dot(inputs_ref[...], g_six, ((0,), (0,))) + more_ref[...].astype(F32)


def weight_terms(which, inputs, g_six, units, more=None):
    feats = inputs.shape[1]
    operands = (inputs, g_six) if more is None else (inputs, g_six, more)
    in_vmem = [pl.BlockSpec(memory_space=pltpu.VMEM)] * len(operands)
    return pl.pallas_call(
        outer_kernel if more is None else outer_add_kernel,
        in_specs=[pl.BlockSpec(memory_space=pltpu.SMEM)] + in_vmem,
        out_shape=jax.ShapeDtypeStruct((feats, units), BF if more is None else F32),
        compiler_params=VMEM,
        cost_estimate=cost(2 * inputs.size * units, 4 * feats * units),
    )(which.reshape(1).astype(jnp.int32), *operands)


def pack_kernel(me_ref, terms_ref, slope_ref, out_ref, parts_ref, own_ref):
    nx, rows, _ = out_ref.shape
    feats = terms_ref.shape[2]
    run = LANES // 2
    runs = feats // run
    total = terms_ref[...].astype(F32).sum(axis=0).astype(BF).astype(F32)
    total = jnp.concatenate([total, jnp.zeros((nx, -feats % LANES), F32)], axis=1)
    parts_ref[...] = jnp.zeros(parts_ref.shape, F32)
    own_ref[...] = jnp.zeros(own_ref.shape, F32)
    for t in range(runs):
        tile = total[:, t // 2 * LANES : (t // 2 + 1) * LANES]
        other = pltpu.roll(tile, run, 1)
        low, high = (tile, other) if t % 2 == 0 else (other, tile)
        parts_ref[t % nx, t // nx * nx : (t // nx + 1) * nx, :] = low
        own_ref[pl.ds(t, nx, rows), :] = high
    lane = lax.broadcasted_iota(jnp.int32, (rows, LANES), 1)
    for e in range(nx):
        dest = lax.rem(me_ref[0] + e, nx)
        own = own_ref[pl.ds(pl.multiple_of(dest * rows, rows), rows), :]
        out_ref[dest, :, :LANES] = jnp.where(lane < run, parts_ref[e], own).astype(BF)
    out_ref[:, :, LANES:] = slope_ref[...]


def pack_dfeat(me, terms, slopes):
    _, nx, feats = terms.shape
    rows = nx * nx
    return pl.pallas_call(
        pack_kernel,
        in_specs=[
            pl.BlockSpec(memory_space=pltpu.SMEM),
            pl.BlockSpec(memory_space=pltpu.VMEM),
            pl.BlockSpec(memory_space=pltpu.VMEM),
        ],
        out_shape=jax.ShapeDtypeStruct((nx, rows, LANES + slopes.shape[2]), BF),
        scratch_shapes=[
            pltpu.VMEM((nx, rows, LANES), F32),
            pltpu.VMEM((nx * rows, LANES), F32),
        ],
        compiler_params=VMEM,
        cost_estimate=cost(4 * terms.size, terms.size * 2),
    )(me, terms, slopes)


def kernel_kernel(high_ref, lines_ref, packs_ref, spread_ref, out_ref, grad_ref, flat_ref, wide_ref):
    images, part, _ = packs_ref.shape
    cols = spread_ref.shape[1]
    chans = lines_ref.shape[2]
    wide_ref[...] = packs_ref[:, :, :LANES].astype(F32).reshape(wide_ref.shape)
    for k in range(images):
        n = lax.rem(high_ref[0] + k % 2, 2) * (images // 2) + k // 2
        cells = wide_ref[pl.ds(n, wide_ref.shape[0] // images, images), :].astype(BF)
        spread = dot(cells, spread_ref[...], ((0,), (0,)))[:part]
        turned = (spread * packs_ref[n, :, LANES:].astype(F32)).astype(BF).astype(F32)
        moved = [turned] + [pltpu.roll(turned, j, 1) for j in (1, 2)]
        grad_ref[:, k * cols : (k + 1) * cols] = jnp.concatenate(moved, axis=0).astype(BF)
    for row in range(3):
        block = lines_ref[:, row * LINE : row * LINE + cols, :].reshape(images * cols, chans)
        term = dot(grad_ref[...], block, ((1,), (0,)))
        for col in range(3):
            tap = 3 * row + col
            flat_ref[tap * chans : (tap + 1) * chans, :] = term[col * part : (col + 1) * part].T
    count, size, _ = out_ref.shape
    for dest in range(count):
        at = dest * 2 * size
        both = [flat_ref[at : at + size, :], flat_ref[at + size : at + 2 * size, :]]
        out_ref[dest] = jnp.concatenate(both, axis=1).astype(BF)


def conv_kernel_grad(high, lines, packs, spread, count):
    images, _, chans = lines.shape
    _, part, _ = packs.shape
    cols = spread.shape[1]
    size = 9 * chans // (2 * count)
    return pl.pallas_call(
        kernel_kernel,
        in_specs=[pl.BlockSpec(memory_space=pltpu.SMEM)] + [pl.BlockSpec(memory_space=pltpu.VMEM)] * 3,
        out_shape=jax.ShapeDtypeStruct((count, size, 2 * part), BF),
        scratch_shapes=[
            pltpu.VMEM((3 * part, images * cols), BF),
            pltpu.VMEM((9 * chans, part), F32),
            pltpu.VMEM((images * part, LANES), F32),
        ],
        compiler_params=VMEM,
        cost_estimate=cost(18 * images * cols * chans * part, lines.size * 2),
    )(high, lines, packs, spread)


def backward_kernel(lines_ref, weight_ref, out_ref, sums_ref):
    step = pl.program_id(0)
    col = lax.rem(step, 3)
    rows = sums_ref.shape[1]
    start = pl.multiple_of((2 - step // 3) * LINE, LINE)
    part = dot(lines_ref[pl.ds(start, rows), :], weight_ref[...], ((1,), (1,)))

    @pl.when(step < 3)
    def _():
        sums_ref[col] = part

    @pl.when(step >= 3)
    def _():
        sums_ref[col] += part

    @pl.when(step == 8)
    def _():
        _, side, _, chans = out_ref.shape
        pix = side * LINE
        grad = sums_ref[0, 2 : pix + 2, :] + sums_ref[1, 1 : pix + 1, :] + sums_ref[2, 0:pix, :]
        out_ref[0] = grad.reshape(side, LINE, chans)[:, :side, :]


def conv_backward(lines, weight, side):
    chans = lines.shape[1]
    depth = weight.shape[0] // 9
    pix = side * LINE
    return pl.pallas_call(
        backward_kernel,
        grid=(9,),
        in_specs=[
            pl.BlockSpec(lines.shape, lambda t: (0, 0)),
            pl.BlockSpec((depth, chans), lambda t: (t, 0)),
        ],
        out_specs=pl.BlockSpec((1, side, side, depth), lambda t: (0, 0, 0, 0)),
        out_shape=jax.ShapeDtypeStruct((1, side, side, depth), F32),
        scratch_shapes=[pltpu.VMEM((3, pix + LINE, depth), F32)],
        compiler_params=VMEM,
        cost_estimate=cost(18 * pix * depth * chans, weight.size * 2),
    )(lines, weight)


def spread_matrix(me, nx, half, cols):
    at = lax.broadcasted_iota(jnp.int32, (nx * nx, cols), 0)
    pixel = lax.broadcasted_iota(jnp.int32, (nx * nx, cols), 1)
    source, run = at // nx, at % nx
    line, place = pixel // LINE, pixel % LINE
    per = half * half // nx
    cell = jnp.where((line < 2 * half) & (place < 2 * half), line // 2 * half + place // 2, -1)
    mine = per * source + run + (me < source).astype(jnp.int32)
    return ((cell == mine) & (run <= per)).astype(BF)


def swap(value, axis):
    return lax.all_to_all(value, axis, 0, 0, tiled=True)


def share(value, axis, count):
    return swap(jnp.broadcast_to(value, (count,) + value.shape), axis)


def bordered(maps):
    side, _, chans = maps.shape
    padded = jnp.pad(maps, ((1, 3), (1, LINE - side - 1), (0, 0)))
    return padded.reshape((side + 4) * LINE, chans)


def make(nh, nv, nz, nc):
    nx, ny = nh * nv, nz * nc
    gx = ("xh", "y")
    near = nz // nx
    gy = ("gz", "core")
    across = [(k, nh - 1 - k) for k in range(nh)]

    def paired(value, axis, way):
        return jnp.concatenate([value, lax.ppermute(value, axis, way)], axis=0)
    pair = [(k, nc - 1 - k) for k in range(nc)]

    def on_device(images, conv_weight, fc6_weight, fc7_weight, cotangent):
        side, chans = images.shape[1], images.shape[3]
        half = side // 2
        feats, units = fc6_weight.shape
        rows7, cols7 = fc7_weight.shape
        total = cotangent.shape[0]
        group = total // nc
        mine = group // nx
        wide = units * nc
        part = chans // nx
        cols = 2 * LANES
        high, core = lax.axis_index("xh"), lax.axis_index("core")
        me = high * nv + lax.axis_index("y")
        me_word = me.reshape(1).astype(jnp.int32)

        known = jnp.concatenate([fc7_weight.T, cotangent.T], axis=1)
        known = lax.all_gather(known, gx + ("core",), axis=0, tiled=False)
        known = known.reshape(nx, nc * cols7, rows7 + total)
        gathered = lax.all_gather(paired(images, "xh", across), "y", axis=0, tiled=True)
        other6 = lax.ppermute(fc6_weight, "core", pair)
        lines = bordered(images[0])
        conv_pre, pooled = conv_forward(lines, conv_weight, side)
        slopes = turned_slope(conv_pre, cols).reshape(nx, part, cols)
        feat = pooled.reshape(half, half + 1, chans)[:, :half].reshape(nx, feats)
        inputs = share(swap(feat, gx), "gz", nz).reshape(group, feats)
        first = jnp.where(core == 0, fc6_weight, other6)
        second = jnp.where(core == 0, other6, fc6_weight)
        weight6 = jnp.concatenate([first, second], axis=1)
        inputs, weight6 = lax.optimization_barrier((inputs, weight6))

        h6_terms = dot(inputs, weight6, ((1,), (0,))).astype(BF).reshape(nx, mine, wide)
        h6_pre = swap(h6_terms, gx).astype(F32).sum(axis=0)
        own_hidden = activate(h6_pre).astype(BF)
        hidden = share(own_hidden, "gz", nz)

        place = lax.broadcasted_iota(jnp.int32, (total, mine), 1)
        source = (place % nx) * ny + (me * near + place // nx) * nc + core
        pick = (lax.broadcasted_iota(jnp.int32, (total, mine), 0) == source).astype(BF)
        g_seven, dh6_terms = fc7_step(known, hidden, pick)
        hidden = hidden.transpose(1, 0, 2).reshape(mine, rows7)
        hidden = paired(hidden, "xh", across)
        dh6_terms, hidden = lax.optimization_barrier((swap(dh6_terms, "gz"), hidden))
        all_hidden = lax.all_gather(hidden, "y", axis=0, tiled=False).reshape(group, rows7)
        grad_hidden = dh6_terms.astype(F32).sum(axis=0)
        own_six = (grad_hidden * slope(h6_pre)).astype(BF)

        columns = g_seven.reshape(nx, cols7, nc * mine)
        columns = jnp.pad(columns, ((0, 0), (0, mine - cols7), (0, LANES - nc * mine)))
        both = jnp.concatenate([jnp.broadcast_to(own_six, (nx, mine, wide)), columns], axis=2)
        both = swap(both, gx)
        g_six = both[:, :, :wide].reshape(group, wide)
        columns = both[:, :cols7, wide : wide + nc * mine]

        feat_terms = features_back(g_six, weight6).reshape(nz, nx, feats)
        feat_terms, g_six = lax.optimization_barrier((feat_terms, g_six))
        feat_terms, gathered = lax.optimization_barrier((swap(feat_terms, "gz"), gathered))
        sent6 = weight_terms(nc - 1 - core, inputs, g_six, units)
        packs = swap(pack_dfeat(me_word, feat_terms, slopes), gx)
        gathered, sent6 = lax.optimization_barrier((gathered, sent6))
        all_lines = jax.vmap(bordered)(gathered)
        grad_fc6 = weight_terms(core, inputs, g_six, units, lax.ppermute(sent6, "core", pair))
        spread = spread_matrix(me, nx, half, cols)
        packed = conv_kernel_grad(high.reshape(1).astype(jnp.int32), all_lines, packs, spread, ny)
        packed = swap(packed, gy)

        runs = feats // part
        dfeat = packs[:, :runs, part : 2 * part].reshape(half, half, chans).astype(F32)
        dfeat = jnp.pad(dfeat, ((0, 0), (0, 1), (0, 0))).reshape(half * (half + 1), chans)
        g_lines = conv_slope(conv_pre, dfeat).reshape(side, LINE, chans)[:, :side]
        grad_images = conv_backward(bordered(g_lines), conv_weight, side)

        columns = columns.reshape(nh, nv, cols7, nc * mine)
        columns = jnp.where(high == 0, columns, columns[::-1])
        columns = columns.reshape(nh, nv, cols7, nc, mine).transpose(3, 2, 1, 0, 4)
        columns = columns.reshape(nc * cols7, group)
        terms7 = dot(columns, all_hidden, ((1,), (0,)))
        own7 = jnp.where(core == 0, terms7[:cols7], terms7[cols7:])
        sent7 = jnp.where(core == 0, terms7[cols7:], terms7[:cols7])
        grad_fc7 = (own7 + lax.ppermute(sent7, "core", pair)).T
        packed, grad_fc7 = lax.optimization_barrier((packed, grad_fc7))
        packed = packed.astype(F32).sum(axis=0)
        grad_conv = jnp.concatenate([packed[:, :part], packed[:, part:]], axis=0)
        return (grad_conv, grad_fc6, grad_fc7, grad_images)

    return on_device


def solution(mesh):
    nx, ny = mesh.shape["gx"], mesh.shape["gy"]
    nh = nc = 2
    nv, nz = nx // nh, ny // nc
    fine = Mesh(mesh.devices.reshape(nh, nv, nz, nc), ("xh", "y", "gz", "core"))
    gx, gy = ("xh", "y"), ("gz", "core")
    both = gx + gy
    return jax.shard_map(
        make(nh, nv, nz, nc),
        mesh=fine,
        in_specs=(P(both, None, None, None), P(), P(gx, gy), P(None, both), P(None, both)),
        out_specs=(P(gy, gx), P(gx, gy), P(None, both), P(both, None, None, None)),
        check_vma=False,
    )
```

```python
import jax
import jax.numpy as jnp
from jax import lax
from jax.experimental import pallas as pl
from jax.experimental.pallas import tpu as pltpu
from jax.sharding import Mesh, PartitionSpec as P

BF = jnp.bfloat16
F32 = jnp.float32
LANES = 128
LINE = 16
VMEM = pltpu.CompilerParams(vmem_limit_bytes=20 * 2**20)


def activate(value):
    return value * jax.nn.sigmoid(value)


def slope(value):
    sig = jax.nn.sigmoid(value)
    return sig * (1.0 + value * (1.0 - sig))


def dot(a, b, dims):
    return lax.dot_general(a, b, (dims, ((), ())), preferred_element_type=F32)


def cost(flops, moved, special=0):
    return pl.CostEstimate(flops=flops, bytes_accessed=moved, transcendentals=special)


def forward_kernel(image_ref, weight_ref, pre_ref, feat_ref, held_ref, sums_ref, pool_ref, sems):
    pix, chans = pre_ref.shape
    depth = image_ref.shape[1]
    rows = sums_ref.shape[1]

    def load(tap):
        return pltpu.make_async_copy(
            weight_ref.at[pl.ds(tap * depth, depth), :],
            held_ref.at[tap % 3, pl.ds(tap // 3 * depth, depth), :],
            sems.at[tap],
        )

    order = [3 * row + col for col in range(3) for row in range(3)]
    for tap in order:
        load(tap).start()
    image = jnp.concatenate([image_ref[k * LINE : k * LINE + rows, :] for k in range(3)], axis=1)
    for col in range(3):
        for row in range(3):
            load(3 * row + col).wait()
        sums_ref[col] = dot(image, held_ref[col], ((1,), (0,)))
    pre = sums_ref[0, 0:pix, :] + sums_ref[1, 1 : pix + 1, :] + sums_ref[2, 2 : pix + 2, :]
    pre_ref[...] = pre
    act = activate(pre).reshape(pix // (2 * LINE), 2, LINE, chans)
    lines = (act[:, 0] + act[:, 1]).reshape(pix // 2, chans)
    half = pix // 4
    for k in range(chans // LANES):
        pool_ref[k] = lines[:, k * LANES : (k + 1) * LANES]
        total = pool_ref[k, pl.ds(0, half, 2), :] + pool_ref[k, pl.ds(1, half, 2), :]
        feat_ref[:, k * LANES : (k + 1) * LANES] = (0.25 * total).astype(BF)


def conv_forward(lines, weight, side):
    depth, chans = lines.shape[1], weight.shape[1]
    pix = side * LINE
    return pl.pallas_call(
        forward_kernel,
        in_specs=[
            pl.BlockSpec(memory_space=pltpu.VMEM),
            pl.BlockSpec(memory_space=pl.ANY),
        ],
        out_shape=[
            jax.ShapeDtypeStruct((pix, chans), F32),
            jax.ShapeDtypeStruct((pix // 4, chans), BF),
        ],
        scratch_shapes=[
            pltpu.VMEM((3, 3 * depth, chans), BF),
            pltpu.VMEM((3, pix + LINE, chans), F32),
            pltpu.VMEM((chans // LANES, pix // 2, LANES), F32),
            pltpu.SemaphoreType.DMA((9,)),
        ],
        compiler_params=VMEM,
        cost_estimate=cost(18 * pix * depth * chans, weight.size * 2, pix * chans),
    )(lines, weight)


def turn_kernel(pre_ref, out_ref):
    pix, chans = pre_ref.shape
    grad = 0.25 * slope(pre_ref[...])
    grad = jnp.concatenate([grad, jnp.zeros((out_ref.shape[1] - pix, chans), F32)], axis=0)
    out_ref[...] = grad.T.astype(BF)


def turned_slope(pre, cols):
    pix, chans = pre.shape
    return pl.pallas_call(
        turn_kernel,
        out_shape=jax.ShapeDtypeStruct((chans, cols), BF),
        compiler_params=VMEM,
        cost_estimate=cost(8 * pix * chans, pix * chans * 6, pix * chans),
    )(pre)


def lines_kernel(pre_ref, dfeat_ref, out_ref, wide_ref):
    pix, chans = pre_ref.shape
    half = pix // 4
    for k in range(chans // LANES):
        dfeat = dfeat_ref[:, k * LANES : (k + 1) * LANES]
        wide_ref[k, pl.ds(0, half, 2), :] = dfeat
        wide_ref[k, pl.ds(1, half, 2), :] = dfeat
    spread = jnp.concatenate([wide_ref[k] for k in range(chans // LANES)], axis=1)
    spread = spread.reshape(pix // (2 * LINE), 1, LINE, chans)
    spread = jnp.broadcast_to(spread, (pix // (2 * LINE), 2, LINE, chans)).reshape(pix, chans)
    out_ref[...] = (0.25 * spread * slope(pre_ref[...])).astype(BF)


def conv_slope(pre, dfeat):
    pix, chans = pre.shape
    return pl.pallas_call(
        lines_kernel,
        out_shape=jax.ShapeDtypeStruct((pix, chans), BF),
        scratch_shapes=[pltpu.VMEM((chans // LANES, pix // 2, LANES), F32)],
        compiler_params=VMEM,
        cost_estimate=cost(8 * pix * chans, pix * chans * 6, pix * chans),
    )(pre, dfeat)


def fc7_kernel(known_ref, hidden_ref, pick_ref, seven_ref, terms_ref):
    count, mine, wide = hidden_ref.shape
    lines, both, _ = known_ref.shape
    rows7, cols7 = count * wide, both // 2

    def weight(k, start, size):
        block = known_ref[:, k * cols7 : (k + 1) * cols7, start : start + size]
        return block.reshape(lines * cols7, size)

    sevens = []
    for k in range(2):
        y7_pre = jnp.zeros((lines * cols7, mine), F32)
        for g in range(count):
            y7_pre += dot(weight(k, g * wide, wide), hidden_ref[g], ((1,), (1,)))
        cot = dot(weight(k, rows7, pick_ref.shape[0]), pick_ref[...], ((1,), (0,)))
        sevens.append((cot * slope(y7_pre)).astype(BF))
        seven_ref[:, k * mine : (k + 1) * mine] = sevens[k]
    for g in range(count):
        parts = [dot(sevens[k], weight(k, g * wide, wide), ((0,), (0,))) for k in range(2)]
        terms_ref[g] = (parts[0] + parts[1]).astype(BF)


def fc7_step(known, hidden, pick):
    lines, both, _ = known.shape
    return pl.pallas_call(
        fc7_kernel,
        out_shape=[
            jax.ShapeDtypeStruct((lines * both // 2, 2 * pick.shape[1]), BF),
            jax.ShapeDtypeStruct(hidden.shape, BF),
        ],
        compiler_params=VMEM,
        cost_estimate=cost(4 * known.size * pick.shape[1], known.size * 2),
    )(known, hidden, pick)


def back_kernel(g_ref, weight_ref, out_ref):
    out_ref[...] = dot(g_ref[...], weight_ref[...], ((1,), (1,))).astype(BF)


def features_back(g_six, weight):
    count, feats = g_six.shape[0], weight.shape[0]
    return pl.pallas_call(
        back_kernel,
        out_shape=jax.ShapeDtypeStruct((count, feats), BF),
        compiler_params=VMEM,
        cost_estimate=cost(2 * count * weight.size, weight.size * 2),
    )(g_six, weight)


def outer_kernel(which_ref, inputs_ref, g_ref, out_ref):
    units = out_ref.shape[1]
    g_six = g_ref[:, pl.ds(pl.multiple_of(which_ref[0] * units, units), units)]
    out_ref[...] = dot(inputs_ref[...], g_six, ((0,), (0,))).astype(out_ref.dtype)


def outer_add_kernel(which_ref, inputs_ref, g_ref, more_ref, out_ref):
    units = out_ref.shape[1]
    g_six = g_ref[:, pl.ds(pl.multiple_of(which_ref[0] * units, units), units)]
    out_ref[...] = dot(inputs_ref[...], g_six, ((0,), (0,))) + more_ref[...].astype(F32)


def weight_terms(which, inputs, g_six, units, more=None):
    feats = inputs.shape[1]
    operands = (inputs, g_six) if more is None else (inputs, g_six, more)
    in_vmem = [pl.BlockSpec(memory_space=pltpu.VMEM)] * len(operands)
    return pl.pallas_call(
        outer_kernel if more is None else outer_add_kernel,
        in_specs=[pl.BlockSpec(memory_space=pltpu.SMEM)] + in_vmem,
        out_shape=jax.ShapeDtypeStruct((feats, units), BF if more is None else F32),
        compiler_params=VMEM,
        cost_estimate=cost(2 * inputs.size * units, 4 * feats * units),
    )(which.reshape(1).astype(jnp.int32), *operands)


def pack_kernel(me_ref, terms_ref, slope_ref, out_ref, parts_ref, own_ref):
    nx, rows, _ = out_ref.shape
    feats = terms_ref.shape[2]
    run = LANES // 2
    runs = feats // run
    total = terms_ref[...].astype(F32).sum(axis=0).astype(BF).astype(F32)
    total = jnp.concatenate([total, jnp.zeros((nx, -feats % LANES), F32)], axis=1)
    parts_ref[...] = jnp.zeros(parts_ref.shape, F32)
    own_ref[...] = jnp.zeros(own_ref.shape, F32)
    for t in range(runs):
        tile = total[:, t // 2 * LANES : (t // 2 + 1) * LANES]
        other = pltpu.roll(tile, run, 1)
        low, high = (tile, other) if t % 2 == 0 else (other, tile)
        parts_ref[t % nx, t // nx * nx : (t // nx + 1) * nx, :] = low
        own_ref[pl.ds(t, nx, rows), :] = high
    lane = lax.broadcasted_iota(jnp.int32, (rows, LANES), 1)
    for e in range(nx):
        dest = lax.rem(me_ref[0] + e, nx)
        own = own_ref[pl.ds(pl.multiple_of(dest * rows, rows), rows), :]
        out_ref[dest, :, :LANES] = jnp.where(lane < run, parts_ref[e], own).astype(BF)
    out_ref[:, :, LANES:] = slope_ref[...]


def pack_dfeat(me, terms, slopes):
    _, nx, feats = terms.shape
    rows = nx * nx
    return pl.pallas_call(
        pack_kernel,
        in_specs=[
            pl.BlockSpec(memory_space=pltpu.SMEM),
            pl.BlockSpec(memory_space=pltpu.VMEM),
            pl.BlockSpec(memory_space=pltpu.VMEM),
        ],
        out_shape=jax.ShapeDtypeStruct((nx, rows, LANES + slopes.shape[2]), BF),
        scratch_shapes=[
            pltpu.VMEM((nx, rows, LANES), F32),
            pltpu.VMEM((nx * rows, LANES), F32),
        ],
        compiler_params=VMEM,
        cost_estimate=cost(4 * terms.size, terms.size * 2),
    )(me, terms, slopes)


def kernel_kernel(lines_ref, packs_ref, spread_ref, out_ref, grad_ref, flat_ref, wide_ref):
    images, part, _ = packs_ref.shape
    cols = spread_ref.shape[1]
    chans = lines_ref.shape[2]
    wide_ref[...] = packs_ref[:, :, :LANES].astype(F32).reshape(wide_ref.shape)
    for n in range(images):
        cells = wide_ref[pl.ds(n, wide_ref.shape[0] // images, images), :].astype(BF)
        spread = dot(cells, spread_ref[...], ((0,), (0,)))[:part]
        turned = (spread * packs_ref[n, :, LANES:].astype(F32)).astype(BF).astype(F32)
        moved = [turned] + [pltpu.roll(turned, j, 1) for j in (1, 2)]
        grad_ref[:, n * cols : (n + 1) * cols] = jnp.concatenate(moved, axis=0).astype(BF)
    for row in range(3):
        block = lines_ref[:, row * LINE : row * LINE + cols, :].reshape(images * cols, chans)
        term = dot(grad_ref[...], block, ((1,), (0,)))
        for col in range(3):
            tap = 3 * row + col
            flat_ref[tap * chans : (tap + 1) * chans, :] = term[col * part : (col + 1) * part].T
    count, size, _ = out_ref.shape
    for dest in range(count):
        at = dest * 2 * size
        both = [flat_ref[at : at + size, :], flat_ref[at + size : at + 2 * size, :]]
        out_ref[dest] = jnp.concatenate(both, axis=1).astype(BF)


def conv_kernel_grad(lines, packs, spread, count):
    images, _, chans = lines.shape
    _, part, _ = packs.shape
    cols = spread.shape[1]
    size = 9 * chans // (2 * count)
    return pl.pallas_call(
        kernel_kernel,
        out_shape=jax.ShapeDtypeStruct((count, size, 2 * part), BF),
        scratch_shapes=[
            pltpu.VMEM((3 * part, images * cols), BF),
            pltpu.VMEM((9 * chans, part), F32),
            pltpu.VMEM((images * part, LANES), F32),
        ],
        compiler_params=VMEM,
        cost_estimate=cost(18 * images * cols * chans * part, lines.size * 2),
    )(lines, packs, spread)


def backward_kernel(lines_ref, weight_ref, out_ref, sums_ref):
    step = pl.program_id(0)
    col = lax.rem(step, 3)
    rows = sums_ref.shape[1]
    start = pl.multiple_of((2 - step // 3) * LINE, LINE)
    part = dot(lines_ref[pl.ds(start, rows), :], weight_ref[...], ((1,), (1,)))

    @pl.when(step < 3)
    def _():
        sums_ref[col] = part

    @pl.when(step >= 3)
    def _():
        sums_ref[col] += part

    @pl.when(step == 8)
    def _():
        _, side, _, chans = out_ref.shape
        pix = side * LINE
        grad = sums_ref[0, 2 : pix + 2, :] + sums_ref[1, 1 : pix + 1, :] + sums_ref[2, 0:pix, :]
        out_ref[0] = grad.reshape(side, LINE, chans)[:, :side, :]


def conv_backward(lines, weight, side):
    chans = lines.shape[1]
    depth = weight.shape[0] // 9
    pix = side * LINE
    return pl.pallas_call(
        backward_kernel,
        grid=(9,),
        in_specs=[
            pl.BlockSpec(lines.shape, lambda t: (0, 0)),
            pl.BlockSpec((depth, chans), lambda t: (t, 0)),
        ],
        out_specs=pl.BlockSpec((1, side, side, depth), lambda t: (0, 0, 0, 0)),
        out_shape=jax.ShapeDtypeStruct((1, side, side, depth), F32),
        scratch_shapes=[pltpu.VMEM((3, pix + LINE, depth), F32)],
        compiler_params=VMEM,
        cost_estimate=cost(18 * pix * depth * chans, weight.size * 2),
    )(lines, weight)


def spread_matrix(me, nx, half, cols):
    at = lax.broadcasted_iota(jnp.int32, (nx * nx, cols), 0)
    pixel = lax.broadcasted_iota(jnp.int32, (nx * nx, cols), 1)
    source, run = at // nx, at % nx
    line, place = pixel // LINE, pixel % LINE
    per = half * half // nx
    cell = jnp.where((line < 2 * half) & (place < 2 * half), line // 2 * half + place // 2, -1)
    mine = per * source + run + (me < source).astype(jnp.int32)
    return ((cell == mine) & (run <= per)).astype(BF)


def swap(value, axis):
    return lax.all_to_all(value, axis, 0, 0, tiled=True)


def share(value, axis, count):
    return swap(jnp.broadcast_to(value, (count,) + value.shape), axis)


def bordered(maps):
    side, _, chans = maps.shape
    padded = jnp.pad(maps, ((1, 3), (1, LINE - side - 1), (0, 0)))
    return padded.reshape((side + 4) * LINE, chans)


def make(nh, nv, nz, nc):
    nx, ny = nh * nv, nz * nc
    gx = ("xh", "y")
    near = nz // nx
    gy = ("gz", "core")
    across = [(k, nh - 1 - k) for k in range(nh)]

    def paired(value, axis, way):
        return jnp.concatenate([value, lax.ppermute(value, axis, way)], axis=0)
    pair = [(k, nc - 1 - k) for k in range(nc)]

    def on_device(images, conv_weight, fc6_weight, fc7_weight, cotangent):
        side, chans = images.shape[1], images.shape[3]
        half = side // 2
        feats, units = fc6_weight.shape
        rows7, cols7 = fc7_weight.shape
        total = cotangent.shape[0]
        group = total // nc
        mine = group // nx
        wide = units * nc
        part = chans // nx
        cols = 2 * LANES
        high, core = lax.axis_index("xh"), lax.axis_index("core")
        me = high * nv + lax.axis_index("y")
        me_word = me.reshape(1).astype(jnp.int32)

        known = jnp.concatenate([fc7_weight.T, cotangent.T], axis=1)
        known = lax.all_gather(known, gx + ("core",), axis=0, tiled=False)
        known = known.reshape(nx, nc * cols7, rows7 + total)
        gathered = lax.all_gather(images[0], gx, axis=0, tiled=False)
        other6 = lax.ppermute(fc6_weight, "core", pair)
        lines = bordered(images[0])
        conv_pre, pooled = conv_forward(lines, conv_weight, side)
        slopes = turned_slope(conv_pre, cols).reshape(nx, part, cols)
        feat = pooled.reshape(half, half + 1, chans)[:, :half].reshape(nx, feats)
        inputs = share(swap(feat, gx), "gz", nz).reshape(group, feats)
        first = jnp.where(core == 0, fc6_weight, other6)
        second = jnp.where(core == 0, other6, fc6_weight)
        weight6 = jnp.concatenate([first, second], axis=1)
        inputs, weight6 = lax.optimization_barrier((inputs, weight6))

        h6_terms = dot(inputs, weight6, ((1,), (0,))).astype(BF).reshape(nx, mine, wide)
        h6_pre = swap(h6_terms, gx).astype(F32).sum(axis=0)
        own_hidden = activate(h6_pre).astype(BF)
        hidden = share(own_hidden, "gz", nz)

        place = lax.broadcasted_iota(jnp.int32, (total, mine), 1)
        source = (place % nx) * ny + (me * near + place // nx) * nc + core
        pick = (lax.broadcasted_iota(jnp.int32, (total, mine), 0) == source).astype(BF)
        g_seven, dh6_terms = fc7_step(known, hidden, pick)
        hidden = hidden.transpose(1, 0, 2).reshape(mine, rows7)
        hidden = paired(hidden, "xh", across)
        dh6_terms, hidden = lax.optimization_barrier((swap(dh6_terms, "gz"), hidden))
        grad_hidden = dh6_terms.astype(F32).sum(axis=0)
        own_six = (grad_hidden * slope(h6_pre)).astype(BF)

        columns = g_seven.reshape(nx, cols7, nc * mine)
        columns = jnp.pad(columns, ((0, 0), (0, mine - cols7), (0, LANES - nc * mine)))
        both = jnp.concatenate([jnp.broadcast_to(own_six, (nx, mine, wide)), columns], axis=2)
        both, hidden = lax.optimization_barrier((swap(both, gx), hidden))
        all_hidden = lax.all_gather(hidden, "y", axis=0, tiled=False).reshape(group, rows7)
        g_six = both[:, :, :wide].reshape(group, wide)
        columns = both[:, :cols7, wide : wide + nc * mine]

        feat_terms = features_back(g_six, weight6).reshape(nz, nx, feats)
        feat_terms, g_six = lax.optimization_barrier((feat_terms, g_six))
        feat_terms, gathered = lax.optimization_barrier((swap(feat_terms, "gz"), gathered))
        sent6 = weight_terms(nc - 1 - core, inputs, g_six, units)
        packs = swap(pack_dfeat(me_word, feat_terms, slopes), gx)
        gathered, sent6 = lax.optimization_barrier((gathered, sent6))
        all_lines = jax.vmap(bordered)(gathered)
        grad_fc6 = weight_terms(core, inputs, g_six, units, lax.ppermute(sent6, "core", pair))
        spread = spread_matrix(me, nx, half, cols)
        packed = conv_kernel_grad(all_lines, packs, spread, ny)
        packed = swap(packed, gy)

        runs = feats // part
        dfeat = packs[:, :runs, part : 2 * part].reshape(half, half, chans).astype(F32)
        dfeat = jnp.pad(dfeat, ((0, 0), (0, 1), (0, 0))).reshape(half * (half + 1), chans)
        g_lines = conv_slope(conv_pre, dfeat).reshape(side, LINE, chans)[:, :side]
        grad_images = conv_backward(bordered(g_lines), conv_weight, side)

        columns = columns.reshape(nh, nv, cols7, nc * mine)
        columns = jnp.where(high == 0, columns, columns[::-1])
        columns = columns.reshape(nh, nv, cols7, nc, mine).transpose(3, 2, 1, 0, 4)
        columns = columns.reshape(nc * cols7, group)
        terms7 = dot(columns, all_hidden, ((1,), (0,)))
        own7 = jnp.where(core == 0, terms7[:cols7], terms7[cols7:])
        sent7 = jnp.where(core == 0, terms7[cols7:], terms7[:cols7])
        grad_fc7 = (own7 + lax.ppermute(sent7, "core", pair)).T
        packed, grad_fc7 = lax.optimization_barrier((packed, grad_fc7))
        packed = packed.astype(F32).sum(axis=0)
        grad_conv = jnp.concatenate([packed[:, :part], packed[:, part:]], axis=0)
        return (grad_conv, grad_fc6, grad_fc7, grad_images)

    return on_device


def solution(mesh):
    nx, ny = mesh.shape["gx"], mesh.shape["gy"]
    nh = nc = 2
    nv, nz = nx // nh, ny // nc
    fine = Mesh(mesh.devices.reshape(nh, nv, nz, nc), ("xh", "y", "gz", "core"))
    gx, gy = ("xh", "y"), ("gz", "core")
    both = gx + gy
    return jax.shard_map(
        make(nh, nv, nz, nc),
        mesh=fine,
        in_specs=(P(both, None, None, None), P(), P(gx, gy), P(None, both), P(None, both)),
        out_specs=(P(gy, gx), P(gx, gy), P(None, both), P(both, None, None, None)),
        check_vma=False,
    )
```

```python
import jax
import jax.numpy as jnp
from jax import lax
from jax.experimental import pallas as pl
from jax.experimental.pallas import tpu as pltpu
from jax.sharding import Mesh, PartitionSpec as P

BF = jnp.bfloat16
F32 = jnp.float32
LANES = 128
LINE = 16
VMEM = pltpu.CompilerParams(vmem_limit_bytes=20 * 2**20)


def activate(value):
    return value * jax.nn.sigmoid(value)


def slope(value):
    sig = jax.nn.sigmoid(value)
    return sig * (1.0 + value * (1.0 - sig))


def dot(a, b, dims):
    return lax.dot_general(a, b, (dims, ((), ())), preferred_element_type=F32)


LITTLE = pl.CostEstimate(flops=1000, bytes_accessed=1000, transcendentals=0)


def cost(flops, moved, special=0):
    return pl.CostEstimate(flops=flops, bytes_accessed=moved, transcendentals=special)


def forward_kernel(image_ref, weight_ref, pre_ref, feat_ref, held_ref, sums_ref, pool_ref, runs_ref, sems):
    pix, chans = pre_ref.shape
    depth = image_ref.shape[1]
    rows = sums_ref.shape[1]

    def load(tap):
        return pltpu.make_async_copy(
            weight_ref.at[pl.ds(tap * depth, depth), :],
            held_ref.at[tap % 3, pl.ds(tap // 3 * depth, depth), :],
            sems.at[tap],
        )

    order = [3 * row + col for col in range(3) for row in range(3)]
    for tap in order:
        load(tap).start()
    image = jnp.concatenate([image_ref[k * LINE : k * LINE + rows, :] for k in range(3)], axis=1)
    for col in range(3):
        for row in range(3):
            load(3 * row + col).wait()
        sums_ref[col] = dot(image, held_ref[col], ((1,), (0,)))
    pre = sums_ref[0, 0:pix, :] + sums_ref[1, 1 : pix + 1, :] + sums_ref[2, 2 : pix + 2, :]
    pre_ref[...] = pre
    act = activate(pre).reshape(pix // (2 * LINE), 2, LINE, chans)
    lines = (act[:, 0] + act[:, 1]).reshape(pix // 2, chans)
    half = pix // 4
    side = pix // LINE // 2
    run = LANES // 2
    runs = feat_ref.shape[1] // run
    for k in range(chans // LANES):
        pool_ref[k] = lines[:, k * LANES : (k + 1) * LANES]
        total = 0.25 * (pool_ref[k, pl.ds(0, half, 2), :] + pool_ref[k, pl.ds(1, half, 2), :])
        other = pltpu.roll(total, run, 1)
        for cell in range(side * side):
            row = cell // side * (LINE // 2) + cell % side
            for part in range(2):
                dest, t = divmod(cell * (chans // run) + 2 * k + part, runs)
                at = t % 2 * run
                piece = total if t % 2 == part else other
                runs_ref[dest : dest + 1, t * run : (t + 1) * run] = piece[row : row + 1, at : at + run]
    feat_ref[...] = runs_ref[...].astype(BF)


def conv_forward(lines, weight, side, nx):
    depth, chans = lines.shape[1], weight.shape[1]
    pix = side * LINE
    feats = side * side // 4 * chans // nx
    return pl.pallas_call(
        forward_kernel,
        in_specs=[
            pl.BlockSpec(memory_space=pltpu.VMEM),
            pl.BlockSpec(memory_space=pl.ANY),
        ],
        out_shape=[
            jax.ShapeDtypeStruct((pix, chans), F32),
            jax.ShapeDtypeStruct((nx, feats), BF),
        ],
        scratch_shapes=[
            pltpu.VMEM((3, 3 * depth, chans), BF),
            pltpu.VMEM((3, pix + LINE, chans), F32),
            pltpu.VMEM((chans // LANES, pix // 2, LANES), F32),
            pltpu.VMEM((nx, feats), F32),
            pltpu.SemaphoreType.DMA((9,)),
        ],
        compiler_params=VMEM,
        cost_estimate=cost(18 * pix * depth * chans, weight.size * 2, pix * chans),
    )(lines, weight)


def turn_kernel(pre_ref, out_ref):
    pix, chans = pre_ref.shape
    grad = 0.25 * slope(pre_ref[...])
    grad = jnp.concatenate([grad, jnp.zeros((out_ref.shape[1] - pix, chans), F32)], axis=0)
    out_ref[...] = grad.T.astype(BF)


def turned_slope(pre, cols):
    pix, chans = pre.shape
    return pl.pallas_call(
        turn_kernel,
        out_shape=jax.ShapeDtypeStruct((chans, cols), BF),
        compiler_params=VMEM,
        cost_estimate=cost(8 * pix * chans, pix * chans * 6, pix * chans),
    )(pre)


def lines_kernel(pre_ref, dfeat_ref, out_ref, wide_ref):
    pix, chans = pre_ref.shape
    half = pix // 4
    for k in range(chans // LANES):
        dfeat = dfeat_ref[:, k * LANES : (k + 1) * LANES]
        wide_ref[k, pl.ds(0, half, 2), :] = dfeat
        wide_ref[k, pl.ds(1, half, 2), :] = dfeat
    spread = jnp.concatenate([wide_ref[k] for k in range(chans // LANES)], axis=1)
    spread = spread.reshape(pix // (2 * LINE), 1, LINE, chans)
    spread = jnp.broadcast_to(spread, (pix // (2 * LINE), 2, LINE, chans)).reshape(pix, chans)
    out_ref[...] = (0.25 * spread * slope(pre_ref[...])).astype(BF)


def conv_slope(pre, dfeat):
    pix, chans = pre.shape
    return pl.pallas_call(
        lines_kernel,
        out_shape=jax.ShapeDtypeStruct((pix, chans), BF),
        scratch_shapes=[pltpu.VMEM((chans // LANES, pix // 2, LANES), F32)],
        compiler_params=VMEM,
        cost_estimate=LITTLE,
    )(pre, dfeat)


def fc7_kernel(known_ref, hidden_ref, pick_ref, seven_ref, terms_ref):
    count, mine, wide = hidden_ref.shape
    lines, both, _ = known_ref.shape
    rows7, cols7 = count * wide, both // 2

    def weight(k, start, size):
        block = known_ref[:, k * cols7 : (k + 1) * cols7, start : start + size]
        return block.reshape(lines * cols7, size)

    sevens = []
    for k in range(2):
        y7_pre = jnp.zeros((lines * cols7, mine), F32)
        for g in range(count):
            y7_pre += dot(weight(k, g * wide, wide), hidden_ref[g], ((1,), (1,)))
        cot = dot(weight(k, rows7, pick_ref.shape[0]), pick_ref[...], ((1,), (0,)))
        sevens.append((cot * slope(y7_pre)).astype(BF))
        seven_ref[:, k * mine : (k + 1) * mine] = sevens[k]
    for g in range(count):
        parts = [dot(sevens[k], weight(k, g * wide, wide), ((0,), (0,))) for k in range(2)]
        terms_ref[g] = (parts[0] + parts[1]).astype(BF)


def fc7_step(known, hidden, pick):
    lines, both, _ = known.shape
    return pl.pallas_call(
        fc7_kernel,
        out_shape=[
            jax.ShapeDtypeStruct((lines * both // 2, 2 * pick.shape[1]), BF),
            jax.ShapeDtypeStruct(hidden.shape, BF),
        ],
        compiler_params=VMEM,
        cost_estimate=cost(4 * known.size * pick.shape[1], known.size * 2),
    )(known, hidden, pick)


def back_kernel(g_ref, weight_ref, out_ref):
    out_ref[...] = dot(g_ref[...], weight_ref[...], ((1,), (1,))).astype(BF)


def features_back(g_six, weight):
    count, feats = g_six.shape[0], weight.shape[0]
    return pl.pallas_call(
        back_kernel,
        out_shape=jax.ShapeDtypeStruct((count, feats), BF),
        compiler_params=VMEM,
        cost_estimate=cost(2 * count * weight.size, weight.size * 2),
    )(g_six, weight)


def outer_kernel(which_ref, inputs_ref, g_ref, out_ref):
    units = out_ref.shape[1]
    g_six = g_ref[:, pl.ds(pl.multiple_of(which_ref[0] * units, units), units)]
    out_ref[...] = dot(inputs_ref[...], g_six, ((0,), (0,))).astype(out_ref.dtype)


def outer_add_kernel(which_ref, inputs_ref, g_ref, more_ref, out_ref):
    units = out_ref.shape[1]
    g_six = g_ref[:, pl.ds(pl.multiple_of(which_ref[0] * units, units), units)]
    out_ref[...] = dot(inputs_ref[...], g_six, ((0,), (0,))) + more_ref[...].astype(F32)


def weight_terms(which, inputs, g_six, units, more=None):
    feats = inputs.shape[1]
    operands = (inputs, g_six) if more is None else (inputs, g_six, more)
    in_vmem = [pl.BlockSpec(memory_space=pltpu.VMEM)] * len(operands)
    return pl.pallas_call(
        outer_kernel if more is None else outer_add_kernel,
        in_specs=[pl.BlockSpec(memory_space=pltpu.SMEM)] + in_vmem,
        out_shape=jax.ShapeDtypeStruct((feats, units), BF if more is None else F32),
        compiler_params=VMEM,
        cost_estimate=LITTLE,
    )(which.reshape(1).astype(jnp.int32), *operands)


def pack_kernel(me_ref, terms_ref, slope_ref, out_ref, parts_ref, own_ref):
    nx, rows, _ = out_ref.shape
    feats = terms_ref.shape[2]
    run = LANES // 2
    runs = feats // run
    total = terms_ref[...].astype(F32).sum(axis=0).astype(BF).astype(F32)
    total = jnp.concatenate([total, jnp.zeros((nx, -feats % LANES), F32)], axis=1)
    parts_ref[...] = jnp.zeros(parts_ref.shape, F32)
    own_ref[...] = jnp.zeros(own_ref.shape, F32)
    for t in range(runs):
        tile = total[:, t // 2 * LANES : (t // 2 + 1) * LANES]
        other = pltpu.roll(tile, run, 1)
        low, high = (tile, other) if t % 2 == 0 else (other, tile)
        parts_ref[t % nx, t // nx * nx : (t // nx + 1) * nx, :] = low
        own_ref[pl.ds(t, nx, rows), :] = high
    lane = lax.broadcasted_iota(jnp.int32, (rows, LANES), 1)
    for e in range(nx):
        dest = lax.rem(me_ref[0] + e, nx)
        own = own_ref[pl.ds(pl.multiple_of(dest * rows, rows), rows), :]
        out_ref[dest, :, :LANES] = jnp.where(lane < run, parts_ref[e], own).astype(BF)
    out_ref[:, :, LANES:] = slope_ref[...]


def pack_dfeat(me, terms, slopes):
    _, nx, feats = terms.shape
    rows = nx * nx
    return pl.pallas_call(
        pack_kernel,
        in_specs=[
            pl.BlockSpec(memory_space=pltpu.SMEM),
            pl.BlockSpec(memory_space=pltpu.VMEM),
            pl.BlockSpec(memory_space=pltpu.VMEM),
        ],
        out_shape=jax.ShapeDtypeStruct((nx, rows, LANES + slopes.shape[2]), BF),
        scratch_shapes=[
            pltpu.VMEM((nx, rows, LANES), F32),
            pltpu.VMEM((nx * rows, LANES), F32),
        ],
        compiler_params=VMEM,
        cost_estimate=cost(4 * terms.size, terms.size * 2),
    )(me, terms, slopes)


def kernel_kernel(place_ref, lines_ref, packs_ref, spread_ref, own_ref, sent_ref, grad_ref, flat_ref, wide_ref):
    images, part, _ = packs_ref.shape
    cols = spread_ref.shape[1]
    chans = lines_ref.shape[2]
    wide_ref[...] = packs_ref[:, :, :LANES].astype(F32).reshape(wide_ref.shape)
    for k in range(images):
        n = lax.rem(place_ref[0] + k % 2, 2) * (images // 2) + k // 2
        cells = wide_ref[pl.ds(n, wide_ref.shape[0] // images, images), :].astype(BF)
        spread = dot(cells, spread_ref[...], ((0,), (0,)))[:part]
        turned = (spread * packs_ref[n, :, LANES:].astype(F32)).astype(BF).astype(F32)
        moved = [turned] + [pltpu.roll(turned, j, 1) for j in (1, 2)]
        grad_ref[:, k * cols : (k + 1) * cols] = jnp.concatenate(moved, axis=0).astype(BF)
    for row in range(3):
        block = lines_ref[:, row * LINE : row * LINE + cols, :].reshape(images * cols, chans)
        term = dot(grad_ref[...], block, ((1,), (0,)))
        for col in range(3):
            tap = 3 * row + col
            flat_ref[tap * chans : (tap + 1) * chans, :] = term[col * part : (col + 1) * part].T
    count, size, _ = own_ref.shape
    for core, out_ref in ((place_ref[1], own_ref), (1 - place_ref[1], sent_ref)):
        for dest in range(count):
            at = pl.multiple_of((2 * dest + core) * (2 * size), 2 * size)
            both = [flat_ref[pl.ds(at + k * size, size), :] for k in range(2)]
            out_ref[dest] = jnp.concatenate(both, axis=1).astype(out_ref.dtype)


def conv_kernel_grad(place, lines, packs, spread, count):
    images, _, chans = lines.shape
    _, part, _ = packs.shape
    cols = spread.shape[1]
    size = 9 * chans // (4 * count)
    return pl.pallas_call(
        kernel_kernel,
        in_specs=[pl.BlockSpec(memory_space=pltpu.SMEM)] + [pl.BlockSpec(memory_space=pltpu.VMEM)] * 3,
        out_shape=[jax.ShapeDtypeStruct((count, size, 2 * part), kind) for kind in (F32, BF)],
        scratch_shapes=[
            pltpu.VMEM((3 * part, images * cols), BF),
            pltpu.VMEM((9 * chans, part), F32),
            pltpu.VMEM((images * part, LANES), F32),
        ],
        compiler_params=VMEM,
        cost_estimate=cost(18 * images * cols * chans * part, lines.size * 2),
    )(place, lines, packs, spread)


def backward_kernel(lines_ref, weight_ref, out_ref, sums_ref):
    step = pl.program_id(0)
    col = lax.rem(step, 3)
    rows = sums_ref.shape[1]
    start = pl.multiple_of((2 - step // 3) * LINE, LINE)
    part = dot(lines_ref[pl.ds(start, rows), :], weight_ref[...], ((1,), (1,)))

    @pl.when(step < 3)
    def _():
        sums_ref[col] = part

    @pl.when(step >= 3)
    def _():
        sums_ref[col] += part

    @pl.when(step == 8)
    def _():
        _, side, _, chans = out_ref.shape
        pix = side * LINE
        grad = sums_ref[0, 2 : pix + 2, :] + sums_ref[1, 1 : pix + 1, :] + sums_ref[2, 0:pix, :]
        out_ref[0] = grad.reshape(side, LINE, chans)[:, :side, :]


def conv_backward(lines, weight, side):
    chans = lines.shape[1]
    depth = weight.shape[0] // 9
    pix = side * LINE
    return pl.pallas_call(
        backward_kernel,
        grid=(9,),
        in_specs=[
            pl.BlockSpec(lines.shape, lambda t: (0, 0)),
            pl.BlockSpec((depth, chans), lambda t: (t, 0)),
        ],
        out_specs=pl.BlockSpec((1, side, side, depth), lambda t: (0, 0, 0, 0)),
        out_shape=jax.ShapeDtypeStruct((1, side, side, depth), F32),
        scratch_shapes=[pltpu.VMEM((3, pix + LINE, depth), F32)],
        compiler_params=VMEM,
        cost_estimate=LITTLE,
    )(lines, weight)


def spread_matrix(me, nx, half, cols):
    at = lax.broadcasted_iota(jnp.int32, (nx * nx, cols), 0)
    pixel = lax.broadcasted_iota(jnp.int32, (nx * nx, cols), 1)
    source, run = at // nx, at % nx
    line, place = pixel // LINE, pixel % LINE
    per = half * half // nx
    cell = jnp.where((line < 2 * half) & (place < 2 * half), line // 2 * half + place // 2, -1)
    mine = per * source + run + (me < source).astype(jnp.int32)
    return ((cell == mine) & (run <= per)).astype(BF)


def swap(value, axis):
    return lax.all_to_all(value, axis, 0, 0, tiled=True)


def share(value, axis, count):
    return swap(jnp.broadcast_to(value, (count,) + value.shape), axis)


def bordered(maps):
    side, _, chans = maps.shape
    padded = jnp.pad(maps, ((1, 3), (1, LINE - side - 1), (0, 0)))
    return padded.reshape((side + 4) * LINE, chans)


def make(nh, nv, nz, nc):
    nx, ny = nh * nv, nz * nc
    gx = ("xh", "y")
    near = nz // nx
    gy = ("gz", "core")
    across = [(k, nh - 1 - k) for k in range(nh)]

    def paired(value, axis, way):
        return jnp.concatenate([value, lax.ppermute(value, axis, way)], axis=0)
    pair = [(k, nc - 1 - k) for k in range(nc)]

    def on_device(images, conv_weight, fc6_weight, fc7_weight, cotangent):
        side, chans = images.shape[1], images.shape[3]
        half = side // 2
        feats, units = fc6_weight.shape
        rows7, cols7 = fc7_weight.shape
        total = cotangent.shape[0]
        group = total // nc
        mine = group // nx
        wide = units * nc
        part = chans // nx
        cols = 2 * LANES
        high, core = lax.axis_index("xh"), lax.axis_index("core")
        me = high * nv + lax.axis_index("y")
        me_word = me.reshape(1).astype(jnp.int32)

        known = jnp.concatenate([fc7_weight.T, cotangent.T], axis=1)
        known = lax.all_gather(known, gx + ("core",), axis=0, tiled=False)
        known = known.reshape(nx, nc * cols7, rows7 + total)
        other6 = lax.ppermute(fc6_weight, "core", pair)
        lines = bordered(images[0])
        conv_pre, feat = conv_forward(lines, conv_weight, side, nx)
        slopes = turned_slope(conv_pre, cols).reshape(nx, part, cols)
        feat, image = lax.optimization_barrier((feat, images))
        gathered = lax.all_gather(paired(image, "xh", across), "y", axis=0, tiled=True)
        inputs = share(swap(feat, gx), "gz", nz).reshape(group, feats)
        first = jnp.where(core == 0, fc6_weight, other6)
        second = jnp.where(core == 0, other6, fc6_weight)
        weight6 = jnp.concatenate([first, second], axis=1)
        inputs, weight6 = lax.optimization_barrier((inputs, weight6))

        h6_terms = dot(inputs, weight6, ((1,), (0,))).astype(BF).reshape(nx, mine, wide)
        h6_pre = swap(h6_terms, gx).astype(F32).sum(axis=0)
        own_hidden = activate(h6_pre).astype(BF)
        hidden = share(own_hidden, "gz", nz)

        place = lax.broadcasted_iota(jnp.int32, (total, mine), 1)
        source = (place % nx) * ny + (me * near + place // nx) * nc + core
        pick = (lax.broadcasted_iota(jnp.int32, (total, mine), 0) == source).astype(BF)
        g_seven, dh6_terms = fc7_step(known, hidden, pick)
        dh6_terms, hidden = lax.optimization_barrier((dh6_terms, hidden))
        hidden = hidden.transpose(1, 0, 2).reshape(mine, rows7)
        hidden = paired(hidden, "xh", across)
        dh6_terms, hidden = lax.optimization_barrier((swap(dh6_terms, "gz"), hidden))
        all_hidden = lax.all_gather(hidden, "y", axis=0, tiled=False).reshape(group, rows7)
        grad_hidden = dh6_terms.astype(F32).sum(axis=0)
        own_six = (grad_hidden * slope(h6_pre)).astype(BF)

        columns = g_seven.reshape(nx, cols7, nc * mine)
        columns = jnp.pad(columns, ((0, 0), (0, mine - cols7), (0, LANES - nc * mine)))
        both = jnp.concatenate([jnp.broadcast_to(own_six, (nx, mine, wide)), columns], axis=2)
        both, gathered = lax.optimization_barrier((swap(both, gx), gathered))
        g_six = both[:, :, :wide].reshape(group, wide)
        columns = both[:, :cols7, wide : wide + nc * mine]

        feat_terms = features_back(g_six, weight6).reshape(nz, nx, feats)
        feat_terms, g_six = lax.optimization_barrier((feat_terms, g_six))
        feat_terms = swap(feat_terms, "gz")
        sent6 = weight_terms(nc - 1 - core, inputs, g_six, units)
        packs = swap(pack_dfeat(me_word, feat_terms, slopes), gx)
        gathered, sent6 = lax.optimization_barrier((gathered, sent6))
        all_lines = jax.vmap(bordered)(gathered)
        grad_fc6 = weight_terms(core, inputs, g_six, units, lax.ppermute(sent6, "core", pair))
        spread = spread_matrix(me, nx, half, cols)
        place = jnp.stack([high, core]).astype(jnp.int32)
        packed, sent = conv_kernel_grad(place, all_lines, packs, spread, nz)
        packed = (packed + lax.ppermute(sent, "core", pair).astype(F32)).astype(BF)
        columns = columns.reshape(nh, nv, cols7, nc * mine)
        columns = jnp.where(high == 0, columns, columns[::-1])
        columns = columns.reshape(nh, nv, cols7, nc, mine).transpose(3, 2, 1, 0, 4)
        columns = columns.reshape(nc * cols7, group)
        terms7 = dot(columns, all_hidden, ((1,), (0,)))
        own7 = jnp.where(core == 0, terms7[:cols7], terms7[cols7:])
        sent7 = jnp.where(core == 0, terms7[cols7:], terms7[:cols7])
        packed = swap(packed, "gz")

        runs = feats // part
        dfeat = packs[:, :runs, part : 2 * part].reshape(half, half, chans).astype(F32)
        dfeat = jnp.pad(dfeat, ((0, 0), (0, 1), (0, 0))).reshape(half * (half + 1), chans)
        g_lines = conv_slope(conv_pre, dfeat).reshape(side, LINE, chans)[:, :side]
        grad_images = conv_backward(bordered(g_lines), conv_weight, side)

        grad_fc7 = (own7 + lax.ppermute(sent7, "core", pair)).T
        packed, grad_fc7 = lax.optimization_barrier((packed, grad_fc7))
        packed = packed.astype(F32).sum(axis=0)
        grad_conv = jnp.concatenate([packed[:, :part], packed[:, part:]], axis=0)
        return (grad_conv, grad_fc6, grad_fc7, grad_images)

    return on_device


def solution(mesh):
    nx, ny = mesh.shape["gx"], mesh.shape["gy"]
    nh = nc = 2
    nv, nz = nx // nh, ny // nc
    fine = Mesh(mesh.devices.reshape(nh, nv, nz, nc), ("xh", "y", "gz", "core"))
    gx, gy = ("xh", "y"), ("gz", "core")
    both = gx + gy
    return jax.shard_map(
        make(nh, nv, nz, nc),
        mesh=fine,
        in_specs=(P(both, None, None, None), P(), P(gx, gy), P(None, both), P(None, both)),
        out_specs=(P(gy, gx), P(gx, gy), P(None, both), P(both, None, None, None)),
        check_vma=False,
    )
```

```python
import jax
import jax.numpy as jnp
from jax import lax
from jax.experimental import pallas as pl
from jax.experimental.pallas import tpu as pltpu
from jax.sharding import Mesh, PartitionSpec as P

BF = jnp.bfloat16
F32 = jnp.float32
LANES = 128
LINE = 16
VMEM = pltpu.CompilerParams(vmem_limit_bytes=20 * 2**20)


def activate(value):
    return value * jax.nn.sigmoid(value)


def slope(value):
    sig = jax.nn.sigmoid(value)
    return sig * (1.0 + value * (1.0 - sig))


def dot(a, b, dims):
    return lax.dot_general(a, b, (dims, ((), ())), preferred_element_type=F32)


LITTLE = pl.CostEstimate(flops=1000, bytes_accessed=1000, transcendentals=0)


def cost(flops, moved, special=0):
    return pl.CostEstimate(flops=flops, bytes_accessed=moved, transcendentals=special)


def forward_kernel(image_ref, weight_ref, pre_ref, feat_ref, held_ref, sums_ref, pool_ref, runs_ref, sems):
    pix, chans = pre_ref.shape
    depth = image_ref.shape[1]
    rows = sums_ref.shape[1]

    def load(tap):
        return pltpu.make_async_copy(
            weight_ref.at[pl.ds(tap * depth, depth), :],
            held_ref.at[tap % 3, pl.ds(tap // 3 * depth, depth), :],
            sems.at[tap],
        )

    order = [3 * row + col for col in range(3) for row in range(3)]
    for tap in order:
        load(tap).start()
    image = jnp.concatenate([image_ref[k * LINE : k * LINE + rows, :] for k in range(3)], axis=1)
    for col in range(3):
        for row in range(3):
            load(3 * row + col).wait()
        sums_ref[col] = dot(image, held_ref[col], ((1,), (0,)))
    pre = sums_ref[0, 0:pix, :] + sums_ref[1, 1 : pix + 1, :] + sums_ref[2, 2 : pix + 2, :]
    pre_ref[...] = pre
    act = activate(pre).reshape(pix // (2 * LINE), 2, LINE, chans)
    lines = (act[:, 0] + act[:, 1]).reshape(pix // 2, chans)
    half = pix // 4
    side = pix // LINE // 2
    run = LANES // 2
    dests, rows, width = feat_ref.shape
    runs = side * side * chans // (dests * run)
    runs_ref[...] = jnp.zeros(runs_ref.shape, F32)
    for k in range(chans // LANES):
        pool_ref[k] = lines[:, k * LANES : (k + 1) * LANES]
        total = 0.25 * (pool_ref[k, pl.ds(0, half, 2), :] + pool_ref[k, pl.ds(1, half, 2), :])
        other = pltpu.roll(total, run, 1)
        for cell in range(side * side):
            line = cell // side * (LINE // 2) + cell % side
            for part in range(2):
                dest, t = divmod(cell * (chans // run) + 2 * k + part, runs)
                at = t % 2 * run
                piece = total if t % 2 == part else other
                row, lane = divmod(t * run, width)
                row = dest * rows + row
                runs_ref[row : row + 1, lane : lane + run] = piece[line : line + 1, at : at + run]
    feat_ref[...] = runs_ref[...].astype(BF).reshape(dests, rows, width)


def conv_forward(lines, weight, side, nx):
    depth, chans = lines.shape[1], weight.shape[1]
    pix = side * LINE
    rows, width = LINE, 2 * LANES
    return pl.pallas_call(
        forward_kernel,
        in_specs=[
            pl.BlockSpec(memory_space=pltpu.VMEM),
            pl.BlockSpec(memory_space=pl.ANY),
        ],
        out_shape=[
            jax.ShapeDtypeStruct((pix, chans), F32),
            jax.ShapeDtypeStruct((nx, rows, width), BF),
        ],
        scratch_shapes=[
            pltpu.VMEM((3, 3 * depth, chans), BF),
            pltpu.VMEM((3, pix + LINE, chans), F32),
            pltpu.VMEM((chans // LANES, pix // 2, LANES), F32),
            pltpu.VMEM((nx * rows, width), F32),
            pltpu.SemaphoreType.DMA((9,)),
        ],
        compiler_params=VMEM,
        cost_estimate=cost(18 * pix * depth * chans, weight.size * 2, pix * chans),
    )(lines, weight)


def copies_kernel(feat_ref, out_ref):
    feats = out_ref.shape[2]
    _, rows, width = feat_ref.shape
    value = feat_ref[...].astype(F32)
    flat = jnp.concatenate([value[:, k, :] for k in range(rows)], axis=1)[:, :feats].astype(BF)
    for k in range(out_ref.shape[0]):
        out_ref[k] = flat


def feature_copies(feat, count, feats):
    return pl.pallas_call(
        copies_kernel,
        out_shape=jax.ShapeDtypeStruct((count, feat.shape[0], feats), BF),
        compiler_params=VMEM,
        cost_estimate=cost(feat.size, feat.size * 2 * count),
    )(feat)


def turn_kernel(pre_ref, out_ref):
    pix, chans = pre_ref.shape
    grad = 0.25 * slope(pre_ref[...])
    grad = jnp.concatenate([grad, jnp.zeros((out_ref.shape[1] - pix, chans), F32)], axis=0)
    out_ref[...] = grad.T.astype(BF)


def turned_slope(pre, cols):
    pix, chans = pre.shape
    return pl.pallas_call(
        turn_kernel,
        out_shape=jax.ShapeDtypeStruct((chans, cols), BF),
        compiler_params=VMEM,
        cost_estimate=cost(8 * pix * chans, pix * chans * 6, pix * chans),
    )(pre)


def lines_kernel(pre_ref, dfeat_ref, out_ref, wide_ref):
    pix, chans = pre_ref.shape
    half = pix // 4
    for k in range(chans // LANES):
        dfeat = dfeat_ref[:, k * LANES : (k + 1) * LANES]
        wide_ref[k, pl.ds(0, half, 2), :] = dfeat
        wide_ref[k, pl.ds(1, half, 2), :] = dfeat
    spread = jnp.concatenate([wide_ref[k] for k in range(chans // LANES)], axis=1)
    spread = spread.reshape(pix // (2 * LINE), 1, LINE, chans)
    spread = jnp.broadcast_to(spread, (pix // (2 * LINE), 2, LINE, chans)).reshape(pix, chans)
    out_ref[...] = (0.25 * spread * slope(pre_ref[...])).astype(BF)


def conv_slope(pre, dfeat):
    pix, chans = pre.shape
    return pl.pallas_call(
        lines_kernel,
        out_shape=jax.ShapeDtypeStruct((pix, chans), BF),
        scratch_shapes=[pltpu.VMEM((chans // LANES, pix // 2, LANES), F32)],
        compiler_params=VMEM,
        cost_estimate=LITTLE,
    )(pre, dfeat)


def fc7_kernel(known_ref, hidden_ref, pick_ref, seven_ref, terms_ref):
    count, mine, wide = hidden_ref.shape
    lines, both, _ = known_ref.shape
    rows7, cols7 = count * wide, both // 2

    def weight(k, start, size):
        block = known_ref[:, k * cols7 : (k + 1) * cols7, start : start + size]
        return block.reshape(lines * cols7, size)

    sevens = []
    for k in range(2):
        y7_pre = jnp.zeros((lines * cols7, mine), F32)
        for g in range(count):
            y7_pre += dot(weight(k, g * wide, wide), hidden_ref[g], ((1,), (1,)))
        cot = dot(weight(k, rows7, pick_ref.shape[0]), pick_ref[...], ((1,), (0,)))
        sevens.append((cot * slope(y7_pre)).astype(BF))
        seven_ref[:, k * mine : (k + 1) * mine] = sevens[k]
    for g in range(count):
        parts = [dot(sevens[k], weight(k, g * wide, wide), ((0,), (0,))) for k in range(2)]
        terms_ref[g] = (parts[0] + parts[1]).astype(BF)


def fc7_step(known, hidden, pick):
    lines, both, _ = known.shape
    return pl.pallas_call(
        fc7_kernel,
        out_shape=[
            jax.ShapeDtypeStruct((lines * both // 2, 2 * pick.shape[1]), BF),
            jax.ShapeDtypeStruct(hidden.shape, BF),
        ],
        compiler_params=VMEM,
        cost_estimate=cost(4 * known.size * pick.shape[1], known.size * 2),
    )(known, hidden, pick)


def back_kernel(g_ref, weight_ref, out_ref):
    out_ref[...] = dot(g_ref[...], weight_ref[...], ((1,), (1,))).astype(BF)


def features_back(g_six, weight):
    count, feats = g_six.shape[0], weight.shape[0]
    return pl.pallas_call(
        back_kernel,
        out_shape=jax.ShapeDtypeStruct((count, feats), BF),
        compiler_params=VMEM,
        cost_estimate=cost(2 * count * weight.size, weight.size * 2),
    )(g_six, weight)


def outer_kernel(which_ref, inputs_ref, g_ref, out_ref):
    units = out_ref.shape[1]
    g_six = g_ref[:, pl.ds(pl.multiple_of(which_ref[0] * units, units), units)]
    out_ref[...] = dot(inputs_ref[...], g_six, ((0,), (0,))).astype(out_ref.dtype)


def outer_add_kernel(which_ref, inputs_ref, g_ref, more_ref, out_ref):
    units = out_ref.shape[1]
    g_six = g_ref[:, pl.ds(pl.multiple_of(which_ref[0] * units, units), units)]
    out_ref[...] = dot(inputs_ref[...], g_six, ((0,), (0,))) + more_ref[...].astype(F32)


def weight_terms(which, inputs, g_six, units, more=None):
    feats = inputs.shape[1]
    operands = (inputs, g_six) if more is None else (inputs, g_six, more)
    in_vmem = [pl.BlockSpec(memory_space=pltpu.VMEM)] * len(operands)
    return pl.pallas_call(
        outer_kernel if more is None else outer_add_kernel,
        in_specs=[pl.BlockSpec(memory_space=pltpu.SMEM)] + in_vmem,
        out_shape=jax.ShapeDtypeStruct((feats, units), BF if more is None else F32),
        compiler_params=VMEM,
        cost_estimate=LITTLE,
    )(which.reshape(1).astype(jnp.int32), *operands)


def pack_kernel(me_ref, terms_ref, slope_ref, out_ref, parts_ref, own_ref):
    nx, rows, _ = out_ref.shape
    feats = terms_ref.shape[2]
    run = LANES // 2
    runs = feats // run
    total = terms_ref[...].astype(F32).sum(axis=0).astype(BF).astype(F32)
    total = jnp.concatenate([total, jnp.zeros((nx, -feats % LANES), F32)], axis=1)
    parts_ref[...] = jnp.zeros(parts_ref.shape, F32)
    own_ref[...] = jnp.zeros(own_ref.shape, F32)
    for t in range(runs):
        tile = total[:, t // 2 * LANES : (t // 2 + 1) * LANES]
        other = pltpu.roll(tile, run, 1)
        low, high = (tile, other) if t % 2 == 0 else (other, tile)
        parts_ref[t % nx, t // nx * nx : (t // nx + 1) * nx, :] = low
        own_ref[pl.ds(t, nx, rows), :] = high
    lane = lax.broadcasted_iota(jnp.int32, (rows, LANES), 1)
    for e in range(nx):
        dest = lax.rem(me_ref[0] + e, nx)
        own = own_ref[pl.ds(pl.multiple_of(dest * rows, rows), rows), :]
        out_ref[dest, :, :LANES] = jnp.where(lane < run, parts_ref[e], own).astype(BF)
    out_ref[:, :, LANES:] = slope_ref[...]


def pack_dfeat(me, terms, slopes):
    _, nx, feats = terms.shape
    rows = nx * nx
    return pl.pallas_call(
        pack_kernel,
        in_specs=[
            pl.BlockSpec(memory_space=pltpu.SMEM),
            pl.BlockSpec(memory_space=pltpu.VMEM),
            pl.BlockSpec(memory_space=pltpu.VMEM),
        ],
        out_shape=jax.ShapeDtypeStruct((nx, rows, LANES + slopes.shape[2]), BF),
        scratch_shapes=[
            pltpu.VMEM((nx, rows, LANES), F32),
            pltpu.VMEM((nx * rows, LANES), F32),
        ],
        compiler_params=VMEM,
        cost_estimate=cost(4 * terms.size, terms.size * 2),
    )(me, terms, slopes)


def kernel_kernel(place_ref, lines_ref, packs_ref, spread_ref, own_ref, sent_ref, grad_ref, flat_ref, wide_ref):
    images, part, _ = packs_ref.shape
    cols = spread_ref.shape[1]
    chans = lines_ref.shape[2]
    wide_ref[...] = packs_ref[:, :, :LANES].astype(F32).reshape(wide_ref.shape)
    for k in range(images):
        n = lax.rem(place_ref[0] + k % 2, 2) * (images // 2) + k // 2
        cells = wide_ref[pl.ds(n, wide_ref.shape[0] // images, images), :].astype(BF)
        spread = dot(cells, spread_ref[...], ((0,), (0,)))[:part]
        turned = (spread * packs_ref[n, :, LANES:].astype(F32)).astype(BF).astype(F32)
        moved = [turned] + [pltpu.roll(turned, j, 1) for j in (1, 2)]
        grad_ref[:, k * cols : (k + 1) * cols] = jnp.concatenate(moved, axis=0).astype(BF)
    for row in range(3):
        block = lines_ref[:, row * LINE : row * LINE + cols, :].reshape(images * cols, chans)
        term = dot(grad_ref[...], block, ((1,), (0,)))
        for col in range(3):
            tap = 3 * row + col
            flat_ref[tap * chans : (tap + 1) * chans, :] = term[col * part : (col + 1) * part].T
    count, size, _ = own_ref.shape
    for core, out_ref in ((place_ref[1], own_ref), (1 - place_ref[1], sent_ref)):
        for dest in range(count):
            at = pl.multiple_of((2 * dest + core) * (2 * size), 2 * size)
            both = [flat_ref[pl.ds(at + k * size, size), :] for k in range(2)]
            out_ref[dest] = jnp.concatenate(both, axis=1).astype(out_ref.dtype)


def conv_kernel_grad(place, lines, packs, spread, count):
    images, _, chans = lines.shape
    _, part, _ = packs.shape
    cols = spread.shape[1]
    size = 9 * chans // (4 * count)
    return pl.pallas_call(
        kernel_kernel,
        in_specs=[pl.BlockSpec(memory_space=pltpu.SMEM)] + [pl.BlockSpec(memory_space=pltpu.VMEM)] * 3,
        out_shape=[jax.ShapeDtypeStruct((count, size, 2 * part), kind) for kind in (F32, BF)],
        scratch_shapes=[
            pltpu.VMEM((3 * part, images * cols), BF),
            pltpu.VMEM((9 * chans, part), F32),
            pltpu.VMEM((images * part, LANES), F32),
        ],
        compiler_params=VMEM,
        cost_estimate=cost(18 * images * cols * chans * part, lines.size * 2),
    )(place, lines, packs, spread)


def backward_kernel(lines_ref, weight_ref, out_ref, sums_ref):
    step = pl.program_id(0)
    col = lax.rem(step, 3)
    rows = sums_ref.shape[1]
    start = pl.multiple_of((2 - step // 3) * LINE, LINE)
    part = dot(lines_ref[pl.ds(start, rows), :], weight_ref[...], ((1,), (1,)))

    @pl.when(step < 3)
    def _():
        sums_ref[col] = part

    @pl.when(step >= 3)
    def _():
        sums_ref[col] += part

    @pl.when(step == 8)
    def _():
        _, side, _, chans = out_ref.shape
        pix = side * LINE
        grad = sums_ref[0, 2 : pix + 2, :] + sums_ref[1, 1 : pix + 1, :] + sums_ref[2, 0:pix, :]
        out_ref[0] = grad.reshape(side, LINE, chans)[:, :side, :]


def conv_backward(lines, weight, side):
    chans = lines.shape[1]
    depth = weight.shape[0] // 9
    pix = side * LINE
    return pl.pallas_call(
        backward_kernel,
        grid=(9,),
        in_specs=[
            pl.BlockSpec(lines.shape, lambda t: (0, 0)),
            pl.BlockSpec((depth, chans), lambda t: (t, 0)),
        ],
        out_specs=pl.BlockSpec((1, side, side, depth), lambda t: (0, 0, 0, 0)),
        out_shape=jax.ShapeDtypeStruct((1, side, side, depth), F32),
        scratch_shapes=[pltpu.VMEM((3, pix + LINE, depth), F32)],
        compiler_params=VMEM,
        cost_estimate=LITTLE,
    )(lines, weight)


def spread_matrix(me, nx, half, cols):
    at = lax.broadcasted_iota(jnp.int32, (nx * nx, cols), 0)
    pixel = lax.broadcasted_iota(jnp.int32, (nx * nx, cols), 1)
    source, run = at // nx, at % nx
    line, place = pixel // LINE, pixel % LINE
    per = half * half // nx
    cell = jnp.where((line < 2 * half) & (place < 2 * half), line // 2 * half + place // 2, -1)
    mine = per * source + run + (me < source).astype(jnp.int32)
    return ((cell == mine) & (run <= per)).astype(BF)


def swap(value, axis):
    return lax.all_to_all(value, axis, 0, 0, tiled=True)


def share(value, axis, count):
    return swap(jnp.broadcast_to(value, (count,) + value.shape), axis)


def bordered(maps):
    side, _, chans = maps.shape
    padded = jnp.pad(maps, ((1, 3), (1, LINE - side - 1), (0, 0)))
    return padded.reshape((side + 4) * LINE, chans)


def make(nh, nv, nz, nc):
    nx, ny = nh * nv, nz * nc
    gx = ("xh", "y")
    near = nz // nx
    gy = ("gz", "core")
    across = [(k, nh - 1 - k) for k in range(nh)]

    def paired(value, axis, way):
        return jnp.concatenate([value, lax.ppermute(value, axis, way)], axis=0)
    pair = [(k, nc - 1 - k) for k in range(nc)]

    def on_device(images, conv_weight, fc6_weight, fc7_weight, cotangent):
        side, chans = images.shape[1], images.shape[3]
        half = side // 2
        feats, units = fc6_weight.shape
        rows7, cols7 = fc7_weight.shape
        total = cotangent.shape[0]
        group = total // nc
        mine = group // nx
        wide = units * nc
        part = chans // nx
        cols = 2 * LANES
        high, core = lax.axis_index("xh"), lax.axis_index("core")
        me = high * nv + lax.axis_index("y")
        me_word = me.reshape(1).astype(jnp.int32)

        known = jnp.concatenate([fc7_weight.T, cotangent.T], axis=1)
        known = lax.all_gather(known, gx + ("core",), axis=0, tiled=False)
        known = known.reshape(nx, nc * cols7, rows7 + total)
        other6 = lax.ppermute(fc6_weight, "core", pair)
        lines = bordered(images[0])
        conv_pre, feat = conv_forward(lines, conv_weight, side, nx)
        slopes = turned_slope(conv_pre, cols).reshape(nx, part, cols)
        other6, image = lax.optimization_barrier((other6, images))
        gathered = lax.all_gather(paired(image, "xh", across), "y", axis=0, tiled=True)
        inputs = swap(feature_copies(swap(feat, gx), nz, feats), "gz").reshape(group, feats)
        first = jnp.where(core == 0, fc6_weight, other6)
        second = jnp.where(core == 0, other6, fc6_weight)
        weight6 = jnp.concatenate([first, second], axis=1)
        inputs, weight6 = lax.optimization_barrier((inputs, weight6))

        h6_terms = dot(inputs, weight6, ((1,), (0,))).astype(BF).reshape(nx, mine, wide)
        h6_pre = swap(h6_terms, gx).astype(F32).sum(axis=0)
        own_hidden = activate(h6_pre).astype(BF)
        hidden = share(own_hidden, "gz", nz)

        place = lax.broadcasted_iota(jnp.int32, (total, mine), 1)
        source = (place % nx) * ny + (me * near + place // nx) * nc + core
        pick = (lax.broadcasted_iota(jnp.int32, (total, mine), 0) == source).astype(BF)
        g_seven, dh6_terms = fc7_step(known, hidden, pick)
        dh6_terms, hidden = lax.optimization_barrier((dh6_terms, hidden))
        hidden = hidden.transpose(1, 0, 2).reshape(mine, rows7)
        hidden = paired(hidden, "xh", across)
        dh6_terms, hidden = lax.optimization_barrier((swap(dh6_terms, "gz"), hidden))
        all_hidden = lax.all_gather(hidden, "y", axis=0, tiled=False).reshape(group, rows7)
        grad_hidden = dh6_terms.astype(F32).sum(axis=0)
        own_six = (grad_hidden * slope(h6_pre)).astype(BF)

        columns = g_seven.reshape(nx, cols7, nc * mine)
        columns = jnp.pad(columns, ((0, 0), (0, mine - cols7), (0, LANES - nc * mine)))
        both = jnp.concatenate([jnp.broadcast_to(own_six, (nx, mine, wide)), columns], axis=2)
        both, gathered = lax.optimization_barrier((swap(both, gx), gathered))
        g_six = both[:, :, :wide].reshape(group, wide)
        columns = both[:, :cols7, wide : wide + nc * mine]

        feat_terms = features_back(g_six, weight6).reshape(nz, nx, feats)
        feat_terms, g_six = lax.optimization_barrier((feat_terms, g_six))
        feat_terms, all_hidden = lax.optimization_barrier((swap(feat_terms, "gz"), all_hidden))
        sent6 = weight_terms(nc - 1 - core, inputs, g_six, units)
        packs = swap(pack_dfeat(me_word, feat_terms, slopes), gx)
        gathered, sent6 = lax.optimization_barrier((gathered, sent6))
        all_lines = jax.vmap(bordered)(gathered)
        grad_fc6 = weight_terms(core, inputs, g_six, units, lax.ppermute(sent6, "core", pair))
        spread = spread_matrix(me, nx, half, cols)
        place = jnp.stack([high, core]).astype(jnp.int32)
        packed, sent = conv_kernel_grad(place, all_lines, packs, spread, nz)
        packed = (packed + lax.ppermute(sent, "core", pair).astype(F32)).astype(BF)
        columns = columns.reshape(nh, nv, cols7, nc * mine)
        columns = jnp.where(high == 0, columns, columns[::-1])
        columns = columns.reshape(nh, nv, cols7, nc, mine).transpose(3, 2, 1, 0, 4)
        columns = columns.reshape(nc * cols7, group)
        terms7 = dot(columns, all_hidden, ((1,), (0,)))
        own7 = jnp.where(core == 0, terms7[:cols7], terms7[cols7:])
        sent7 = jnp.where(core == 0, terms7[cols7:], terms7[:cols7])
        packed = swap(packed, "gz")

        runs = feats // part
        dfeat = packs[:, :runs, part : 2 * part].reshape(half, half, chans).astype(F32)
        dfeat = jnp.pad(dfeat, ((0, 0), (0, 1), (0, 0))).reshape(half * (half + 1), chans)
        g_lines = conv_slope(conv_pre, dfeat).reshape(side, LINE, chans)[:, :side]
        grad_images = conv_backward(bordered(g_lines), conv_weight, side)

        grad_fc7 = (own7 + lax.ppermute(sent7, "core", pair)).T
        packed, grad_fc7 = lax.optimization_barrier((packed, grad_fc7))
        packed = packed.astype(F32).sum(axis=0)
        grad_conv = jnp.concatenate([packed[:, :part], packed[:, part:]], axis=0)
        return (grad_conv, grad_fc6, grad_fc7, grad_images)

    return on_device


def solution(mesh):
    nx, ny = mesh.shape["gx"], mesh.shape["gy"]
    nh = nc = 2
    nv, nz = nx // nh, ny // nc
    fine = Mesh(mesh.devices.reshape(nh, nv, nz, nc), ("xh", "y", "gz", "core"))
    gx, gy = ("xh", "y"), ("gz", "core")
    both = gx + gy
    return jax.shard_map(
        make(nh, nv, nz, nc),
        mesh=fine,
        in_specs=(P(both, None, None, None), P(), P(gx, gy), P(None, both), P(None, both)),
        out_specs=(P(gy, gx), P(gx, gy), P(None, both), P(both, None, None, None)),
        check_vma=False,
    )
```

```python
import jax
import jax.numpy as jnp
from jax import lax
from jax.experimental import pallas as pl
from jax.experimental.pallas import tpu as pltpu
from jax.sharding import Mesh, PartitionSpec as P

BF = jnp.bfloat16
F32 = jnp.float32
LANES = 128
LINE = 16
VMEM = pltpu.CompilerParams(vmem_limit_bytes=20 * 2**20)


def activate(value):
    return value * jax.nn.sigmoid(value)


def slope(value):
    sig = jax.nn.sigmoid(value)
    return sig * (1.0 + value * (1.0 - sig))


def dot(a, b, dims):
    return lax.dot_general(a, b, (dims, ((), ())), preferred_element_type=F32)


LITTLE = pl.CostEstimate(flops=1000, bytes_accessed=1000, transcendentals=0)


def cost(flops, moved, special=0):
    return pl.CostEstimate(flops=flops, bytes_accessed=moved, transcendentals=special)


def forward_kernel(
    maps_ref, weight_ref, pre_ref, feat_ref, held_ref, lines_ref, sums_ref, pool_ref, runs_ref, sems
):
    pix, chans = pre_ref.shape
    _, height, width, depth = maps_ref.shape
    rows = sums_ref.shape[1]

    def load(tap):
        return pltpu.make_async_copy(
            weight_ref.at[pl.ds(tap * depth, depth), :],
            held_ref.at[tap % 3, pl.ds(tap // 3 * depth, depth), :],
            sems.at[tap],
        )

    order = [3 * row + col for col in range(3) for row in range(3)]
    for tap in order:
        load(tap).start()
    lines_ref[...] = jnp.zeros(lines_ref.shape, F32)
    for k in range(height):
        at = (k + 1) * LINE + 1
        lines_ref[at : at + width, :] = maps_ref[0, k].astype(F32)
    image = [lines_ref[k * LINE : k * LINE + rows, :].astype(BF) for k in range(3)]
    image = jnp.concatenate(image, axis=1)
    for col in range(3):
        for row in range(3):
            load(3 * row + col).wait()
        sums_ref[col] = dot(image, held_ref[col], ((1,), (0,)))
    pre = sums_ref[0, 0:pix, :] + sums_ref[1, 1 : pix + 1, :] + sums_ref[2, 2 : pix + 2, :]
    pre_ref[...] = pre
    act = activate(pre).reshape(pix // (2 * LINE), 2, LINE, chans)
    lines = (act[:, 0] + act[:, 1]).reshape(pix // 2, chans)
    half = pix // 4
    side = pix // LINE // 2
    run = LANES // 2
    dests, rows, across = feat_ref.shape
    runs = side * side * chans // (dests * run)
    runs_ref[...] = jnp.zeros(runs_ref.shape, F32)
    for k in range(chans // LANES):
        pool_ref[k] = lines[:, k * LANES : (k + 1) * LANES]
        total = 0.25 * (pool_ref[k, pl.ds(0, half, 2), :] + pool_ref[k, pl.ds(1, half, 2), :])
        other = pltpu.roll(total, run, 1)
        for cell in range(side * side):
            line = cell // side * (LINE // 2) + cell % side
            for part in range(2):
                dest, t = divmod(cell * (chans // run) + 2 * k + part, runs)
                at = t % 2 * run
                piece = total if t % 2 == part else other
                row, lane = divmod(t * run, across)
                row = dest * rows + row
                runs_ref[row : row + 1, lane : lane + run] = piece[line : line + 1, at : at + run]
    feat_ref[...] = runs_ref[...].astype(BF).reshape(dests, rows, across)


def conv_forward(maps, weight, nx):
    _, side, _, depth = maps.shape
    chans = weight.shape[1]
    pix = side * LINE
    rows, width = LINE, 2 * LANES
    return pl.pallas_call(
        forward_kernel,
        in_specs=[
            pl.BlockSpec(memory_space=pltpu.VMEM),
            pl.BlockSpec(memory_space=pl.ANY),
        ],
        out_shape=[
            jax.ShapeDtypeStruct((pix, chans), F32),
            jax.ShapeDtypeStruct((nx, rows, width), BF),
        ],
        scratch_shapes=[
            pltpu.VMEM((3, 3 * depth, chans), BF),
            pltpu.VMEM((pix + 3 * LINE, depth), F32),
            pltpu.VMEM((3, pix + LINE, chans), F32),
            pltpu.VMEM((chans // LANES, pix // 2, LANES), F32),
            pltpu.VMEM((nx * rows, width), F32),
            pltpu.SemaphoreType.DMA((9,)),
        ],
        compiler_params=VMEM,
        cost_estimate=cost(18 * pix * depth * chans, weight.size * 2, pix * chans),
    )(maps, weight)


def join_kernel(left_ref, right_ref, out_ref):
    cut = left_ref.shape[1]
    out_ref[:, :cut] = left_ref[...]
    out_ref[:, cut:] = right_ref[...]


def join(left, right):
    rows, cut = left.shape
    return pl.pallas_call(
        join_kernel,
        out_shape=jax.ShapeDtypeStruct((rows, cut + right.shape[1]), left.dtype),
        cost_estimate=cost(0, left.size * 4),
    )(left, right)


def copies_kernel(feat_ref, out_ref):
    feats = out_ref.shape[2]
    _, rows, width = feat_ref.shape
    value = feat_ref[...].astype(F32)
    flat = jnp.concatenate([value[:, k, :] for k in range(rows)], axis=1)[:, :feats].astype(BF)
    for k in range(out_ref.shape[0]):
        out_ref[k] = flat


def feature_copies(feat, count, feats):
    return pl.pallas_call(
        copies_kernel,
        out_shape=jax.ShapeDtypeStruct((count, feat.shape[0], feats), BF),
        compiler_params=VMEM,
        cost_estimate=cost(feat.size, feat.size * 2 * count),
    )(feat)


def turn_kernel(pre_ref, out_ref):
    pix, chans = pre_ref.shape
    grad = 0.25 * slope(pre_ref[...])
    grad = jnp.concatenate([grad, jnp.zeros((out_ref.shape[1] - pix, chans), F32)], axis=0)
    out_ref[...] = grad.T.astype(BF)


def turned_slope(pre, cols):
    pix, chans = pre.shape
    return pl.pallas_call(
        turn_kernel,
        out_shape=jax.ShapeDtypeStruct((chans, cols), BF),
        compiler_params=VMEM,
        cost_estimate=cost(8 * pix * chans, pix * chans * 6, pix * chans),
    )(pre)


def lines_kernel(pre_ref, dfeat_ref, out_ref, wide_ref):
    pix, chans = pre_ref.shape
    half = pix // 4
    for k in range(chans // LANES):
        dfeat = dfeat_ref[:, k * LANES : (k + 1) * LANES]
        wide_ref[k, pl.ds(0, half, 2), :] = dfeat
        wide_ref[k, pl.ds(1, half, 2), :] = dfeat
    spread = jnp.concatenate([wide_ref[k] for k in range(chans // LANES)], axis=1)
    spread = spread.reshape(pix // (2 * LINE), 1, LINE, chans)
    spread = jnp.broadcast_to(spread, (pix // (2 * LINE), 2, LINE, chans)).reshape(pix, chans)
    out_ref[...] = (0.25 * spread * slope(pre_ref[...])).astype(BF)


def conv_slope(pre, dfeat):
    pix, chans = pre.shape
    return pl.pallas_call(
        lines_kernel,
        out_shape=jax.ShapeDtypeStruct((pix, chans), BF),
        scratch_shapes=[pltpu.VMEM((chans // LANES, pix // 2, LANES), F32)],
        compiler_params=VMEM,
        cost_estimate=LITTLE,
    )(pre, dfeat)


def fc7_kernel(known_ref, hidden_ref, pick_ref, seven_ref, terms_ref):
    count, mine, wide = hidden_ref.shape
    lines, both, _ = known_ref.shape
    rows7, cols7 = count * wide, both // 2

    def weight(k, start, size):
        block = known_ref[:, k * cols7 : (k + 1) * cols7, start : start + size]
        return block.reshape(lines * cols7, size)

    sevens = []
    for k in range(2):
        y7_pre = jnp.zeros((lines * cols7, mine), F32)
        for g in range(count):
            y7_pre += dot(weight(k, g * wide, wide), hidden_ref[g], ((1,), (1,)))
        cot = dot(weight(k, rows7, pick_ref.shape[0]), pick_ref[...], ((1,), (0,)))
        sevens.append((cot * slope(y7_pre)).astype(BF))
        seven_ref[:, k * mine : (k + 1) * mine] = sevens[k]
    for g in range(count):
        parts = [dot(sevens[k], weight(k, g * wide, wide), ((0,), (0,))) for k in range(2)]
        terms_ref[g] = (parts[0] + parts[1]).astype(BF)


def fc7_step(known, hidden, pick):
    lines, both, _ = known.shape
    return pl.pallas_call(
        fc7_kernel,
        out_shape=[
            jax.ShapeDtypeStruct((lines * both // 2, 2 * pick.shape[1]), BF),
            jax.ShapeDtypeStruct(hidden.shape, BF),
        ],
        compiler_params=VMEM,
        cost_estimate=cost(4 * known.size * pick.shape[1], known.size * 2),
    )(known, hidden, pick)


def back_kernel(g_ref, weight_ref, out_ref):
    out_ref[...] = dot(g_ref[...], weight_ref[...], ((1,), (1,))).astype(BF)


def features_back(g_six, weight):
    count, feats = g_six.shape[0], weight.shape[0]
    return pl.pallas_call(
        back_kernel,
        out_shape=jax.ShapeDtypeStruct((count, feats), BF),
        compiler_params=VMEM,
        cost_estimate=cost(2 * count * weight.size, weight.size * 2),
    )(g_six, weight)


def outer_kernel(which_ref, inputs_ref, g_ref, out_ref):
    units = out_ref.shape[1]
    g_six = g_ref[:, pl.ds(pl.multiple_of(which_ref[0] * units, units), units)]
    out_ref[...] = dot(inputs_ref[...], g_six, ((0,), (0,))).astype(out_ref.dtype)


def outer_add_kernel(which_ref, inputs_ref, g_ref, more_ref, out_ref):
    units = out_ref.shape[1]
    g_six = g_ref[:, pl.ds(pl.multiple_of(which_ref[0] * units, units), units)]
    out_ref[...] = dot(inputs_ref[...], g_six, ((0,), (0,))) + more_ref[...].astype(F32)


def weight_terms(which, inputs, g_six, units, more=None):
    feats = inputs.shape[1]
    operands = (inputs, g_six) if more is None else (inputs, g_six, more)
    in_vmem = [pl.BlockSpec(memory_space=pltpu.VMEM)] * len(operands)
    return pl.pallas_call(
        outer_kernel if more is None else outer_add_kernel,
        in_specs=[pl.BlockSpec(memory_space=pltpu.SMEM)] + in_vmem,
        out_shape=jax.ShapeDtypeStruct((feats, units), BF if more is None else F32),
        compiler_params=VMEM,
        cost_estimate=LITTLE,
    )(which.reshape(1).astype(jnp.int32), *operands)


def pack_kernel(me_ref, terms_ref, slope_ref, out_ref, parts_ref, own_ref):
    nx, rows, _ = out_ref.shape
    feats = terms_ref.shape[2]
    run = LANES // 2
    runs = feats // run
    total = terms_ref[...].astype(F32).sum(axis=0).astype(BF).astype(F32)
    total = jnp.concatenate([total, jnp.zeros((nx, -feats % LANES), F32)], axis=1)
    parts_ref[...] = jnp.zeros(parts_ref.shape, F32)
    own_ref[...] = jnp.zeros(own_ref.shape, F32)
    for t in range(runs):
        tile = total[:, t // 2 * LANES : (t // 2 + 1) * LANES]
        other = pltpu.roll(tile, run, 1)
        low, high = (tile, other) if t % 2 == 0 else (other, tile)
        parts_ref[t % nx, t // nx * nx : (t // nx + 1) * nx, :] = low
        own_ref[pl.ds(t, nx, rows), :] = high
    lane = lax.broadcasted_iota(jnp.int32, (rows, LANES), 1)
    for e in range(nx):
        dest = lax.rem(me_ref[0] + e, nx)
        own = own_ref[pl.ds(pl.multiple_of(dest * rows, rows), rows), :]
        out_ref[dest, :, :LANES] = jnp.where(lane < run, parts_ref[e], own).astype(BF)
    out_ref[:, :, LANES:] = slope_ref[...]


def pack_dfeat(me, terms, slopes):
    _, nx, feats = terms.shape
    rows = nx * nx
    return pl.pallas_call(
        pack_kernel,
        in_specs=[
            pl.BlockSpec(memory_space=pltpu.SMEM),
            pl.BlockSpec(memory_space=pltpu.VMEM),
            pl.BlockSpec(memory_space=pltpu.VMEM),
        ],
        out_shape=jax.ShapeDtypeStruct((nx, rows, LANES + slopes.shape[2]), BF),
        scratch_shapes=[
            pltpu.VMEM((nx, rows, LANES), F32),
            pltpu.VMEM((nx * rows, LANES), F32),
        ],
        compiler_params=VMEM,
        cost_estimate=cost(4 * terms.size, terms.size * 2),
    )(me, terms, slopes)


def kernel_kernel(place_ref, lines_ref, packs_ref, spread_ref, own_ref, sent_ref, grad_ref, flat_ref, wide_ref):
    images, part, _ = packs_ref.shape
    cols = spread_ref.shape[1]
    chans = lines_ref.shape[2]
    wide_ref[...] = packs_ref[:, :, :LANES].astype(F32).reshape(wide_ref.shape)
    for k in range(images):
        n = lax.rem(place_ref[0] + k % 2, 2) * (images // 2) + k // 2
        cells = wide_ref[pl.ds(n, wide_ref.shape[0] // images, images), :].astype(BF)
        spread = dot(cells, spread_ref[...], ((0,), (0,)))[:part]
        turned = (spread * packs_ref[n, :, LANES:].astype(F32)).astype(BF).astype(F32)
        moved = [turned] + [pltpu.roll(turned, j, 1) for j in (1, 2)]
        grad_ref[:, k * cols : (k + 1) * cols] = jnp.concatenate(moved, axis=0).astype(BF)
    for row in range(3):
        block = lines_ref[:, row * LINE : row * LINE + cols, :].reshape(images * cols, chans)
        term = dot(grad_ref[...], block, ((1,), (0,)))
        for col in range(3):
            tap = 3 * row + col
            flat_ref[tap * chans : (tap + 1) * chans, :] = term[col * part : (col + 1) * part].T
    count, size, _ = own_ref.shape
    for core, out_ref in ((place_ref[1], own_ref), (1 - place_ref[1], sent_ref)):
        for dest in range(count):
            at = pl.multiple_of((2 * dest + core) * (2 * size), 2 * size)
            both = [flat_ref[pl.ds(at + k * size, size), :] for k in range(2)]
            out_ref[dest] = jnp.concatenate(both, axis=1).astype(out_ref.dtype)


def conv_kernel_grad(place, lines, packs, spread, count):
    images, _, chans = lines.shape
    _, part, _ = packs.shape
    cols = spread.shape[1]
    size = 9 * chans // (4 * count)
    return pl.pallas_call(
        kernel_kernel,
        in_specs=[pl.BlockSpec(memory_space=pltpu.SMEM)] + [pl.BlockSpec(memory_space=pltpu.VMEM)] * 3,
        out_shape=[jax.ShapeDtypeStruct((count, size, 2 * part), kind) for kind in (F32, BF)],
        scratch_shapes=[
            pltpu.VMEM((3 * part, images * cols), BF),
            pltpu.VMEM((9 * chans, part), F32),
            pltpu.VMEM((images * part, LANES), F32),
        ],
        compiler_params=VMEM,
        cost_estimate=cost(18 * images * cols * chans * part, lines.size * 2),
    )(place, lines, packs, spread)


def backward_kernel(lines_ref, weight_ref, out_ref, sums_ref):
    step = pl.program_id(0)
    col = lax.rem(step, 3)
    rows = sums_ref.shape[1]
    start = pl.multiple_of((2 - step // 3) * LINE, LINE)
    part = dot(lines_ref[pl.ds(start, rows), :], weight_ref[...], ((1,), (1,)))

    @pl.when(step < 3)
    def _():
        sums_ref[col] = part

    @pl.when(step >= 3)
    def _():
        sums_ref[col] += part

    @pl.when(step == 8)
    def _():
        _, side, _, chans = out_ref.shape
        pix = side * LINE
        grad = sums_ref[0, 2 : pix + 2, :] + sums_ref[1, 1 : pix + 1, :] + sums_ref[2, 0:pix, :]
        out_ref[0] = grad.reshape(side, LINE, chans)[:, :side, :]


def conv_backward(lines, weight, side):
    chans = lines.shape[1]
    depth = weight.shape[0] // 9
    pix = side * LINE
    return pl.pallas_call(
        backward_kernel,
        grid=(9,),
        in_specs=[
            pl.BlockSpec(lines.shape, lambda t: (0, 0)),
            pl.BlockSpec((depth, chans), lambda t: (t, 0)),
        ],
        out_specs=pl.BlockSpec((1, side, side, depth), lambda t: (0, 0, 0, 0)),
        out_shape=jax.ShapeDtypeStruct((1, side, side, depth), F32),
        scratch_shapes=[pltpu.VMEM((3, pix + LINE, depth), F32)],
        compiler_params=VMEM,
        cost_estimate=LITTLE,
    )(lines, weight)


def spread_matrix(me, nx, half, cols):
    at = lax.broadcasted_iota(jnp.int32, (nx * nx, cols), 0)
    pixel = lax.broadcasted_iota(jnp.int32, (nx * nx, cols), 1)
    source, run = at // nx, at % nx
    line, place = pixel // LINE, pixel % LINE
    per = half * half // nx
    cell = jnp.where((line < 2 * half) & (place < 2 * half), line // 2 * half + place // 2, -1)
    mine = per * source + run + (me < source).astype(jnp.int32)
    return ((cell == mine) & (run <= per)).astype(BF)


def swap(value, axis):
    return lax.all_to_all(value, axis, 0, 0, tiled=True)


def share(value, axis, count):
    return swap(jnp.broadcast_to(value, (count,) + value.shape), axis)


def bordered(maps):
    side, _, chans = maps.shape
    padded = jnp.pad(maps, ((1, 3), (1, LINE - side - 1), (0, 0)))
    return padded.reshape((side + 4) * LINE, chans)


def make(nh, nv, nz, nc):
    nx, ny = nh * nv, nz * nc
    gx = ("xh", "y")
    near = nz // nx
    gy = ("gz", "core")
    across = [(k, nh - 1 - k) for k in range(nh)]

    def paired(value, axis, way):
        return jnp.concatenate([value, lax.ppermute(value, axis, way)], axis=0)
    pair = [(k, nc - 1 - k) for k in range(nc)]

    def on_device(images, conv_weight, fc6_weight, fc7_weight, cotangent):
        side, chans = images.shape[1], images.shape[3]
        half = side // 2
        feats, units = fc6_weight.shape
        rows7, cols7 = fc7_weight.shape
        total = cotangent.shape[0]
        group = total // nc
        mine = group // nx
        wide = units * nc
        part = chans // nx
        cols = 2 * LANES
        high, core = lax.axis_index("xh"), lax.axis_index("core")
        me = high * nv + lax.axis_index("y")
        me_word = me.reshape(1).astype(jnp.int32)

        known = join(fc7_weight.T, cotangent.T)
        known = lax.all_gather(known, gx + ("core",), axis=0, tiled=False)
        known = known.reshape(nx, nc * cols7, rows7 + total)
        other6 = lax.ppermute(fc6_weight, "core", pair)
        conv_pre, feat = conv_forward(images, conv_weight, nx)
        slopes = turned_slope(conv_pre, cols).reshape(nx, part, cols)
        feat, other6 = lax.optimization_barrier((swap(feat, gx), other6))
        other6, image = lax.optimization_barrier((other6, images))
        gathered = lax.all_gather(paired(image, "xh", across), "y", axis=0, tiled=True)
        inputs = swap(feature_copies(feat, nz, feats), "gz").reshape(group, feats)
        first = jnp.where(core == 0, fc6_weight, other6)
        second = jnp.where(core == 0, other6, fc6_weight)
        weight6 = jnp.concatenate([first, second], axis=1)
        inputs, weight6 = lax.optimization_barrier((inputs, weight6))

        h6_terms = dot(inputs, weight6, ((1,), (0,))).astype(BF).reshape(nx, mine, wide)
        h6_pre = swap(h6_terms, gx).astype(F32).sum(axis=0)
        own_hidden = activate(h6_pre).astype(BF)
        hidden = share(own_hidden, "gz", nz)

        place = lax.broadcasted_iota(jnp.int32, (total, mine), 1)
        source = (place % nx) * ny + (me * near + place // nx) * nc + core
        pick = (lax.broadcasted_iota(jnp.int32, (total, mine), 0) == source).astype(BF)
        g_seven, dh6_terms = fc7_step(known, hidden, pick)
        dh6_terms, hidden = lax.optimization_barrier((dh6_terms, hidden))
        hidden = hidden.transpose(1, 0, 2).reshape(mine, rows7)
        hidden = paired(hidden, "xh", across)
        dh6_terms, hidden = lax.optimization_barrier((swap(dh6_terms, "gz"), hidden))
        all_hidden = lax.all_gather(hidden, "y", axis=0, tiled=False).reshape(group, rows7)
        grad_hidden = dh6_terms.astype(F32).sum(axis=0)
        own_six = (grad_hidden * slope(h6_pre)).astype(BF)

        columns = g_seven.reshape(nx, cols7, nc * mine)
        columns = jnp.pad(columns, ((0, 0), (0, mine - cols7), (0, LANES - nc * mine)))
        both = jnp.concatenate([jnp.broadcast_to(own_six, (nx, mine, wide)), columns], axis=2)
        both, gathered = lax.optimization_barrier((swap(both, gx), gathered))
        g_six = both[:, :, :wide].reshape(group, wide)
        columns = both[:, :cols7, wide : wide + nc * mine]

        feat_terms = features_back(g_six, weight6).reshape(nz, nx, feats)
        feat_terms, g_six = lax.optimization_barrier((feat_terms, g_six))
        feat_terms, all_hidden = lax.optimization_barrier((swap(feat_terms, "gz"), all_hidden))
        sent6 = weight_terms(nc - 1 - core, inputs, g_six, units)
        packs = swap(pack_dfeat(me_word, feat_terms, slopes), gx)
        gathered, sent6 = lax.optimization_barrier((gathered, sent6))
        all_lines = jax.vmap(bordered)(gathered)
        grad_fc6 = weight_terms(core, inputs, g_six, units, lax.ppermute(sent6, "core", pair))
        spread = spread_matrix(me, nx, half, cols)
        place = jnp.stack([high, core]).astype(jnp.int32)
        packed, sent = conv_kernel_grad(place, all_lines, packs, spread, nz)
        packed = (packed + lax.ppermute(sent, "core", pair).astype(F32)).astype(BF)
        columns = columns.reshape(nh, nv, cols7, nc * mine)
        columns = jnp.where(high == 0, columns, columns[::-1])
        columns = columns.reshape(nh, nv, cols7, nc, mine).transpose(3, 2, 1, 0, 4)
        columns = columns.reshape(nc * cols7, group)
        terms7 = dot(columns, all_hidden, ((1,), (0,)))
        own7 = jnp.where(core == 0, terms7[:cols7], terms7[cols7:])
        sent7 = jnp.where(core == 0, terms7[cols7:], terms7[:cols7])
        packed = swap(packed, "gz")

        runs = feats // part
        dfeat = packs[:, :runs, part : 2 * part].reshape(half, half, chans).astype(F32)
        dfeat = jnp.pad(dfeat, ((0, 0), (0, 1), (0, 0))).reshape(half * (half + 1), chans)
        g_lines = conv_slope(conv_pre, dfeat).reshape(side, LINE, chans)[:, :side]
        grad_images = conv_backward(bordered(g_lines), conv_weight, side)

        grad_fc7 = (own7 + lax.ppermute(sent7, "core", pair)).T
        packed, grad_fc7 = lax.optimization_barrier((packed, grad_fc7))
        packed = packed.astype(F32).sum(axis=0)
        grad_conv = jnp.concatenate([packed[:, :part], packed[:, part:]], axis=0)
        return (grad_conv, grad_fc6, grad_fc7, grad_images)

    return on_device


def solution(mesh):
    nx, ny = mesh.shape["gx"], mesh.shape["gy"]
    nh = nc = 2
    nv, nz = nx // nh, ny // nc
    fine = Mesh(mesh.devices.reshape(nh, nv, nz, nc), ("xh", "y", "gz", "core"))
    gx, gy = ("xh", "y"), ("gz", "core")
    both = gx + gy
    return jax.shard_map(
        make(nh, nv, nz, nc),
        mesh=fine,
        in_specs=(P(both, None, None, None), P(), P(gx, gy), P(None, both), P(None, both)),
        out_specs=(P(gy, gx), P(gx, gy), P(None, both), P(both, None, None, None)),
        check_vma=False,
    )
```

```python
import jax
import jax.numpy as jnp
from jax import lax
from jax.experimental import pallas as pl
from jax.experimental.pallas import tpu as pltpu
from jax.sharding import Mesh, PartitionSpec as P

BF = jnp.bfloat16
F32 = jnp.float32
LANES = 128
LINE = 16
VMEM = pltpu.CompilerParams(vmem_limit_bytes=20 * 2**20)


def activate(value):
    return value * jax.nn.sigmoid(value)


def slope(value):
    sig = jax.nn.sigmoid(value)
    return sig * (1.0 + value * (1.0 - sig))


def dot(a, b, dims):
    return lax.dot_general(a, b, (dims, ((), ())), preferred_element_type=F32)


LITTLE = pl.CostEstimate(flops=1000, bytes_accessed=1000, transcendentals=0)


def cost(flops, moved, special=0):
    return pl.CostEstimate(flops=flops, bytes_accessed=moved, transcendentals=special)


def forward_kernel(
    maps_ref, weight_ref, pre_ref, feat_ref, held_ref, lines_ref, sums_ref, pool_ref, runs_ref, sems
):
    pix, chans = pre_ref.shape
    _, height, width, depth = maps_ref.shape
    rows = sums_ref.shape[1]

    def load(tap):
        return pltpu.make_async_copy(
            weight_ref.at[pl.ds(tap * depth, depth), :],
            held_ref.at[tap % 3, pl.ds(tap // 3 * depth, depth), :],
            sems.at[tap],
        )

    order = [3 * row + col for col in range(3) for row in range(3)]
    for tap in order:
        load(tap).start()
    lines_ref[...] = jnp.zeros(lines_ref.shape, F32)
    for k in range(height):
        at = (k + 1) * LINE + 1
        lines_ref[at : at + width, :] = maps_ref[0, k].astype(F32)
    image = [lines_ref[k * LINE : k * LINE + rows, :].astype(BF) for k in range(3)]
    image = jnp.concatenate(image, axis=1)
    for col in range(3):
        for row in range(3):
            load(3 * row + col).wait()
        sums_ref[col] = dot(image, held_ref[col], ((1,), (0,)))
    pre = sums_ref[0, 0:pix, :] + sums_ref[1, 1 : pix + 1, :] + sums_ref[2, 2 : pix + 2, :]
    pre_ref[...] = pre
    act = activate(pre).reshape(pix // (2 * LINE), 2, LINE, chans)
    lines = (act[:, 0] + act[:, 1]).reshape(pix // 2, chans)
    half = pix // 4
    side = pix // LINE // 2
    run = LANES // 2
    dests, rows, across = feat_ref.shape
    runs = side * side * chans // (dests * run)
    runs_ref[...] = jnp.zeros(runs_ref.shape, F32)
    for k in range(chans // LANES):
        pool_ref[k] = lines[:, k * LANES : (k + 1) * LANES]
        total = 0.25 * (pool_ref[k, pl.ds(0, half, 2), :] + pool_ref[k, pl.ds(1, half, 2), :])
        other = pltpu.roll(total, run, 1)
        for cell in range(side * side):
            line = cell // side * (LINE // 2) + cell % side
            for part in range(2):
                dest, t = divmod(cell * (chans // run) + 2 * k + part, runs)
                at = t % 2 * run
                piece = total if t % 2 == part else other
                row, lane = divmod(t * run, across)
                row = dest * rows + row
                runs_ref[row : row + 1, lane : lane + run] = piece[line : line + 1, at : at + run]
    feat_ref[...] = runs_ref[...].astype(BF).reshape(dests, rows, across)


def conv_forward(maps, weight, nx):
    _, side, _, depth = maps.shape
    chans = weight.shape[1]
    pix = side * LINE
    rows, width = LINE, 2 * LANES
    return pl.pallas_call(
        forward_kernel,
        in_specs=[
            pl.BlockSpec(memory_space=pltpu.VMEM),
            pl.BlockSpec(memory_space=pl.ANY),
        ],
        out_shape=[
            jax.ShapeDtypeStruct((pix, chans), F32),
            jax.ShapeDtypeStruct((nx, rows, width), BF),
        ],
        scratch_shapes=[
            pltpu.VMEM((3, 3 * depth, chans), BF),
            pltpu.VMEM((pix + 3 * LINE, depth), F32),
            pltpu.VMEM((3, pix + LINE, chans), F32),
            pltpu.VMEM((chans // LANES, pix // 2, LANES), F32),
            pltpu.VMEM((nx * rows, width), F32),
            pltpu.SemaphoreType.DMA((9,)),
        ],
        compiler_params=VMEM,
        cost_estimate=cost(18 * pix * depth * chans, weight.size * 2, pix * chans),
    )(maps, weight)


def join_kernel(left_ref, right_ref, out_ref):
    cut = left_ref.shape[1]
    out_ref[:, :cut] = left_ref[...]
    out_ref[:, cut:] = right_ref[...]


def join(left, right):
    rows, cut = left.shape
    return pl.pallas_call(
        join_kernel,
        out_shape=jax.ShapeDtypeStruct((rows, cut + right.shape[1]), left.dtype),
        cost_estimate=cost(0, left.size * 4),
    )(left, right)


def copies_kernel(feat_ref, out_ref):
    feats = out_ref.shape[2]
    _, rows, width = feat_ref.shape
    value = feat_ref[...].astype(F32)
    flat = jnp.concatenate([value[:, k, :] for k in range(rows)], axis=1)[:, :feats].astype(BF)
    for k in range(out_ref.shape[0]):
        out_ref[k] = flat


def feature_copies(feat, count, feats):
    return pl.pallas_call(
        copies_kernel,
        out_shape=jax.ShapeDtypeStruct((count, feat.shape[0], feats), BF),
        compiler_params=VMEM,
        cost_estimate=cost(feat.size, feat.size * 2 * count),
    )(feat)


def turn_kernel(pre_ref, out_ref):
    pix, chans = pre_ref.shape
    grad = 0.25 * slope(pre_ref[...])
    grad = jnp.concatenate([grad, jnp.zeros((out_ref.shape[1] - pix, chans), F32)], axis=0)
    out_ref[...] = grad.T.astype(BF)


def turned_slope(pre, cols):
    pix, chans = pre.shape
    return pl.pallas_call(
        turn_kernel,
        out_shape=jax.ShapeDtypeStruct((chans, cols), BF),
        compiler_params=VMEM,
        cost_estimate=cost(8 * pix * chans, pix * chans * 6, pix * chans),
    )(pre)


def lines_kernel(pre_ref, dfeat_ref, out_ref, wide_ref):
    pix, chans = pre_ref.shape
    half = pix // 4
    for k in range(chans // LANES):
        dfeat = dfeat_ref[:, k * LANES : (k + 1) * LANES]
        wide_ref[k, pl.ds(0, half, 2), :] = dfeat
        wide_ref[k, pl.ds(1, half, 2), :] = dfeat
    spread = jnp.concatenate([wide_ref[k] for k in range(chans // LANES)], axis=1)
    spread = spread.reshape(pix // (2 * LINE), 1, LINE, chans)
    spread = jnp.broadcast_to(spread, (pix // (2 * LINE), 2, LINE, chans)).reshape(pix, chans)
    out_ref[...] = (0.25 * spread * slope(pre_ref[...])).astype(BF)


def conv_slope(pre, dfeat):
    pix, chans = pre.shape
    return pl.pallas_call(
        lines_kernel,
        out_shape=jax.ShapeDtypeStruct((pix, chans), BF),
        scratch_shapes=[pltpu.VMEM((chans // LANES, pix // 2, LANES), F32)],
        compiler_params=VMEM,
        cost_estimate=LITTLE,
    )(pre, dfeat)


def fc7_kernel(near_ref, far_ref, hidden_ref, pick_ref, seven_ref, terms_ref):
    count, mine, wide = hidden_ref.shape
    lines, both, _ = near_ref.shape
    rows7, cols7 = count * wide, both // 2
    cols = lines * cols7

    def weight(ref, k, start, size):
        return ref[:, k * cols7 : (k + 1) * cols7, start : start + size].reshape(cols, size)

    parts = [(ref, h, k) for h, ref in enumerate((near_ref, far_ref)) for k in range(2)]
    sevens = []
    for ref, h, k in parts:
        y7_pre = jnp.zeros((cols, mine), F32)
        for g in range(count):
            y7_pre += dot(weight(ref, k, g * wide, wide), hidden_ref[g], ((1,), (1,)))
        cot = dot(weight(ref, k, rows7, pick_ref.shape[0]), pick_ref[...], ((1,), (0,)))
        sevens.append((cot * slope(y7_pre)).astype(BF))
        seven_ref[h * cols : (h + 1) * cols, k * mine : (k + 1) * mine] = sevens[-1]
    for g in range(count):
        total = jnp.zeros((mine, wide), F32)
        for seven, (ref, _, k) in zip(sevens, parts):
            total += dot(seven, weight(ref, k, g * wide, wide), ((0,), (0,)))
        terms_ref[g] = total.astype(BF)


def fc7_step(near, far, hidden, pick):
    lines, both, _ = near.shape
    return pl.pallas_call(
        fc7_kernel,
        out_shape=[
            jax.ShapeDtypeStruct((lines * both, 2 * pick.shape[1]), BF),
            jax.ShapeDtypeStruct(hidden.shape, BF),
        ],
        compiler_params=VMEM,
        cost_estimate=cost(8 * near.size * pick.shape[1], near.size * 4),
    )(near, far, hidden, pick)


def back_kernel(g_ref, weight_ref, out_ref):
    out_ref[...] = dot(g_ref[...], weight_ref[...], ((1,), (1,))).astype(BF)


def features_back(g_six, weight):
    count, feats = g_six.shape[0], weight.shape[0]
    return pl.pallas_call(
        back_kernel,
        out_shape=jax.ShapeDtypeStruct((count, feats), BF),
        compiler_params=VMEM,
        cost_estimate=cost(2 * count * weight.size, weight.size * 2),
    )(g_six, weight)


def outer_kernel(which_ref, inputs_ref, g_ref, out_ref):
    units = out_ref.shape[1]
    g_six = g_ref[:, pl.ds(pl.multiple_of(which_ref[0] * units, units), units)]
    out_ref[...] = dot(inputs_ref[...], g_six, ((0,), (0,))).astype(out_ref.dtype)


def outer_add_kernel(which_ref, inputs_ref, g_ref, more_ref, out_ref):
    units = out_ref.shape[1]
    g_six = g_ref[:, pl.ds(pl.multiple_of(which_ref[0] * units, units), units)]
    out_ref[...] = dot(inputs_ref[...], g_six, ((0,), (0,))) + more_ref[...].astype(F32)


def weight_terms(which, inputs, g_six, units, more=None):
    feats = inputs.shape[1]
    operands = (inputs, g_six) if more is None else (inputs, g_six, more)
    in_vmem = [pl.BlockSpec(memory_space=pltpu.VMEM)] * len(operands)
    return pl.pallas_call(
        outer_kernel if more is None else outer_add_kernel,
        in_specs=[pl.BlockSpec(memory_space=pltpu.SMEM)] + in_vmem,
        out_shape=jax.ShapeDtypeStruct((feats, units), BF if more is None else F32),
        compiler_params=VMEM,
        cost_estimate=LITTLE,
    )(which.reshape(1).astype(jnp.int32), *operands)


def pack_kernel(me_ref, terms_ref, slope_ref, out_ref, parts_ref, own_ref):
    nx, rows, _ = out_ref.shape
    feats = terms_ref.shape[2]
    run = LANES // 2
    runs = feats // run
    total = terms_ref[...].astype(F32).sum(axis=0).astype(BF).astype(F32)
    total = jnp.concatenate([total, jnp.zeros((nx, -feats % LANES), F32)], axis=1)
    parts_ref[...] = jnp.zeros(parts_ref.shape, F32)
    own_ref[...] = jnp.zeros(own_ref.shape, F32)
    for t in range(runs):
        tile = total[:, t // 2 * LANES : (t // 2 + 1) * LANES]
        other = pltpu.roll(tile, run, 1)
        low, high = (tile, other) if t % 2 == 0 else (other, tile)
        parts_ref[t % nx, t // nx * nx : (t // nx + 1) * nx, :] = low
        own_ref[pl.ds(t, nx, rows), :] = high
    lane = lax.broadcasted_iota(jnp.int32, (rows, LANES), 1)
    for e in range(nx):
        dest = lax.rem(me_ref[0] + e, nx)
        own = own_ref[pl.ds(pl.multiple_of(dest * rows, rows), rows), :]
        out_ref[dest, :, :LANES] = jnp.where(lane < run, parts_ref[e], own).astype(BF)
    out_ref[:, :, LANES:] = slope_ref[...]


def pack_dfeat(me, terms, slopes):
    _, nx, feats = terms.shape
    rows = nx * nx
    return pl.pallas_call(
        pack_kernel,
        in_specs=[
            pl.BlockSpec(memory_space=pltpu.SMEM),
            pl.BlockSpec(memory_space=pltpu.VMEM),
            pl.BlockSpec(memory_space=pltpu.VMEM),
        ],
        out_shape=jax.ShapeDtypeStruct((nx, rows, LANES + slopes.shape[2]), BF),
        scratch_shapes=[
            pltpu.VMEM((nx, rows, LANES), F32),
            pltpu.VMEM((nx * rows, LANES), F32),
        ],
        compiler_params=VMEM,
        cost_estimate=cost(4 * terms.size, terms.size * 2),
    )(me, terms, slopes)


def kernel_kernel(place_ref, lines_ref, packs_ref, spread_ref, own_ref, sent_ref, grad_ref, flat_ref, wide_ref):
    images, part, _ = packs_ref.shape
    cols = spread_ref.shape[1]
    chans = lines_ref.shape[2]
    wide_ref[...] = packs_ref[:, :, :LANES].astype(F32).reshape(wide_ref.shape)
    for k in range(images):
        n = lax.rem(place_ref[0] + k % 2, 2) * (images // 2) + k // 2
        cells = wide_ref[pl.ds(n, wide_ref.shape[0] // images, images), :].astype(BF)
        spread = dot(cells, spread_ref[...], ((0,), (0,)))[:part]
        turned = (spread * packs_ref[n, :, LANES:].astype(F32)).astype(BF).astype(F32)
        moved = [turned] + [pltpu.roll(turned, j, 1) for j in (1, 2)]
        grad_ref[:, k * cols : (k + 1) * cols] = jnp.concatenate(moved, axis=0).astype(BF)
    for row in range(3):
        block = lines_ref[:, row * LINE : row * LINE + cols, :].reshape(images * cols, chans)
        term = dot(grad_ref[...], block, ((1,), (0,)))
        for col in range(3):
            tap = 3 * row + col
            flat_ref[tap * chans : (tap + 1) * chans, :] = term[col * part : (col + 1) * part].T
    count, size, _ = own_ref.shape
    for core, out_ref in ((place_ref[1], own_ref), (1 - place_ref[1], sent_ref)):
        for dest in range(count):
            at = pl.multiple_of((2 * dest + core) * (2 * size), 2 * size)
            both = [flat_ref[pl.ds(at + k * size, size), :] for k in range(2)]
            out_ref[dest] = jnp.concatenate(both, axis=1).astype(out_ref.dtype)


def conv_kernel_grad(place, lines, packs, spread, count):
    images, _, chans = lines.shape
    _, part, _ = packs.shape
    cols = spread.shape[1]
    size = 9 * chans // (4 * count)
    return pl.pallas_call(
        kernel_kernel,
        in_specs=[pl.BlockSpec(memory_space=pltpu.SMEM)] + [pl.BlockSpec(memory_space=pltpu.VMEM)] * 3,
        out_shape=[jax.ShapeDtypeStruct((count, size, 2 * part), kind) for kind in (F32, BF)],
        scratch_shapes=[
            pltpu.VMEM((3 * part, images * cols), BF),
            pltpu.VMEM((9 * chans, part), F32),
            pltpu.VMEM((images * part, LANES), F32),
        ],
        compiler_params=VMEM,
        cost_estimate=cost(18 * images * cols * chans * part, lines.size * 2),
    )(place, lines, packs, spread)


def backward_kernel(lines_ref, weight_ref, out_ref, sums_ref):
    step = pl.program_id(0)
    col = lax.rem(step, 3)
    rows = sums_ref.shape[1]
    start = pl.multiple_of((2 - step // 3) * LINE, LINE)
    part = dot(lines_ref[pl.ds(start, rows), :], weight_ref[...], ((1,), (1,)))

    @pl.when(step < 3)
    def _():
        sums_ref[col] = part

    @pl.when(step >= 3)
    def _():
        sums_ref[col] += part

    @pl.when(step == 8)
    def _():
        _, side, _, chans = out_ref.shape
        pix = side * LINE
        grad = sums_ref[0, 2 : pix + 2, :] + sums_ref[1, 1 : pix + 1, :] + sums_ref[2, 0:pix, :]
        out_ref[0] = grad.reshape(side, LINE, chans)[:, :side, :]


def conv_backward(lines, weight, side):
    chans = lines.shape[1]
    depth = weight.shape[0] // 9
    pix = side * LINE
    return pl.pallas_call(
        backward_kernel,
        grid=(9,),
        in_specs=[
            pl.BlockSpec(lines.shape, lambda t: (0, 0)),
            pl.BlockSpec((depth, chans), lambda t: (t, 0)),
        ],
        out_specs=pl.BlockSpec((1, side, side, depth), lambda t: (0, 0, 0, 0)),
        out_shape=jax.ShapeDtypeStruct((1, side, side, depth), F32),
        scratch_shapes=[pltpu.VMEM((3, pix + LINE, depth), F32)],
        compiler_params=VMEM,
        cost_estimate=LITTLE,
    )(lines, weight)


def spread_matrix(me, nx, half, cols):
    at = lax.broadcasted_iota(jnp.int32, (nx * nx, cols), 0)
    pixel = lax.broadcasted_iota(jnp.int32, (nx * nx, cols), 1)
    source, run = at // nx, at % nx
    line, place = pixel // LINE, pixel % LINE
    per = half * half // nx
    cell = jnp.where((line < 2 * half) & (place < 2 * half), line // 2 * half + place // 2, -1)
    mine = per * source + run + (me < source).astype(jnp.int32)
    return ((cell == mine) & (run <= per)).astype(BF)


def swap(value, axis):
    return lax.all_to_all(value, axis, 0, 0, tiled=True)


def share(value, axis, count):
    return swap(jnp.broadcast_to(value, (count,) + value.shape), axis)


def bordered(maps):
    side, _, chans = maps.shape
    padded = jnp.pad(maps, ((1, 3), (1, LINE - side - 1), (0, 0)))
    return padded.reshape((side + 4) * LINE, chans)


def make(nh, nv, nz, nc):
    nx, ny = nh * nv, nz * nc
    gx = ("xh", "y")
    near = nz // nx
    gy = ("gz", "core")
    across = [(k, nh - 1 - k) for k in range(nh)]

    def paired(value, axis, way):
        return jnp.concatenate([value, lax.ppermute(value, axis, way)], axis=0)
    pair = [(k, nc - 1 - k) for k in range(nc)]

    def on_device(images, conv_weight, fc6_weight, fc7_weight, cotangent):
        side, chans = images.shape[1], images.shape[3]
        half = side // 2
        feats, units = fc6_weight.shape
        rows7, cols7 = fc7_weight.shape
        total = cotangent.shape[0]
        group = total // nc
        mine = group // nx
        wide = units * nc
        part = chans // nx
        cols = 2 * LANES
        high, core = lax.axis_index("xh"), lax.axis_index("core")
        me = high * nv + lax.axis_index("y")
        me_word = me.reshape(1).astype(jnp.int32)

        known = join(fc7_weight.T, cotangent.T)
        known = lax.all_gather(paired(known, "core", pair), "y", axis=0, tiled=False)
        other6 = lax.ppermute(fc6_weight, "core", pair)
        conv_pre, feat = conv_forward(images, conv_weight, nx)
        slopes = turned_slope(conv_pre, cols).reshape(nx, part, cols)
        feat, other6 = lax.optimization_barrier((swap(feat, gx), other6))
        other6, image = lax.optimization_barrier((other6, images))
        gathered = lax.all_gather(paired(image, "xh", across), "y", axis=0, tiled=True)
        inputs = swap(feature_copies(feat, nz, feats), "gz").reshape(group, feats)
        first = jnp.where(core == 0, fc6_weight, other6)
        second = jnp.where(core == 0, other6, fc6_weight)
        weight6 = jnp.concatenate([first, second], axis=1)
        inputs, weight6, known = lax.optimization_barrier((inputs, weight6, known))
        known_far = lax.ppermute(known, "xh", across)

        h6_terms = dot(inputs, weight6, ((1,), (0,))).astype(BF).reshape(nx, mine, wide)
        h6_pre = swap(h6_terms, gx).astype(F32).sum(axis=0)
        own_hidden = activate(h6_pre).astype(BF)
        hidden = share(own_hidden, "gz", nz)

        place = lax.broadcasted_iota(jnp.int32, (total, mine), 1)
        source = (place % nx) * ny + (me * near + place // nx) * nc + core
        pick = (lax.broadcasted_iota(jnp.int32, (total, mine), 0) == source).astype(BF)
        g_seven, dh6_terms = fc7_step(known, known_far, hidden, pick)
        dh6_terms, hidden = lax.optimization_barrier((dh6_terms, hidden))
        hidden = hidden.transpose(1, 0, 2).reshape(mine, rows7)
        hidden = paired(hidden, "xh", across)
        dh6_terms, hidden = lax.optimization_barrier((swap(dh6_terms, "gz"), hidden))
        all_hidden = lax.all_gather(hidden, "y", axis=0, tiled=False).reshape(group, rows7)
        grad_hidden = dh6_terms.astype(F32).sum(axis=0)
        own_six = (grad_hidden * slope(h6_pre)).astype(BF)

        columns = g_seven.reshape(nh, nv, cols7, nc * mine)
        columns = jnp.where(high == 0, columns, columns[::-1]).reshape(nx, cols7, nc * mine)
        columns = jnp.pad(columns, ((0, 0), (0, mine - cols7), (0, LANES - nc * mine)))
        both = jnp.concatenate([jnp.broadcast_to(own_six, (nx, mine, wide)), columns], axis=2)
        both, gathered = lax.optimization_barrier((swap(both, gx), gathered))
        g_six = both[:, :, :wide].reshape(group, wide)
        columns = both[:, :cols7, wide : wide + nc * mine]

        feat_terms = features_back(g_six, weight6).reshape(nz, nx, feats)
        feat_terms, g_six = lax.optimization_barrier((feat_terms, g_six))
        feat_terms, all_hidden = lax.optimization_barrier((swap(feat_terms, "gz"), all_hidden))
        sent6 = weight_terms(nc - 1 - core, inputs, g_six, units)
        packs = swap(pack_dfeat(me_word, feat_terms, slopes), gx)
        gathered, sent6 = lax.optimization_barrier((gathered, sent6))
        all_lines = jax.vmap(bordered)(gathered)
        grad_fc6 = weight_terms(core, inputs, g_six, units, lax.ppermute(sent6, "core", pair))
        spread = spread_matrix(me, nx, half, cols)
        place = jnp.stack([high, core]).astype(jnp.int32)
        packed, sent = conv_kernel_grad(place, all_lines, packs, spread, nz)
        packed = (packed + lax.ppermute(sent, "core", pair).astype(F32)).astype(BF)
        columns = columns.reshape(nh, nv, cols7, nc * mine)
        columns = jnp.where(high == 0, columns, columns[::-1])
        columns = columns.reshape(nh, nv, cols7, nc, mine).transpose(3, 2, 1, 0, 4)
        columns = columns.reshape(nc * cols7, group)
        terms7 = dot(columns, all_hidden, ((1,), (0,)))
        own7, sent7 = terms7[:cols7], terms7[cols7:]
        packed = swap(packed, "gz")

        runs = feats // part
        dfeat = packs[:, :runs, part : 2 * part].reshape(half, half, chans).astype(F32)
        dfeat = jnp.pad(dfeat, ((0, 0), (0, 1), (0, 0))).reshape(half * (half + 1), chans)
        g_lines = conv_slope(conv_pre, dfeat).reshape(side, LINE, chans)[:, :side]
        grad_images = conv_backward(bordered(g_lines), conv_weight, side)

        grad_fc7 = (own7 + lax.ppermute(sent7, "core", pair)).T
        packed, grad_fc7 = lax.optimization_barrier((packed, grad_fc7))
        packed = packed.astype(F32).sum(axis=0)
        grad_conv = jnp.concatenate([packed[:, :part], packed[:, part:]], axis=0)
        return (grad_conv, grad_fc6, grad_fc7, grad_images)

    return on_device


def solution(mesh):
    nx, ny = mesh.shape["gx"], mesh.shape["gy"]
    nh = nc = 2
    nv, nz = nx // nh, ny // nc
    fine = Mesh(mesh.devices.reshape(nh, nv, nz, nc), ("xh", "y", "gz", "core"))
    gx, gy = ("xh", "y"), ("gz", "core")
    both = gx + gy
    return jax.shard_map(
        make(nh, nv, nz, nc),
        mesh=fine,
        in_specs=(P(both, None, None, None), P(), P(gx, gy), P(None, both), P(None, both)),
        out_specs=(P(gy, gx), P(gx, gy), P(None, both), P(both, None, None, None)),
        check_vma=False,
    )
```

```python
import jax
import jax.numpy as jnp
from jax import lax
from jax.experimental import pallas as pl
from jax.experimental.pallas import tpu as pltpu
from jax.sharding import Mesh, PartitionSpec as P

BF = jnp.bfloat16
F32 = jnp.float32
LANES = 128
LINE = 16
VMEM = pltpu.CompilerParams(vmem_limit_bytes=20 * 2**20)
WHOLE = pltpu.CompilerParams(vmem_limit_bytes=57 * 2**20)


def activate(value):
    return value * jax.nn.sigmoid(value)


def slope(value):
    sig = jax.nn.sigmoid(value)
    return sig * (1.0 + value * (1.0 - sig))


def dot(a, b, dims):
    return lax.dot_general(a, b, (dims, ((), ())), preferred_element_type=F32)


LITTLE = pl.CostEstimate(flops=1000, bytes_accessed=1000, transcendentals=0)


def cost(flops, moved, special=0):
    return pl.CostEstimate(flops=flops, bytes_accessed=moved, transcendentals=special)


def forward_kernel(
    image_ref, weight_ref, pre_ref, feat_ref, held_ref, maps_ref, lines_ref, sums_ref, pool_ref, runs_ref, sems
):
    pix, chans = pre_ref.shape
    _, height, width, depth = maps_ref.shape
    rows = sums_ref.shape[1]

    def load(tap):
        return pltpu.make_async_copy(
            weight_ref.at[pl.ds(tap * depth, depth), :],
            held_ref.at[tap % 3, pl.ds(tap // 3 * depth, depth), :],
            sems.at[tap],
        )

    order = [3 * row + col for col in range(3) for row in range(3)]
    fetch = pltpu.make_async_copy(image_ref, maps_ref, sems.at[9])
    fetch.start()
    for tap in order:
        load(tap).start()
    lines_ref[...] = jnp.zeros(lines_ref.shape, F32)
    fetch.wait()
    for k in range(height):
        at = (k + 1) * LINE + 1
        lines_ref[at : at + width, :] = maps_ref[0, k].astype(F32)
    image = [lines_ref[k * LINE : k * LINE + rows, :].astype(BF) for k in range(3)]
    image = jnp.concatenate(image, axis=1)
    for col in range(3):
        for row in range(3):
            load(3 * row + col).wait()
        sums_ref[col] = dot(image, held_ref[col], ((1,), (0,)))
    pre = sums_ref[0, 0:pix, :] + sums_ref[1, 1 : pix + 1, :] + sums_ref[2, 2 : pix + 2, :]
    pre_ref[...] = pre
    act = activate(pre).reshape(pix // (2 * LINE), 2, LINE, chans)
    lines = (act[:, 0] + act[:, 1]).reshape(pix // 2, chans)
    half = pix // 4
    side = pix // LINE // 2
    run = LANES // 2
    dests, rows, across = feat_ref.shape
    runs = side * side * chans // (dests * run)
    runs_ref[...] = jnp.zeros(runs_ref.shape, F32)
    for k in range(chans // LANES):
        pool_ref[k] = lines[:, k * LANES : (k + 1) * LANES]
        total = 0.25 * (pool_ref[k, pl.ds(0, half, 2), :] + pool_ref[k, pl.ds(1, half, 2), :])
        other = pltpu.roll(total, run, 1)
        for cell in range(side * side):
            line = cell // side * (LINE // 2) + cell % side
            for part in range(2):
                dest, t = divmod(cell * (chans // run) + 2 * k + part, runs)
                at = t % 2 * run
                piece = total if t % 2 == part else other
                row, lane = divmod(t * run, across)
                row = dest * rows + row
                runs_ref[row : row + 1, lane : lane + run] = piece[line : line + 1, at : at + run]
    feat_ref[...] = runs_ref[...].astype(BF).reshape(dests, rows, across)


def conv_forward(maps, weight, nx):
    _, side, _, depth = maps.shape
    chans = weight.shape[1]
    pix = side * LINE
    rows, width = LINE, 2 * LANES
    return pl.pallas_call(
        forward_kernel,
        in_specs=[
            pl.BlockSpec(memory_space=pl.ANY),
            pl.BlockSpec(memory_space=pl.ANY),
        ],
        out_shape=[
            jax.ShapeDtypeStruct((pix, chans), F32),
            jax.ShapeDtypeStruct((nx, rows, width), BF),
        ],
        scratch_shapes=[
            pltpu.VMEM((3, 3 * depth, chans), BF),
            pltpu.VMEM(maps.shape, BF),
            pltpu.VMEM((pix + 3 * LINE, depth), F32),
            pltpu.VMEM((3, pix + LINE, chans), F32),
            pltpu.VMEM((chans // LANES, pix // 2, LANES), F32),
            pltpu.VMEM((nx * rows, width), F32),
            pltpu.SemaphoreType.DMA((10,)),
        ],
        compiler_params=WHOLE,
        cost_estimate=cost(18 * pix * depth * chans, weight.size * 2, pix * chans),
    )(maps, weight)


def join_kernel(left_ref, right_ref, out_ref, sems):
    cut, more = left_ref.shape[1], right_ref.shape[1]
    copies = [
        pltpu.make_async_copy(left_ref, out_ref.at[:, pl.ds(0, cut)], sems.at[0]),
        pltpu.make_async_copy(right_ref, out_ref.at[:, pl.ds(cut, more)], sems.at[1]),
    ]
    for copy in copies:
        copy.start()
    for copy in copies:
        copy.wait()


def join(left, right):
    rows, cut = left.shape
    return pl.pallas_call(
        join_kernel,
        in_specs=[pl.BlockSpec(memory_space=pl.ANY)] * 2,
        out_specs=pl.BlockSpec(memory_space=pl.ANY),
        scratch_shapes=[pltpu.SemaphoreType.DMA((2,))],
        out_shape=jax.ShapeDtypeStruct((rows, cut + right.shape[1]), left.dtype),
        cost_estimate=cost(0, left.size * 4),
    )(left, right)


def copies_kernel(feat_ref, out_ref):
    feats = out_ref.shape[2]
    _, rows, width = feat_ref.shape
    value = feat_ref[...].astype(F32)
    flat = jnp.concatenate([value[:, k, :] for k in range(rows)], axis=1)[:, :feats].astype(BF)
    for k in range(out_ref.shape[0]):
        out_ref[k] = flat


def feature_copies(feat, count, feats):
    return pl.pallas_call(
        copies_kernel,
        out_shape=jax.ShapeDtypeStruct((count, feat.shape[0], feats), BF),
        compiler_params=VMEM,
        cost_estimate=cost(feat.size, feat.size * 2 * count),
    )(feat)


def turn_kernel(pre_ref, out_ref):
    pix, chans = pre_ref.shape
    grad = 0.25 * slope(pre_ref[...])
    grad = jnp.concatenate([grad, jnp.zeros((out_ref.shape[1] - pix, chans), F32)], axis=0)
    out_ref[...] = grad.T.astype(BF)


def turned_slope(pre, cols):
    pix, chans = pre.shape
    return pl.pallas_call(
        turn_kernel,
        out_shape=jax.ShapeDtypeStruct((chans, cols), BF),
        compiler_params=VMEM,
        cost_estimate=cost(8 * pix * chans, pix * chans * 6, pix * chans),
    )(pre)


def lines_kernel(pre_ref, dfeat_ref, out_ref, wide_ref):
    pix, chans = pre_ref.shape
    half = pix // 4
    for k in range(chans // LANES):
        dfeat = dfeat_ref[:, k * LANES : (k + 1) * LANES]
        wide_ref[k, pl.ds(0, half, 2), :] = dfeat
        wide_ref[k, pl.ds(1, half, 2), :] = dfeat
    spread = jnp.concatenate([wide_ref[k] for k in range(chans // LANES)], axis=1)
    spread = spread.reshape(pix // (2 * LINE), 1, LINE, chans)
    spread = jnp.broadcast_to(spread, (pix // (2 * LINE), 2, LINE, chans)).reshape(pix, chans)
    out_ref[...] = (0.25 * spread * slope(pre_ref[...])).astype(BF)


def conv_slope(pre, dfeat):
    pix, chans = pre.shape
    return pl.pallas_call(
        lines_kernel,
        out_shape=jax.ShapeDtypeStruct((pix, chans), BF),
        scratch_shapes=[pltpu.VMEM((chans // LANES, pix // 2, LANES), F32)],
        compiler_params=VMEM,
        cost_estimate=LITTLE,
    )(pre, dfeat)


def fc7_kernel(known_ref, hidden_ref, pick_ref, seven_ref, terms_ref):
    count, mine, wide = hidden_ref.shape
    lines, both, _ = known_ref.shape
    rows7, cols7 = count * wide, both // 2

    def weight(k, start, size):
        block = known_ref[:, k * cols7 : (k + 1) * cols7, start : start + size]
        return block.reshape(lines * cols7, size)

    sevens = []
    for k in range(2):
        y7_pre = jnp.zeros((lines * cols7, mine), F32)
        for g in range(count):
            y7_pre += dot(weight(k, g * wide, wide), hidden_ref[g], ((1,), (1,)))
        cot = dot(weight(k, rows7, pick_ref.shape[0]), pick_ref[...], ((1,), (0,)))
        sevens.append((cot * slope(y7_pre)).astype(BF))
        seven_ref[:, k * mine : (k + 1) * mine] = sevens[k]
    for g in range(count):
        parts = [dot(sevens[k], weight(k, g * wide, wide), ((0,), (0,))) for k in range(2)]
        terms_ref[g] = (parts[0] + parts[1]).astype(BF)


def fc7_step(known, hidden, pick):
    lines, both, _ = known.shape
    return pl.pallas_call(
        fc7_kernel,
        out_shape=[
            jax.ShapeDtypeStruct((lines * both // 2, 2 * pick.shape[1]), BF),
            jax.ShapeDtypeStruct(hidden.shape, BF),
        ],
        compiler_params=VMEM,
        cost_estimate=cost(4 * known.size * pick.shape[1], known.size * 2),
    )(known, hidden, pick)


def back_kernel(g_ref, weight_ref, out_ref):
    out_ref[...] = dot(g_ref[...], weight_ref[...], ((1,), (1,))).astype(BF)


def features_back(g_six, weight):
    count, feats = g_six.shape[0], weight.shape[0]
    return pl.pallas_call(
        back_kernel,
        out_shape=jax.ShapeDtypeStruct((count, feats), BF),
        compiler_params=VMEM,
        cost_estimate=cost(2 * count * weight.size, weight.size * 2),
    )(g_six, weight)


def outer_kernel(which_ref, inputs_ref, g_ref, out_ref):
    units = out_ref.shape[1]
    g_six = g_ref[:, pl.ds(pl.multiple_of(which_ref[0] * units, units), units)]
    out_ref[...] = dot(inputs_ref[...], g_six, ((0,), (0,))).astype(out_ref.dtype)


def outer_add_kernel(which_ref, inputs_ref, g_ref, more_ref, out_ref):
    units = out_ref.shape[1]
    g_six = g_ref[:, pl.ds(pl.multiple_of(which_ref[0] * units, units), units)]
    out_ref[...] = dot(inputs_ref[...], g_six, ((0,), (0,))) + more_ref[...].astype(F32)


def weight_terms(which, inputs, g_six, units, more=None):
    feats = inputs.shape[1]
    operands = (inputs, g_six) if more is None else (inputs, g_six, more)
    in_vmem = [pl.BlockSpec(memory_space=pltpu.VMEM)] * len(operands)
    return pl.pallas_call(
        outer_kernel if more is None else outer_add_kernel,
        in_specs=[pl.BlockSpec(memory_space=pltpu.SMEM)] + in_vmem,
        out_shape=jax.ShapeDtypeStruct((feats, units), BF if more is None else F32),
        compiler_params=VMEM,
        cost_estimate=LITTLE,
    )(which.reshape(1).astype(jnp.int32), *operands)


def pack_kernel(me_ref, terms_ref, slope_ref, out_ref, parts_ref, own_ref):
    nx, rows, _ = out_ref.shape
    feats = terms_ref.shape[2]
    run = LANES // 2
    runs = feats // run
    total = terms_ref[...].astype(F32).sum(axis=0).astype(BF).astype(F32)
    total = jnp.concatenate([total, jnp.zeros((nx, -feats % LANES), F32)], axis=1)
    parts_ref[...] = jnp.zeros(parts_ref.shape, F32)
    own_ref[...] = jnp.zeros(own_ref.shape, F32)
    for t in range(runs):
        tile = total[:, t // 2 * LANES : (t // 2 + 1) * LANES]
        other = pltpu.roll(tile, run, 1)
        low, high = (tile, other) if t % 2 == 0 else (other, tile)
        parts_ref[t % nx, t // nx * nx : (t // nx + 1) * nx, :] = low
        own_ref[pl.ds(t, nx, rows), :] = high
    lane = lax.broadcasted_iota(jnp.int32, (rows, LANES), 1)
    for e in range(nx):
        dest = lax.rem(me_ref[0] + e, nx)
        own = own_ref[pl.ds(pl.multiple_of(dest * rows, rows), rows), :]
        out_ref[dest, :, :LANES] = jnp.where(lane < run, parts_ref[e], own).astype(BF)
    out_ref[:, :, LANES:] = slope_ref[...]


def pack_dfeat(me, terms, slopes):
    _, nx, feats = terms.shape
    rows = nx * nx
    return pl.pallas_call(
        pack_kernel,
        in_specs=[
            pl.BlockSpec(memory_space=pltpu.SMEM),
            pl.BlockSpec(memory_space=pltpu.VMEM),
            pl.BlockSpec(memory_space=pltpu.VMEM),
        ],
        out_shape=jax.ShapeDtypeStruct((nx, rows, LANES + slopes.shape[2]), BF),
        scratch_shapes=[
            pltpu.VMEM((nx, rows, LANES), F32),
            pltpu.VMEM((nx * rows, LANES), F32),
        ],
        compiler_params=VMEM,
        cost_estimate=cost(4 * terms.size, terms.size * 2),
    )(me, terms, slopes)


def kernel_kernel(place_ref, lines_ref, packs_ref, spread_ref, own_ref, sent_ref, grad_ref, flat_ref, wide_ref):
    images, part, _ = packs_ref.shape
    cols = spread_ref.shape[1]
    chans = lines_ref.shape[2]
    wide_ref[...] = packs_ref[:, :, :LANES].astype(F32).reshape(wide_ref.shape)
    for k in range(images):
        n = lax.rem(place_ref[0] + k % 2, 2) * (images // 2) + k // 2
        cells = wide_ref[pl.ds(n, wide_ref.shape[0] // images, images), :].astype(BF)
        spread = dot(cells, spread_ref[...], ((0,), (0,)))[:part]
        turned = (spread * packs_ref[n, :, LANES:].astype(F32)).astype(BF).astype(F32)
        moved = [turned] + [pltpu.roll(turned, j, 1) for j in (1, 2)]
        grad_ref[:, k * cols : (k + 1) * cols] = jnp.concatenate(moved, axis=0).astype(BF)
    for row in range(3):
        block = lines_ref[:, row * LINE : row * LINE + cols, :].reshape(images * cols, chans)
        term = dot(grad_ref[...], block, ((1,), (0,)))
        for col in range(3):
            tap = 3 * row + col
            flat_ref[tap * chans : (tap + 1) * chans, :] = term[col * part : (col + 1) * part].T
    count, size, _ = own_ref.shape
    for core, out_ref in ((place_ref[1], own_ref), (1 - place_ref[1], sent_ref)):
        for dest in range(count):
            at = pl.multiple_of((2 * dest + core) * (2 * size), 2 * size)
            both = [flat_ref[pl.ds(at + k * size, size), :] for k in range(2)]
            out_ref[dest] = jnp.concatenate(both, axis=1).astype(out_ref.dtype)


def conv_kernel_grad(place, lines, packs, spread, count):
    images, _, chans = lines.shape
    _, part, _ = packs.shape
    cols = spread.shape[1]
    size = 9 * chans // (4 * count)
    return pl.pallas_call(
        kernel_kernel,
        in_specs=[pl.BlockSpec(memory_space=pltpu.SMEM)] + [pl.BlockSpec(memory_space=pltpu.VMEM)] * 3,
        out_shape=[jax.ShapeDtypeStruct((count, size, 2 * part), kind) for kind in (F32, BF)],
        scratch_shapes=[
            pltpu.VMEM((3 * part, images * cols), BF),
            pltpu.VMEM((9 * chans, part), F32),
            pltpu.VMEM((images * part, LANES), F32),
        ],
        compiler_params=VMEM,
        cost_estimate=cost(18 * images * cols * chans * part, lines.size * 2),
    )(place, lines, packs, spread)


def backward_kernel(lines_ref, weight_ref, out_ref, sums_ref):
    step = pl.program_id(0)
    col = lax.rem(step, 3)
    rows = sums_ref.shape[1]
    start = pl.multiple_of((2 - step // 3) * LINE, LINE)
    part = dot(lines_ref[pl.ds(start, rows), :], weight_ref[...], ((1,), (1,)))

    @pl.when(step < 3)
    def _():
        sums_ref[col] = part

    @pl.when(step >= 3)
    def _():
        sums_ref[col] += part

    @pl.when(step == 8)
    def _():
        _, side, _, chans = out_ref.shape
        pix = side * LINE
        grad = sums_ref[0, 2 : pix + 2, :] + sums_ref[1, 1 : pix + 1, :] + sums_ref[2, 0:pix, :]
        out_ref[0] = grad.reshape(side, LINE, chans)[:, :side, :]


def conv_backward(lines, weight, side):
    chans = lines.shape[1]
    depth = weight.shape[0] // 9
    pix = side * LINE
    return pl.pallas_call(
        backward_kernel,
        grid=(9,),
        in_specs=[
            pl.BlockSpec(lines.shape, lambda t: (0, 0)),
            pl.BlockSpec((depth, chans), lambda t: (t, 0)),
        ],
        out_specs=pl.BlockSpec((1, side, side, depth), lambda t: (0, 0, 0, 0)),
        out_shape=jax.ShapeDtypeStruct((1, side, side, depth), F32),
        scratch_shapes=[pltpu.VMEM((3, pix + LINE, depth), F32)],
        compiler_params=VMEM,
        cost_estimate=LITTLE,
    )(lines, weight)


def spread_matrix(me, nx, half, cols):
    at = lax.broadcasted_iota(jnp.int32, (nx * nx, cols), 0)
    pixel = lax.broadcasted_iota(jnp.int32, (nx * nx, cols), 1)
    source, run = at // nx, at % nx
    line, place = pixel // LINE, pixel % LINE
    per = half * half // nx
    cell = jnp.where((line < 2 * half) & (place < 2 * half), line // 2 * half + place // 2, -1)
    mine = per * source + run + (me < source).astype(jnp.int32)
    return ((cell == mine) & (run <= per)).astype(BF)


def swap(value, axis):
    return lax.all_to_all(value, axis, 0, 0, tiled=True)


def share(value, axis, count):
    return swap(jnp.broadcast_to(value, (count,) + value.shape), axis)


def bordered(maps):
    side, _, chans = maps.shape
    padded = jnp.pad(maps, ((1, 3), (1, LINE - side - 1), (0, 0)))
    return padded.reshape((side + 4) * LINE, chans)


def make(nh, nv, nz, nc):
    nx, ny = nh * nv, nz * nc
    gx = ("xh", "y")
    near = nz // nx
    gy = ("gz", "core")
    across = [(k, nh - 1 - k) for k in range(nh)]

    def paired(value, axis, way):
        return jnp.concatenate([value, lax.ppermute(value, axis, way)], axis=0)
    pair = [(k, nc - 1 - k) for k in range(nc)]

    def on_device(images, conv_weight, fc6_weight, fc7_weight, cotangent):
        side, chans = images.shape[1], images.shape[3]
        half = side // 2
        feats, units = fc6_weight.shape
        rows7, cols7 = fc7_weight.shape
        total = cotangent.shape[0]
        group = total // nc
        mine = group // nx
        wide = units * nc
        part = chans // nx
        cols = 2 * LANES
        high, core = lax.axis_index("xh"), lax.axis_index("core")
        me = high * nv + lax.axis_index("y")
        me_word = me.reshape(1).astype(jnp.int32)

        known = join(fc7_weight.T, cotangent.T)
        known = lax.all_gather(known, gx + ("core",), axis=0, tiled=False)
        known = known.reshape(nx, nc * cols7, rows7 + total)
        other6 = lax.ppermute(fc6_weight, "core", pair)
        conv_pre, feat = conv_forward(images, conv_weight, nx)
        slopes = turned_slope(conv_pre, cols).reshape(nx, part, cols)
        feat, other6 = lax.optimization_barrier((swap(feat, gx), other6))
        other6, image = lax.optimization_barrier((other6, images))
        gathered = lax.all_gather(paired(image, "xh", across), "y", axis=0, tiled=True)
        inputs = swap(feature_copies(feat, nz, feats), "gz").reshape(group, feats)
        first = jnp.where(core == 0, fc6_weight, other6)
        second = jnp.where(core == 0, other6, fc6_weight)
        weight6 = jnp.concatenate([first, second], axis=1)
        inputs, weight6 = lax.optimization_barrier((inputs, weight6))

        h6_terms = dot(inputs, weight6, ((1,), (0,))).astype(BF).reshape(nx, mine, wide)
        h6_pre = swap(h6_terms, gx).astype(F32).sum(axis=0)
        own_hidden = activate(h6_pre).astype(BF)
        hidden = share(own_hidden, "gz", nz)

        place = lax.broadcasted_iota(jnp.int32, (total, mine), 1)
        source = (place % nx) * ny + (me * near + place // nx) * nc + core
        pick = (lax.broadcasted_iota(jnp.int32, (total, mine), 0) == source).astype(BF)
        g_seven, dh6_terms = fc7_step(known, hidden, pick)
        dh6_terms, hidden = lax.optimization_barrier((dh6_terms, hidden))
        hidden = hidden.transpose(1, 0, 2).reshape(mine, rows7)
        hidden = paired(hidden, "xh", across)
        dh6_terms, hidden = lax.optimization_barrier((swap(dh6_terms, "gz"), hidden))
        all_hidden = lax.all_gather(hidden, "y", axis=0, tiled=False).reshape(group, rows7)
        grad_hidden = dh6_terms.astype(F32).sum(axis=0)
        own_six = (grad_hidden * slope(h6_pre)).astype(BF)

        columns = g_seven.reshape(nx, cols7, nc * mine)
        columns = jnp.pad(columns, ((0, 0), (0, mine - cols7), (0, LANES - nc * mine)))
        both = jnp.concatenate([jnp.broadcast_to(own_six, (nx, mine, wide)), columns], axis=2)
        both, gathered = lax.optimization_barrier((swap(both, gx), gathered))
        g_six = both[:, :, :wide].reshape(group, wide)
        columns = both[:, :cols7, wide : wide + nc * mine]

        feat_terms = features_back(g_six, weight6).reshape(nz, nx, feats)
        feat_terms, g_six = lax.optimization_barrier((feat_terms, g_six))
        feat_terms, all_hidden = lax.optimization_barrier((swap(feat_terms, "gz"), all_hidden))
        sent6 = weight_terms(nc - 1 - core, inputs, g_six, units)
        packs = swap(pack_dfeat(me_word, feat_terms, slopes), gx)
        gathered, sent6 = lax.optimization_barrier((gathered, sent6))
        all_lines = jax.vmap(bordered)(gathered)
        grad_fc6 = weight_terms(core, inputs, g_six, units, lax.ppermute(sent6, "core", pair))
        spread = spread_matrix(me, nx, half, cols)
        place = jnp.stack([high, core]).astype(jnp.int32)
        packed, sent = conv_kernel_grad(place, all_lines, packs, spread, nz)
        packed = (packed + lax.ppermute(sent, "core", pair).astype(F32)).astype(BF)
        columns = columns.reshape(nh, nv, cols7, nc * mine)
        columns = jnp.where(high == 0, columns, columns[::-1])
        columns = columns.reshape(nh, nv, cols7, nc, mine).transpose(3, 2, 1, 0, 4)
        columns = columns.reshape(nc * cols7, group)
        terms7 = dot(columns, all_hidden, ((1,), (0,)))
        own7 = jnp.where(core == 0, terms7[:cols7], terms7[cols7:])
        sent7 = jnp.where(core == 0, terms7[cols7:], terms7[:cols7])
        packed = swap(packed, "gz")

        runs = feats // part
        dfeat = packs[:, :runs, part : 2 * part].reshape(half, half, chans).astype(F32)
        dfeat = jnp.pad(dfeat, ((0, 0), (0, 1), (0, 0))).reshape(half * (half + 1), chans)
        g_lines = conv_slope(conv_pre, dfeat).reshape(side, LINE, chans)[:, :side]
        grad_images = conv_backward(bordered(g_lines), conv_weight, side)

        grad_fc7 = (own7 + lax.ppermute(sent7, "core", pair)).T
        packed, grad_fc7 = lax.optimization_barrier((packed, grad_fc7))
        packed = packed.astype(F32).sum(axis=0)
        grad_conv = jnp.concatenate([packed[:, :part], packed[:, part:]], axis=0)
        return (grad_conv, grad_fc6, grad_fc7, grad_images)

    return on_device


def solution(mesh):
    nx, ny = mesh.shape["gx"], mesh.shape["gy"]
    nh = nc = 2
    nv, nz = nx // nh, ny // nc
    fine = Mesh(mesh.devices.reshape(nh, nv, nz, nc), ("xh", "y", "gz", "core"))
    gx, gy = ("xh", "y"), ("gz", "core")
    both = gx + gy
    return jax.shard_map(
        make(nh, nv, nz, nc),
        mesh=fine,
        in_specs=(P(both, None, None, None), P(), P(gx, gy), P(None, both), P(None, both)),
        out_specs=(P(gy, gx), P(gx, gy), P(None, both), P(both, None, None, None)),
        check_vma=False,
    )
```

```python
import jax
import jax.numpy as jnp
from jax import lax
from jax.experimental import pallas as pl
from jax.experimental.pallas import tpu as pltpu
from jax.sharding import Mesh, PartitionSpec as P

BF = jnp.bfloat16
F32 = jnp.float32
LANES = 128
LINE = 16
VMEM = pltpu.CompilerParams(vmem_limit_bytes=20 * 2**20)
WHOLE = pltpu.CompilerParams(vmem_limit_bytes=57 * 2**20)


def activate(value):
    return value * jax.nn.sigmoid(value)


def slope(value):
    sig = jax.nn.sigmoid(value)
    return sig * (1.0 + value * (1.0 - sig))


def dot(a, b, dims):
    return lax.dot_general(a, b, (dims, ((), ())), preferred_element_type=F32)


LITTLE = pl.CostEstimate(flops=1000, bytes_accessed=1000, transcendentals=0)


def cost(flops, moved, special=0):
    return pl.CostEstimate(flops=flops, bytes_accessed=moved, transcendentals=special)


def forward_kernel(
    image_ref, weight_ref, pre_ref, feat_ref, held_ref, maps_ref, lines_ref, sums_ref, pool_ref, runs_ref, sems
):
    pix, chans = pre_ref.shape
    _, height, width, depth = maps_ref.shape
    rows = sums_ref.shape[1]

    def load(tap):
        return pltpu.make_async_copy(
            weight_ref.at[pl.ds(tap * depth, depth), :],
            held_ref.at[tap % 3, pl.ds(tap // 3 * depth, depth), :],
            sems.at[tap],
        )

    order = [3 * row + col for col in range(3) for row in range(3)]
    fetch = pltpu.make_async_copy(image_ref, maps_ref, sems.at[9])
    fetch.start()
    for tap in order:
        load(tap).start()
    lines_ref[...] = jnp.zeros(lines_ref.shape, F32)
    fetch.wait()
    for k in range(height):
        at = (k + 1) * LINE + 1
        lines_ref[at : at + width, :] = maps_ref[0, k].astype(F32)
    image = [lines_ref[k * LINE : k * LINE + rows, :].astype(BF) for k in range(3)]
    image = jnp.concatenate(image, axis=1)
    for col in range(3):
        for row in range(3):
            load(3 * row + col).wait()
        sums_ref[col] = dot(image, held_ref[col], ((1,), (0,)))
    pre = sums_ref[0, 0:pix, :] + sums_ref[1, 1 : pix + 1, :] + sums_ref[2, 2 : pix + 2, :]
    pre_ref[...] = pre
    act = activate(pre).reshape(pix // (2 * LINE), 2, LINE, chans)
    lines = (act[:, 0] + act[:, 1]).reshape(pix // 2, chans)
    half = pix // 4
    side = pix // LINE // 2
    run = LANES // 2
    dests, rows, across = feat_ref.shape
    runs = side * side * chans // (dests * run)
    runs_ref[...] = jnp.zeros(runs_ref.shape, F32)
    for k in range(chans // LANES):
        pool_ref[k] = lines[:, k * LANES : (k + 1) * LANES]
        total = 0.25 * (pool_ref[k, pl.ds(0, half, 2), :] + pool_ref[k, pl.ds(1, half, 2), :])
        other = pltpu.roll(total, run, 1)
        for cell in range(side * side):
            line = cell // side * (LINE // 2) + cell % side
            for part in range(2):
                dest, t = divmod(cell * (chans // run) + 2 * k + part, runs)
                at = t % 2 * run
                piece = total if t % 2 == part else other
                row, lane = divmod(t * run, across)
                row = dest * rows + row
                runs_ref[row : row + 1, lane : lane + run] = piece[line : line + 1, at : at + run]
    feat_ref[...] = runs_ref[...].astype(BF).reshape(dests, rows, across)


def conv_forward(maps, weight, nx):
    _, side, _, depth = maps.shape
    chans = weight.shape[1]
    pix = side * LINE
    rows, width = LINE, 2 * LANES
    return pl.pallas_call(
        forward_kernel,
        in_specs=[
            pl.BlockSpec(memory_space=pl.ANY),
            pl.BlockSpec(memory_space=pl.ANY),
        ],
        out_shape=[
            jax.ShapeDtypeStruct((pix, chans), F32),
            jax.ShapeDtypeStruct((nx, rows, width), BF),
        ],
        scratch_shapes=[
            pltpu.VMEM((3, 3 * depth, chans), BF),
            pltpu.VMEM(maps.shape, BF),
            pltpu.VMEM((pix + 3 * LINE, depth), F32),
            pltpu.VMEM((3, pix + LINE, chans), F32),
            pltpu.VMEM((chans // LANES, pix // 2, LANES), F32),
            pltpu.VMEM((nx * rows, width), F32),
            pltpu.SemaphoreType.DMA((10,)),
        ],
        compiler_params=WHOLE,
        cost_estimate=cost(18 * pix * depth * chans, weight.size * 2, pix * chans),
    )(maps, weight)


def join_kernel(left_ref, right_ref, out_ref):
    cut = left_ref.shape[1]
    out_ref[:, :cut] = left_ref[...]
    out_ref[:, cut:] = right_ref[...]


def join(left, right):
    rows, cut = left.shape
    return pl.pallas_call(
        join_kernel,
        out_shape=jax.ShapeDtypeStruct((rows, cut + right.shape[1]), left.dtype),
        cost_estimate=cost(0, left.size * 4),
    )(left, right)


def copies_kernel(feat_ref, out_ref):
    feats = out_ref.shape[2]
    _, rows, width = feat_ref.shape
    value = feat_ref[...].astype(F32)
    flat = jnp.concatenate([value[:, k, :] for k in range(rows)], axis=1)[:, :feats].astype(BF)
    for k in range(out_ref.shape[0]):
        out_ref[k] = flat


def feature_copies(feat, count, feats):
    return pl.pallas_call(
        copies_kernel,
        out_shape=jax.ShapeDtypeStruct((count, feat.shape[0], feats), BF),
        compiler_params=VMEM,
        cost_estimate=cost(feat.size, feat.size * 2 * count),
    )(feat)


def turn_kernel(pre_ref, out_ref):
    pix, chans = pre_ref.shape
    grad = 0.25 * slope(pre_ref[...])
    grad = jnp.concatenate([grad, jnp.zeros((out_ref.shape[1] - pix, chans), F32)], axis=0)
    out_ref[...] = grad.T.astype(BF)


def turned_slope(pre, cols):
    pix, chans = pre.shape
    return pl.pallas_call(
        turn_kernel,
        out_shape=jax.ShapeDtypeStruct((chans, cols), BF),
        compiler_params=VMEM,
        cost_estimate=cost(8 * pix * chans, pix * chans * 6, pix * chans),
    )(pre)


def lines_kernel(pre_ref, dfeat_ref, out_ref, wide_ref):
    pix, chans = pre_ref.shape
    half = pix // 4
    for k in range(chans // LANES):
        dfeat = dfeat_ref[:, k * LANES : (k + 1) * LANES]
        wide_ref[k, pl.ds(0, half, 2), :] = dfeat
        wide_ref[k, pl.ds(1, half, 2), :] = dfeat
    spread = jnp.concatenate([wide_ref[k] for k in range(chans // LANES)], axis=1)
    spread = spread.reshape(pix // (2 * LINE), 1, LINE, chans)
    spread = jnp.broadcast_to(spread, (pix // (2 * LINE), 2, LINE, chans)).reshape(pix, chans)
    out_ref[...] = (0.25 * spread * slope(pre_ref[...])).astype(BF)


def conv_slope(pre, dfeat):
    pix, chans = pre.shape
    return pl.pallas_call(
        lines_kernel,
        out_shape=jax.ShapeDtypeStruct((pix, chans), BF),
        scratch_shapes=[pltpu.VMEM((chans // LANES, pix // 2, LANES), F32)],
        compiler_params=VMEM,
        cost_estimate=LITTLE,
    )(pre, dfeat)


def fc7_kernel(known_ref, hidden_ref, pick_ref, seven_ref, terms_ref):
    count, mine, wide = hidden_ref.shape
    lines, both, _ = known_ref.shape
    rows7, cols7 = count * wide, both // 2

    def weight(k, start, size):
        block = known_ref[:, k * cols7 : (k + 1) * cols7, start : start + size]
        return block.reshape(lines * cols7, size)

    sevens = []
    for k in range(2):
        y7_pre = jnp.zeros((lines * cols7, mine), F32)
        for g in range(count):
            y7_pre += dot(weight(k, g * wide, wide), hidden_ref[g], ((1,), (1,)))
        cot = dot(weight(k, rows7, pick_ref.shape[0]), pick_ref[...], ((1,), (0,)))
        sevens.append((cot * slope(y7_pre)).astype(BF))
        seven_ref[:, k * mine : (k + 1) * mine] = sevens[k]
    for g in range(count):
        parts = [dot(sevens[k], weight(k, g * wide, wide), ((0,), (0,))) for k in range(2)]
        terms_ref[g] = (parts[0] + parts[1]).astype(BF)


def fc7_step(known, hidden, pick):
    lines, both, _ = known.shape
    return pl.pallas_call(
        fc7_kernel,
        out_shape=[
            jax.ShapeDtypeStruct((lines * both // 2, 2 * pick.shape[1]), BF),
            jax.ShapeDtypeStruct(hidden.shape, BF),
        ],
        compiler_params=VMEM,
        cost_estimate=cost(4 * known.size * pick.shape[1], known.size * 2),
    )(known, hidden, pick)


def back_kernel(g_ref, weight_ref, out_ref):
    out_ref[...] = dot(g_ref[...], weight_ref[...], ((1,), (1,))).astype(BF)


def features_back(g_six, weight):
    count, feats = g_six.shape[0], weight.shape[0]
    return pl.pallas_call(
        back_kernel,
        out_shape=jax.ShapeDtypeStruct((count, feats), BF),
        compiler_params=VMEM,
        cost_estimate=cost(2 * count * weight.size, weight.size * 2),
    )(g_six, weight)


def outer_kernel(which_ref, inputs_ref, g_ref, out_ref):
    units = out_ref.shape[1]
    g_six = g_ref[:, pl.ds(pl.multiple_of(which_ref[0] * units, units), units)]
    out_ref[...] = dot(inputs_ref[...], g_six, ((0,), (0,))).astype(out_ref.dtype)


def outer_add_kernel(which_ref, inputs_ref, g_ref, more_ref, out_ref):
    units = out_ref.shape[1]
    g_six = g_ref[:, pl.ds(pl.multiple_of(which_ref[0] * units, units), units)]
    out_ref[...] = dot(inputs_ref[...], g_six, ((0,), (0,))) + more_ref[...].astype(F32)


def weight_terms(which, inputs, g_six, units, more=None):
    feats = inputs.shape[1]
    operands = (inputs, g_six) if more is None else (inputs, g_six, more)
    in_vmem = [pl.BlockSpec(memory_space=pltpu.VMEM)] * len(operands)
    return pl.pallas_call(
        outer_kernel if more is None else outer_add_kernel,
        in_specs=[pl.BlockSpec(memory_space=pltpu.SMEM)] + in_vmem,
        out_shape=jax.ShapeDtypeStruct((feats, units), BF if more is None else F32),
        compiler_params=VMEM,
        cost_estimate=LITTLE,
    )(which.reshape(1).astype(jnp.int32), *operands)


def pack_kernel(me_ref, terms_ref, slope_ref, out_ref, parts_ref, own_ref):
    nx, rows, _ = out_ref.shape
    feats = terms_ref.shape[2]
    run = LANES // 2
    runs = feats // run
    total = terms_ref[...].astype(F32).sum(axis=0).astype(BF).astype(F32)
    total = jnp.concatenate([total, jnp.zeros((nx, -feats % LANES), F32)], axis=1)
    parts_ref[...] = jnp.zeros(parts_ref.shape, F32)
    own_ref[...] = jnp.zeros(own_ref.shape, F32)
    for t in range(runs):
        tile = total[:, t // 2 * LANES : (t // 2 + 1) * LANES]
        other = pltpu.roll(tile, run, 1)
        low, high = (tile, other) if t % 2 == 0 else (other, tile)
        parts_ref[t % nx, t // nx * nx : (t // nx + 1) * nx, :] = low
        own_ref[pl.ds(t, nx, rows), :] = high
    lane = lax.broadcasted_iota(jnp.int32, (rows, LANES), 1)
    for e in range(nx):
        dest = lax.rem(me_ref[0] + e, nx)
        own = own_ref[pl.ds(pl.multiple_of(dest * rows, rows), rows), :]
        out_ref[dest, :, :LANES] = jnp.where(lane < run, parts_ref[e], own).astype(BF)
    out_ref[:, :, LANES:] = slope_ref[...]


def pack_dfeat(me, terms, slopes):
    _, nx, feats = terms.shape
    rows = nx * nx
    return pl.pallas_call(
        pack_kernel,
        in_specs=[
            pl.BlockSpec(memory_space=pltpu.SMEM),
            pl.BlockSpec(memory_space=pltpu.VMEM),
            pl.BlockSpec(memory_space=pltpu.VMEM),
        ],
        out_shape=jax.ShapeDtypeStruct((nx, rows, LANES + slopes.shape[2]), BF),
        scratch_shapes=[
            pltpu.VMEM((nx, rows, LANES), F32),
            pltpu.VMEM((nx * rows, LANES), F32),
        ],
        compiler_params=VMEM,
        cost_estimate=cost(4 * terms.size, terms.size * 2),
    )(me, terms, slopes)


def kernel_kernel(place_ref, lines_ref, packs_ref, spread_ref, own_ref, sent_ref, grad_ref, flat_ref, wide_ref):
    images, part, _ = packs_ref.shape
    cols = spread_ref.shape[1]
    chans = lines_ref.shape[2]
    wide_ref[...] = packs_ref[:, :, :LANES].astype(F32).reshape(wide_ref.shape)
    for k in range(images):
        n = lax.rem(place_ref[0] + k % 2, 2) * (images // 2) + k // 2
        cells = wide_ref[pl.ds(n, wide_ref.shape[0] // images, images), :].astype(BF)
        spread = dot(cells, spread_ref[...], ((0,), (0,)))[:part]
        turned = (spread * packs_ref[n, :, LANES:].astype(F32)).astype(BF).astype(F32)
        moved = [turned] + [pltpu.roll(turned, j, 1) for j in (1, 2)]
        grad_ref[:, k * cols : (k + 1) * cols] = jnp.concatenate(moved, axis=0).astype(BF)
    for row in range(3):
        block = lines_ref[:, row * LINE : row * LINE + cols, :].reshape(images * cols, chans)
        term = dot(grad_ref[...], block, ((1,), (0,)))
        for col in range(3):
            tap = 3 * row + col
            flat_ref[tap * chans : (tap + 1) * chans, :] = term[col * part : (col + 1) * part].T
    count, size, _ = own_ref.shape
    for core, out_ref in ((place_ref[1], own_ref), (1 - place_ref[1], sent_ref)):
        for dest in range(count):
            at = pl.multiple_of((2 * dest + core) * (2 * size), 2 * size)
            both = [flat_ref[pl.ds(at + k * size, size), :] for k in range(2)]
            out_ref[dest] = jnp.concatenate(both, axis=1).astype(out_ref.dtype)


def conv_kernel_grad(place, lines, packs, spread, count):
    images, _, chans = lines.shape
    _, part, _ = packs.shape
    cols = spread.shape[1]
    size = 9 * chans // (4 * count)
    return pl.pallas_call(
        kernel_kernel,
        in_specs=[pl.BlockSpec(memory_space=pltpu.SMEM)] + [pl.BlockSpec(memory_space=pltpu.VMEM)] * 3,
        out_shape=[jax.ShapeDtypeStruct((count, size, 2 * part), kind) for kind in (F32, BF)],
        scratch_shapes=[
            pltpu.VMEM((3 * part, images * cols), BF),
            pltpu.VMEM((9 * chans, part), F32),
            pltpu.VMEM((images * part, LANES), F32),
        ],
        compiler_params=VMEM,
        cost_estimate=cost(18 * images * cols * chans * part, lines.size * 2),
    )(place, lines, packs, spread)


def backward_kernel(lines_ref, weight_ref, out_ref, sums_ref):
    step = pl.program_id(0)
    col = lax.rem(step, 3)
    rows = sums_ref.shape[1]
    start = pl.multiple_of((2 - step // 3) * LINE, LINE)
    part = dot(lines_ref[pl.ds(start, rows), :], weight_ref[...], ((1,), (1,)))

    @pl.when(step < 3)
    def _():
        sums_ref[col] = part

    @pl.when(step >= 3)
    def _():
        sums_ref[col] += part

    @pl.when(step == 8)
    def _():
        _, side, _, chans = out_ref.shape
        pix = side * LINE
        grad = sums_ref[0, 2 : pix + 2, :] + sums_ref[1, 1 : pix + 1, :] + sums_ref[2, 0:pix, :]
        out_ref[0] = grad.reshape(side, LINE, chans)[:, :side, :]


def conv_backward(lines, weight, side):
    chans = lines.shape[1]
    depth = weight.shape[0] // 9
    pix = side * LINE
    return pl.pallas_call(
        backward_kernel,
        grid=(9,),
        in_specs=[
            pl.BlockSpec(lines.shape, lambda t: (0, 0)),
            pl.BlockSpec((depth, chans), lambda t: (t, 0)),
        ],
        out_specs=pl.BlockSpec((1, side, side, depth), lambda t: (0, 0, 0, 0)),
        out_shape=jax.ShapeDtypeStruct((1, side, side, depth), F32),
        scratch_shapes=[pltpu.VMEM((3, pix + LINE, depth), F32)],
        compiler_params=VMEM,
        cost_estimate=LITTLE,
    )(lines, weight)


def spread_matrix(me, nx, half, cols):
    at = lax.broadcasted_iota(jnp.int32, (nx * nx, cols), 0)
    pixel = lax.broadcasted_iota(jnp.int32, (nx * nx, cols), 1)
    source, run = at // nx, at % nx
    line, place = pixel // LINE, pixel % LINE
    per = half * half // nx
    cell = jnp.where((line < 2 * half) & (place < 2 * half), line // 2 * half + place // 2, -1)
    mine = per * source + run + (me < source).astype(jnp.int32)
    return ((cell == mine) & (run <= per)).astype(BF)


def swap(value, axis):
    return lax.all_to_all(value, axis, 0, 0, tiled=True)


def share(value, axis, count):
    return swap(jnp.broadcast_to(value, (count,) + value.shape), axis)


def bordered(maps):
    side, _, chans = maps.shape
    padded = jnp.pad(maps, ((1, 3), (1, LINE - side - 1), (0, 0)))
    return padded.reshape((side + 4) * LINE, chans)


def make(nh, nv, nz, nc):
    nx, ny = nh * nv, nz * nc
    gx = ("xh", "y")
    near = nz // nx
    gy = ("gz", "core")
    across = [(k, nh - 1 - k) for k in range(nh)]

    def paired(value, axis, way):
        return jnp.concatenate([value, lax.ppermute(value, axis, way)], axis=0)
    pair = [(k, nc - 1 - k) for k in range(nc)]

    def on_device(images, conv_weight, fc6_weight, fc7_weight, cotangent):
        side, chans = images.shape[1], images.shape[3]
        half = side // 2
        feats, units = fc6_weight.shape
        rows7, cols7 = fc7_weight.shape
        total = cotangent.shape[0]
        group = total // nc
        mine = group // nx
        wide = units * nc
        part = chans // nx
        cols = 2 * LANES
        high, core = lax.axis_index("xh"), lax.axis_index("core")
        me = high * nv + lax.axis_index("y")
        me_word = me.reshape(1).astype(jnp.int32)

        known = join(fc7_weight.T, cotangent.T)
        known = lax.all_gather(known, gx + ("core",), axis=0, tiled=False)
        known = known.reshape(nx, nc * cols7, rows7 + total)
        other6 = lax.ppermute(fc6_weight, "core", pair)
        conv_pre, feat = conv_forward(images, conv_weight, nx)
        slopes = turned_slope(conv_pre, cols).reshape(nx, part, cols)
        feat, other6 = lax.optimization_barrier((swap(feat, gx), other6))
        other6, image = lax.optimization_barrier((other6, images))
        gathered = lax.all_gather(paired(image, "xh", across), "y", axis=0, tiled=True)
        inputs = swap(feature_copies(feat, nz, feats), "gz").reshape(group, feats)
        first = jnp.where(core == 0, fc6_weight, other6)
        second = jnp.where(core == 0, other6, fc6_weight)
        weight6 = jnp.concatenate([first, second], axis=1)
        inputs, weight6 = lax.optimization_barrier((inputs, weight6))

        h6_terms = dot(inputs, weight6, ((1,), (0,))).astype(BF).reshape(nx, mine, wide)
        h6_pre = swap(h6_terms, gx).astype(F32).sum(axis=0)
        own_hidden = activate(h6_pre).astype(BF)
        hidden = share(own_hidden, "gz", nz)

        place = lax.broadcasted_iota(jnp.int32, (total, mine), 1)
        source = (place % nx) * ny + (me * near + place // nx) * nc + core
        pick = (lax.broadcasted_iota(jnp.int32, (total, mine), 0) == source).astype(BF)
        g_seven, dh6_terms = fc7_step(known, hidden, pick)
        dh6_terms, hidden = lax.optimization_barrier((dh6_terms, hidden))
        hidden = hidden.transpose(1, 0, 2).reshape(mine, rows7)
        hidden = paired(hidden, "xh", across)
        dh6_terms, hidden = lax.optimization_barrier((swap(dh6_terms, "gz"), hidden))
        all_hidden = lax.all_gather(hidden, "y", axis=0, tiled=False).reshape(group, rows7)
        grad_hidden = dh6_terms.astype(F32).sum(axis=0)
        own_six = (grad_hidden * slope(h6_pre)).astype(BF)

        columns = g_seven.reshape(nx, cols7, nc * mine)
        columns = jnp.pad(columns, ((0, 0), (0, mine - cols7), (0, LANES - nc * mine)))
        both = jnp.concatenate([jnp.broadcast_to(own_six, (nx, mine, wide)), columns], axis=2)
        both, gathered = lax.optimization_barrier((swap(both, gx), gathered))
        g_six = both[:, :, :wide].reshape(group, wide)
        columns = both[:, :cols7, wide : wide + nc * mine]

        feat_terms = features_back(g_six, weight6).reshape(nz, nx, feats)
        feat_terms, g_six = lax.optimization_barrier((feat_terms, g_six))
        feat_terms, all_hidden = lax.optimization_barrier((swap(feat_terms, "gz"), all_hidden))
        sent6 = weight_terms(nc - 1 - core, inputs, g_six, units)
        packs = swap(pack_dfeat(me_word, feat_terms, slopes), gx)
        gathered, sent6 = lax.optimization_barrier((gathered, sent6))
        all_lines = jax.vmap(bordered)(gathered)
        grad_fc6 = weight_terms(core, inputs, g_six, units, lax.ppermute(sent6, "core", pair))
        spread = spread_matrix(me, nx, half, cols)
        place = jnp.stack([high, core]).astype(jnp.int32)
        packed, sent = conv_kernel_grad(place, all_lines, packs, spread, nz)
        packed = (packed + lax.ppermute(sent, "core", pair).astype(F32)).astype(BF)
        columns = columns.reshape(nh, nv, cols7, nc * mine)
        columns = jnp.where(high == 0, columns, columns[::-1])
        columns = columns.reshape(nh, nv, cols7, nc, mine).transpose(3, 2, 1, 0, 4)
        columns = columns.reshape(nc * cols7, group)
        terms7 = dot(columns, all_hidden, ((1,), (0,)))
        own7 = jnp.where(core == 0, terms7[:cols7], terms7[cols7:])
        sent7 = jnp.where(core == 0, terms7[cols7:], terms7[:cols7])
        packed = swap(packed, "gz")

        runs = feats // part
        dfeat = packs[:, :runs, part : 2 * part].reshape(half, half, chans).astype(F32)
        dfeat = jnp.pad(dfeat, ((0, 0), (0, 1), (0, 0))).reshape(half * (half + 1), chans)
        g_lines = conv_slope(conv_pre, dfeat).reshape(side, LINE, chans)[:, :side]
        grad_images = conv_backward(bordered(g_lines), conv_weight, side)

        grad_fc7 = (own7 + lax.ppermute(sent7, "core", pair)).T
        packed, grad_fc7 = lax.optimization_barrier((packed, grad_fc7))
        packed = packed.astype(F32).sum(axis=0)
        grad_conv = jnp.concatenate([packed[:, :part], packed[:, part:]], axis=0)
        return (grad_conv, grad_fc6, grad_fc7, grad_images)

    return on_device


def solution(mesh):
    nx, ny = mesh.shape["gx"], mesh.shape["gy"]
    nh = nc = 2
    nv, nz = nx // nh, ny // nc
    fine = Mesh(mesh.devices.reshape(nh, nv, nz, nc), ("xh", "y", "gz", "core"))
    gx, gy = ("xh", "y"), ("gz", "core")
    both = gx + gy
    return jax.shard_map(
        make(nh, nv, nz, nc),
        mesh=fine,
        in_specs=(P(both, None, None, None), P(), P(gx, gy), P(None, both), P(None, both)),
        out_specs=(P(gy, gx), P(gx, gy), P(None, both), P(both, None, None, None)),
        check_vma=False,
    )
```
